256 devices in a mesh: dp: 2 (over z_hi), seq: 64 (over z_lo, x, y), head: 2 (over core).
Axes of the slice: x: 4, y: 4, z: 8 (z_hi: 2, z_lo: 4; z = z_hi * 4 + z_lo), core: 2. Of those that a mesh axis runs over, the one named last changes fastest.
Arguments:
- fine_queries: bfloat16 [2, 24576, 32, 128], P('dp', 'seq', 'head'), may hold values from -96 to 96
- fine_keys: bfloat16 [2, 24576, 32, 128], P('dp', 'seq', 'head'), may hold values from -10 to 10
- fine_values: bfloat16 [2, 24576, 32, 128], P('dp', 'seq', 'head'), may hold values from -6 to 6
- coarse_keys: bfloat16 [2, 256, 32, 128], P('dp', 'seq', 'head'), may hold values from -8 to 8
- coarse_values: bfloat16 [2, 256, 32, 128], P('dp', 'seq', 'head'), may hold values from -6 to 6
- out_grad: bfloat16 [2, 24576, 32, 128], P('dp', 'seq', 'head'), may hold values from -6 to 6
Outputs:
- attended: bfloat16 [2, 24576, 32, 128], P('dp', 'seq', 'head')
- query_grad: bfloat16 [2, 24576, 32, 128], P('dp', 'seq', 'head')
- key_grad: bfloat16 [2, 24576, 32, 128], P('dp', 'seq', 'head')
- value_grad: bfloat16 [2, 24576, 32, 128], P('dp', 'seq', 'head')
The draws below stay inside these ranges and needn't reach their ends.
All inputs are finite; a program needn't handle non-finite values.
Results may differ from the reference program's by a relative error of at most 0.012.
Values may be sent and summed in bfloat16 or wider, within the bound.
No kernel may reach another device: no remote copies, remote signals or barrier semaphores. Data moves between devices by JAX's collectives and lax.ppermute only.
A program may use at most 128 MiB of HBM per device.

```python
import jax
import jax.numpy as jnp
from jax import lax

HEADS = 32
HEAD_DIM = 128
TILE_H = 24
TILE_W = 16
RADIUS = 4
TILES_X = 8
IMAGES = 2
FINE = 24576
COARSE = 256
N_SEQ = 64


def shared_parts(key):
    shape = (IMAGES, FINE, HEADS, HEAD_DIM)
    base = jnp.clip(1.4 * jax.random.normal(key, shape, jnp.float32), -8.0, 8.0)
    return base


def draw_fine_keys(key, part):
    base = shared_parts(key)
    keys = base
    return jnp.clip(keys, -10.0, 10.0).astype(jnp.bfloat16)


def draw_fine_queries(key, part):
    key = jax.random.fold_in(key, 9)
    shape = (IMAGES, FINE, HEADS, HEAD_DIM)
    queries = 1.4 * jax.random.normal(key, shape, jnp.float32)
    return jnp.clip(queries, -96.0, 96.0).astype(jnp.bfloat16)


def levels(rng, dims, split, least, largest):
    factor_of = 1.0
    for position, blocks in split:
        steps = jax.random.uniform(jax.random.fold_in(jax.random.fold_in(rng, 6), position), (blocks,), jnp.float32, least / len(split), largest / len(split))
        factor_of = factor_of * jnp.repeat(jnp.exp(steps), dims[position] // blocks).reshape((-1,) + (1,) * (len(dims) - 1 - position))
    return factor_of


def normal_values(own_key, dims, scale, limit, split=(), held_as=jnp.bfloat16):
    values = jax.random.normal(own_key, dims, jnp.float32) * scale
    if len(split) > 0:
        values = levels(own_key, dims, split, -0.22, 0.18) * values
    return jnp.clip(values, min=-limit, max=limit).astype(held_as)


def setup_inputs(seed: int = 0) -> dict:
    key_list = jax.random.split(jax.random.key(seed), 7)
    fine_queries = draw_fine_queries(jax.random.fold_in(key_list[6], 71), 0)
    fine_keys = draw_fine_keys(jax.random.fold_in(key_list[6], 71), 0)
    fine_values = normal_values(key_list[2], (IMAGES, FINE, HEADS, HEAD_DIM), 1.0, 6.0, ((0, 2), (1, 64), (2, 2)))
    coarse_keys = normal_values(key_list[3], (IMAGES, COARSE, HEADS, HEAD_DIM), 1.4, 8.0, ((0, 2), (1, 64), (2, 2)))
    coarse_values = normal_values(key_list[4], (IMAGES, COARSE, HEADS, HEAD_DIM), 1.0, 6.0, ((0, 2), (1, 64), (2, 2)))
    out_grad = normal_values(key_list[5], (IMAGES, FINE, HEADS, HEAD_DIM), 1.0, 6.0, ((0, 2), (1, 64), (2, 2)))
    return {"fine_queries": fine_queries, "fine_keys": fine_keys, "fine_values": fine_values, "coarse_keys": coarse_keys, "coarse_values": coarse_values, "out_grad": out_grad}


FLOOR_SCORE = -1e30


def to_map(tokens):
    tiles_y = N_SEQ // TILES_X
    heads, depth = tokens.shape[1], tokens.shape[2]
    shaped = tokens.reshape(tiles_y, TILES_X, TILE_H, TILE_W, heads, depth)
    return shaped.transpose(0, 2, 1, 3, 4, 5).reshape(tiles_y * TILE_H, TILES_X * TILE_W, heads, depth)


def from_map(grid):
    tiles_y = N_SEQ // TILES_X
    heads, depth = grid.shape[2], grid.shape[3]
    shaped = grid.reshape(tiles_y, TILE_H, TILES_X, TILE_W, heads, depth)
    return shaped.transpose(0, 2, 1, 3, 4, 5).reshape(-1, heads, depth)


def window(array, row_step, col_step, height, width):
    return array[row_step:row_step + height, col_step:col_step + width]


def head_pass(parts):
    queries, keys, values, grads_out, far_keys, far_values = parts
    height, width, depth = queries.shape
    scale = depth ** -0.5
    span = 2 * RADIUS + 1
    offsets = [(row_step, col_step) for row_step in range(span) for col_step in range(span)]
    query_f = queries.astype(jnp.float32)
    grad_f = grads_out.astype(jnp.float32)
    pad_widths = ((RADIUS, RADIUS), (RADIUS, RADIUS), (0, 0))
    keys_pad = jnp.pad(keys.astype(jnp.float32), pad_widths)
    values_pad = jnp.pad(values.astype(jnp.float32), pad_widths)
    inside = jnp.pad(jnp.ones((height, width), jnp.bool_), RADIUS)
    far_k = far_keys.astype(jnp.float32)
    far_v = far_values.astype(jnp.float32)
    near_scores = jnp.stack([
        jnp.where(window(inside, row_step, col_step, height, width),
                  jnp.sum(query_f * window(keys_pad, row_step, col_step, height, width), -1) * scale,
                  FLOOR_SCORE)
        for row_step, col_step in offsets])
    flat_query = query_f.reshape(-1, depth)
    flat_grad = grad_f.reshape(-1, depth)
    far_scores = jnp.dot(flat_query, far_k.T, preferred_element_type=jnp.float32) * scale
    highest = jnp.maximum(jnp.max(near_scores, 0).reshape(-1), jnp.max(far_scores, 1))
    near_exp = jnp.exp(near_scores - highest.reshape(1, height, width))
    far_exp = jnp.exp(far_scores - highest[:, None])
    total = jnp.sum(near_exp, 0).reshape(-1) + jnp.sum(far_exp, 1)
    near_weight = near_exp / total.reshape(1, height, width)
    far_weight = far_exp / total[:, None]
    near_rounded = lax.optimization_barrier(near_weight.astype(jnp.bfloat16)).astype(jnp.float32)
    far_rounded = lax.optimization_barrier(far_weight.astype(jnp.bfloat16)).astype(jnp.float32)
    near_mix = jnp.zeros((height, width, depth), jnp.float32)
    for which, (row_step, col_step) in enumerate(offsets):
        near_mix = near_mix + near_rounded[which][..., None] * window(values_pad, row_step, col_step, height, width)
    attended = (near_mix.reshape(-1, depth) + jnp.dot(far_rounded, far_v, preferred_element_type=jnp.float32)).astype(jnp.bfloat16)
    deltas = jnp.sum(flat_grad * attended.astype(jnp.float32), 1)
    near_dots = jnp.stack([
        jnp.sum(grad_f * window(values_pad, row_step, col_step, height, width), -1)
        for row_step, col_step in offsets])
    far_dots = jnp.dot(flat_grad, far_v.T, preferred_element_type=jnp.float32)
    near_grad = (scale * near_weight * (near_dots - deltas.reshape(1, height, width))).astype(jnp.bfloat16)
    far_grad = (scale * far_weight * (far_dots - deltas[:, None])).astype(jnp.bfloat16)
    near_grad = lax.optimization_barrier(near_grad).astype(jnp.float32)
    far_grad = lax.optimization_barrier(far_grad).astype(jnp.float32)
    query_mix = jnp.zeros((height, width, depth), jnp.float32)
    key_pad_grad = jnp.zeros_like(keys_pad)
    value_pad_grad = jnp.zeros_like(values_pad)
    for which, (row_step, col_step) in enumerate(offsets):
        query_mix = query_mix + near_grad[which][..., None] * window(keys_pad, row_step, col_step, height, width)
        key_pad_grad = key_pad_grad.at[row_step:row_step + height, col_step:col_step + width].add(near_grad[which][..., None] * query_f)
        value_pad_grad = value_pad_grad.at[row_step:row_step + height, col_step:col_step + width].add(near_rounded[which][..., None] * grad_f)
    query_grad = (query_mix.reshape(-1, depth) + jnp.dot(far_grad, far_k, preferred_element_type=jnp.float32)).astype(jnp.bfloat16)
    key_grad = key_pad_grad[RADIUS:RADIUS + height, RADIUS:RADIUS + width].astype(jnp.bfloat16)
    value_grad = value_pad_grad[RADIUS:RADIUS + height, RADIUS:RADIUS + width].astype(jnp.bfloat16)
    return (attended.reshape(height, width, depth), query_grad.reshape(height, width, depth), key_grad, value_grad)


def reference(fine_queries, fine_keys, fine_values, coarse_keys, coarse_values, out_grad):
    results = []
    for image in range(IMAGES):
        maps = [jnp.moveaxis(to_map(array[image]), 2, 0) for array in (fine_queries, fine_keys, fine_values, out_grad)]
        far = [jnp.moveaxis(array[image], 1, 0) for array in (coarse_keys, coarse_values)]
        outcome = lax.map(head_pass, (maps[0], maps[1], maps[2], maps[3], far[0], far[1]))
        results.append([from_map(jnp.moveaxis(item, 0, 2)) for item in outcome])
    stacked = [jnp.stack([entry[which] for entry in results]) for which in range(4)]
    return (stacked[0], stacked[1], stacked[2], stacked[3])
```

```python
import functools

import jax
import jax.numpy as jnp
from jax import lax
from jax.experimental import pallas as pl
from jax.experimental.pallas import tpu as pltpu
from jax.sharding import PartitionSpec as P

TILE_H = 24
TILE_W = 16
RADIUS = 4
TILES_X = 8
TOKENS = TILE_H * TILE_W
EDGE = RADIUS * TILE_W
SIDE = TILE_H * RADIUS
CORNER = RADIUS * RADIUS
BLOCK_ROWS = 8
BLOCKS = TILE_H // BLOCK_ROWS
QUERIES = BLOCK_ROWS * TILE_W
WIN_ROWS = BLOCK_ROWS + 2 * RADIUS
NEAR = WIN_ROWS * (TILE_W + 2 * RADIUS)
FLOOR = -1e30
LOG2E = 1.4426950408889634
BF = jnp.bfloat16
F32 = jnp.float32
PARAMS = pltpu.CompilerParams(vmem_limit_bytes=56 << 20)


def nt(a, b):
    return lax.dot_general(a, b, (((1,), (1,)), ((), ())), preferred_element_type=F32)


def tn(a, b):
    return lax.dot_general(a, b, (((0,), (0,)), ((), ())), preferred_element_type=F32)


def nn(a, b):
    return lax.dot_general(a, b, (((1,), (0,)), ((), ())), preferred_element_type=F32)


def sds(*shape):
    return jax.ShapeDtypeStruct(shape, BF)


def tile_shift(value, step_row, step_col):
    count = lax.axis_size("seq")
    rows = count // TILES_X
    pairs = []
    for source in range(count):
        row, col = divmod(source, TILES_X)
        target = (row + step_row) % rows * TILES_X + (col + step_col) % TILES_X
        pairs.append((source, target))
    return lax.ppermute(value, "seq", pairs)


def stage_shift(value, stride, step):
    count = lax.axis_size("seq")
    pairs = []
    for source in range(count):
        digit = source // stride % 4
        pairs.append((source, source + ((digit + step) % 4 - digit) * stride))
    return lax.ppermute(value, "seq", pairs)


def gather_coarse(block):
    for stride in (16, 4):
        block = jnp.concatenate([block] + [stage_shift(block, stride, step) for step in (1, 2, 3)], 0)
    return [block] + [stage_shift(block, 1, step) for step in (1, 2, 3)]


def pack_kernel(k, v, kv, left, right, top, bottom):
    for i, x in enumerate((k, v)):
        heads = jnp.swapaxes(x[0], 0, 1)
        kv[:, i] = heads
        top[:, i] = heads[:, :EDGE]
        bottom[:, i] = heads[:, TOKENS - EDGE :]
        grid = x[0].reshape(TILE_H, TILE_W, *x.shape[2:])
        left[:, i] = jnp.swapaxes(grid[:, :RADIUS].reshape(SIDE, *x.shape[2:]), 0, 1)
        right[:, i] = jnp.swapaxes(grid[:, TILE_W - RADIUS :].reshape(SIDE, *x.shape[2:]), 0, 1)


def pack(k, v):
    h, d = k.shape[2:]
    return pl.pallas_call(
        pack_kernel,
        out_shape=[sds(h, 2, n, d) for n in (TOKENS, SIDE, SIDE, EDGE, EDGE)],
        compiler_params=PARAMS,
        name="pack",
    )(k, v)


def to_heads_kernel(x, y, a, b):
    a[...] = jnp.swapaxes(x[0], 0, 1)
    b[...] = jnp.swapaxes(y[0], 0, 1)


def to_heads(x, y):
    t, h, d = x.shape[1:]
    return pl.pallas_call(
        to_heads_kernel, out_shape=[sds(h, t, d)] * 2, compiler_params=PARAMS, name="to_heads"
    )(x, y)


def far_kernel(*refs):
    out = refs[-1]
    n = refs[0].shape[0]
    for j, piece in enumerate(refs[:-1]):
        for i in range(2):
            out[:, i, j * n : (j + 1) * n] = jnp.swapaxes(piece[:, i], 0, 1)


def far_heads(pieces):
    n, _, h, d = pieces[0].shape
    return pl.pallas_call(
        far_kernel, out_shape=sds(h, 2, n * len(pieces), d), compiler_params=PARAMS, name="far_heads"
    )(*pieces)


def to_tokens_kernel(x, y, a, b):
    a[0] = jnp.swapaxes(x[...], 0, 1)
    b[0] = jnp.swapaxes(y[...], 0, 1)


def to_tokens(x, y):
    h, t, d = x.shape
    return pl.pallas_call(
        to_tokens_kernel, out_shape=[sds(1, t, h, d)] * 2, compiler_params=PARAMS, name="to_tokens"
    )(x, y)


def merge_kernel(own, top, bottom, left, right, dk, dv):
    for i, out in enumerate((dk, dv)):
        h, d = out.shape[2:]
        def tokens(ref, *lead):
            return jnp.swapaxes(ref[:, i], 0, 1).astype(F32).reshape(*lead, h, d)
        t = tokens(own, TILE_H, TILE_W)
        u = tokens(top, RADIUS, TILE_W)
        b = tokens(bottom, RADIUS, TILE_W)
        le = tokens(left, TILE_H, RADIUS)
        ri = tokens(right, TILE_H, RADIUS)
        t = jnp.concatenate([t[:RADIUS] + u, t[RADIUS : TILE_H - RADIUS], t[TILE_H - RADIUS :] + b], 0)
        t = jnp.concatenate(
            [t[:, :RADIUS] + le, t[:, RADIUS : TILE_W - RADIUS], t[:, TILE_W - RADIUS :] + ri], 1
        )
        out[0] = t.reshape(TOKENS, h, d).astype(BF)


def merge(own, top, bottom, left, right):
    h, _, t, d = own.shape
    return pl.pallas_call(
        merge_kernel, out_shape=[sds(1, t, h, d)] * 2, compiler_params=PARAMS, name="merge"
    )(own, top, bottom, left, right)


def attend_kernel(
    heads, q, do, kv, up, dn, cup, cdn, lf, rt, far, bias, att, dq, own, gup, gdn, gcup, gcdn, glf, grt
):
    scale = q.shape[-1] ** -0.5
    half = WIN_ROWS * RADIUS
    mid = WIN_ROWS * TILE_W

    def strips(h, i):
        center = jnp.concatenate([up[h, i], kv[h, i], dn[h, i]], 0)
        sides = [
            jnp.concatenate([cup[h, i, o : o + CORNER], s[h, i], cdn[h, i, o : o + CORNER]], 0)
            for o, s in ((0, lf), (CORNER, rt))
        ]
        return center, sides[0], sides[1], far[h, i]

    def window(parts, b):
        c, l, r, f = parts
        o, s = b * BLOCK_ROWS * TILE_W, b * BLOCK_ROWS * RADIUS
        return jnp.concatenate([c[o : o + mid], l[s : s + half], r[s : s + half], f], 0)

    parts = [[strips(h, i) for i in range(2)] for h in range(heads)]
    grads = {}

    def block(h, b):
        rows = slice(b * QUERIES, (b + 1) * QUERIES)
        queries, cots = q[h, rows], do[h, rows]
        keys, values = window(parts[h][0], b), window(parts[h][1], b)
        s = nt(queries, keys)
        dp = nt(cots, values)
        yield
        s = s * (scale * LOG2E)
        s = jnp.concatenate([s[:, :NEAR] + bias[b], s[:, NEAR:]], 1)
        top = jnp.max(s, 1, keepdims=True)
        yield
        e = jnp.exp2(s - top)
        inverse = 1.0 / jnp.sum(e, 1, keepdims=True)
        yield
        p = e * inverse
        rounded = p.astype(BF)
        out = nn(rounded, values).astype(BF)
        dv = tn(rounded[:, :NEAR], cots)
        yield
        att[h, rows] = out
        delta = jnp.sum(out.astype(F32) * cots.astype(F32), 1, keepdims=True)
        ds = (p * (dp - delta) * scale).astype(BF)
        dqs = nn(ds, keys)
        dk = tn(ds[:, :NEAR], queries)
        yield
        dq[h, rows] = dqs.astype(BF)
        grads[h, b] = (dk, dv)

    live = [block(h, b) for h in range(heads) for b in range(BLOCKS)]
    while live:
        for g in list(live):
            try:
                next(g)
            except StopIteration:
                live.remove(g)

    step = BLOCK_ROWS * TILE_W
    for h in range(heads):
        for i in range(2):
            g = [grads[h, b][i] for b in range(BLOCKS)]
            c = [g[0][:step], g[0][step:mid] + g[1][:step], g[1][step:mid] + g[2][:step], g[2][step:mid]]
            c = jnp.concatenate(c, 0)
            gup[h, i] = c[:EDGE].astype(BF)
            own[h, i] = c[EDGE : EDGE + TOKENS].astype(own.dtype)
            gdn[h, i] = c[EDGE + TOKENS :].astype(BF)
            w = BLOCK_ROWS * RADIUS
            for j, out in enumerate((glf, grt)):
                s = [x[mid + j * half : mid + (j + 1) * half] for x in g]
                s = jnp.concatenate([s[0][:w], s[0][w:] + s[1][:w], s[1][w:] + s[2][:w], s[2][w:]], 0)
                o = j * CORNER
                gcup[h, i, o : o + CORNER] = s[:CORNER].astype(BF)
                out[h, i] = s[CORNER : CORNER + SIDE].astype(BF)
                gcdn[h, i, o : o + CORNER] = s[CORNER + SIDE :].astype(BF)


def attend(q, do, kv, up, dn, cup, cdn, lf, rt, far, bias, heads=2):
    h, t, d = q.shape

    def spec(x):
        return pl.BlockSpec((heads,) + x.shape[1:], lambda g, n=len(x.shape): (g,) + (0,) * (n - 1))

    args = (q, do, kv, up, dn, cup, cdn, lf, rt, far)
    outs = [sds(h, t, d)] * 2 + [sds(h, 2, n, d) for n in (t, EDGE, EDGE, 2 * CORNER, 2 * CORNER, SIDE, SIDE)]
    flops = h * BLOCKS * QUERIES * (4 * (NEAR + far.shape[2]) + 2 * NEAR) * d * 2
    return pl.pallas_call(
        functools.partial(attend_kernel, heads),
        grid=(h // heads,),
        in_specs=[spec(x) for x in args] + [pl.BlockSpec(bias.shape, lambda g: (0, 0, 0))],
        out_specs=[spec(x) for x in outs],
        out_shape=outs,
        compiler_params=PARAMS,
        cost_estimate=pl.CostEstimate(flops=flops, bytes_accessed=24 << 20, transcendentals=0),
        name="attend",
    )(*args, bias)


def near_bias():
    position = lax.axis_index("seq")
    tiles_y = lax.axis_size("seq") // TILES_X
    shape = (BLOCKS, QUERIES, NEAR)
    b = lax.broadcasted_iota(jnp.int32, shape, 0)
    i = lax.broadcasted_iota(jnp.int32, shape, 1)
    k = lax.broadcasted_iota(jnp.int32, shape, 2)
    mid = WIN_ROWS * TILE_W
    half = WIN_ROWS * RADIUS
    k_row = jnp.where(k < mid, k // TILE_W, (k - mid) % half // RADIUS) - RADIUS
    side = jnp.where(k < mid + half, k % RADIUS - RADIUS, k % RADIUS + TILE_W)
    k_col = jnp.where(k < mid, k % TILE_W, side)
    seen = (jnp.abs(k_row - i // TILE_W) <= RADIUS) & (jnp.abs(k_col - i % TILE_W) <= RADIUS)
    row = position // TILES_X * TILE_H + b * BLOCK_ROWS + k_row
    col = position % TILES_X * TILE_W + k_col
    inside = (row >= 0) & (row < tiles_y * TILE_H) & (col >= 0) & (col < TILES_X * TILE_W)
    return jnp.where(seen & inside, 0.0, FLOOR).astype(F32)


def shards(fine_queries, fine_keys, fine_values, coarse_keys, coarse_values, out_grad):
    pieces = gather_coarse(jnp.stack([coarse_keys[0], coarse_values[0]], 1))
    kv, left, right, top, bottom = pack(fine_keys, fine_values)
    rt = tile_shift(left, 0, -1)
    lf = tile_shift(right, 0, 1)
    dn = tile_shift(top, -1, 0)
    up = tile_shift(bottom, 1, 0)
    cdn = tile_shift(jnp.concatenate([lf[:, :, :CORNER], rt[:, :, :CORNER]], 2), -1, 0)
    cup = tile_shift(jnp.concatenate([lf[:, :, SIDE - CORNER :], rt[:, :, SIDE - CORNER :]], 2), 1, 0)
    queries, cots = to_heads(fine_queries, out_grad)
    far = far_heads(pieces)
    att, dq, own, gup, gdn, gcup, gcdn, glf, grt = attend(
        queries, cots, kv, up, dn, cup, cdn, lf, rt, far, near_bias()
    )
    from_dn = tile_shift(gcup, -1, 0).astype(F32)
    from_up = tile_shift(gcdn, 1, 0).astype(F32)
    bottom_grad = tile_shift(gup, -1, 0)
    top_grad = tile_shift(gdn, 1, 0)

    def folded(g, o):
        first = g[:, :, :CORNER] + from_up[:, :, o : o + CORNER]
        last = g[:, :, SIDE - CORNER :] + from_dn[:, :, o : o + CORNER]
        return jnp.concatenate([first.astype(BF), g[:, :, CORNER : SIDE - CORNER], last.astype(BF)], 2)

    right_grad = tile_shift(folded(glf, 0), 0, -1)
    left_grad = tile_shift(folded(grt, CORNER), 0, 1)
    attended, query_grad = to_tokens(att, dq)
    key_grad, value_grad = merge(own, top_grad, bottom_grad, left_grad, right_grad)
    return (attended, query_grad, key_grad, value_grad)


def solution(mesh):
    spec = P("dp", "seq", "head", None)
    return jax.shard_map(
        shards, mesh=mesh, in_specs=(spec,) * 6, out_specs=(spec,) * 4, check_vma=False
    )
```

```python
import functools

import jax
import jax.numpy as jnp
from jax import lax
from jax.experimental import pallas as pl
from jax.experimental.pallas import tpu as pltpu
from jax.sharding import PartitionSpec as P

TILE_H = 24
TILE_W = 16
RADIUS = 4
TILES_X = 8
TOKENS = TILE_H * TILE_W
EDGE = RADIUS * TILE_W
SIDE = TILE_H * RADIUS
CORNER = RADIUS * RADIUS
STRIP = SIDE + 2 * CORNER
CHUNKS = 2
BLOCK_ROWS = 8
BLOCKS = TILE_H // BLOCK_ROWS
QUERIES = BLOCK_ROWS * TILE_W
WIN_ROWS = BLOCK_ROWS + 2 * RADIUS
NEAR = WIN_ROWS * (TILE_W + 2 * RADIUS)
FLOOR = -1e30
LOG2E = 1.4426950408889634
BF = jnp.bfloat16
F32 = jnp.float32
PARAMS = pltpu.CompilerParams(vmem_limit_bytes=56 << 20)


def nt(a, b):
    return lax.dot_general(a, b, (((1,), (1,)), ((), ())), preferred_element_type=F32)


def tn(a, b):
    return lax.dot_general(a, b, (((0,), (0,)), ((), ())), preferred_element_type=F32)


def nn(a, b):
    return lax.dot_general(a, b, (((1,), (0,)), ((), ())), preferred_element_type=F32)


def sds(*shape):
    return jax.ShapeDtypeStruct(shape, BF)


def tile_shift(value, step_row, step_col):
    count = lax.axis_size("seq")
    rows = count // TILES_X
    pairs = []
    for source in range(count):
        row, col = divmod(source, TILES_X)
        target = (row + step_row) % rows * TILES_X + (col + step_col) % TILES_X
        pairs.append((source, target))
    return lax.ppermute(value, "seq", pairs)


def stage_shift(value, stride, step):
    count = lax.axis_size("seq")
    pairs = []
    for source in range(count):
        digit = source // stride % 4
        pairs.append((source, source + ((digit + step) % 4 - digit) * stride))
    return lax.ppermute(value, "seq", pairs)


def widened(block, stride):
    return jnp.concatenate([block] + [stage_shift(block, stride, step) for step in (1, 2, 3)], 0)


def pairs_to_heads_kernel(k, v, kv):
    for i, x in enumerate((k, v)):
        kv[:, i] = jnp.swapaxes(x[0], 0, 1)


def pairs_to_heads(k, v):
    t, h, d = k.shape[1:]
    return pl.pallas_call(
        pairs_to_heads_kernel, out_shape=sds(h, 2, t, d), compiler_params=PARAMS, name="pairs_to_heads"
    )(k, v)


def to_heads_kernel(x, y, a, b):
    a[...] = jnp.swapaxes(x[0], 0, 1)
    b[...] = jnp.swapaxes(y[0], 0, 1)


def to_heads(x, y):
    t, h, d = x.shape[1:]
    return pl.pallas_call(
        to_heads_kernel, out_shape=[sds(h, t, d)] * 2, compiler_params=PARAMS, name="to_heads"
    )(x, y)


def halo_to_heads_kernel(x, y, a, b):
    for i in range(2):
        a[:, i] = jnp.swapaxes(x[:, i], 0, 1)
        b[:, i] = jnp.swapaxes(y[:, i], 0, 1)


def halo_to_heads(x, y):
    t, _, h, d = x.shape
    return pl.pallas_call(
        halo_to_heads_kernel, out_shape=[sds(h, 2, t, d)] * 2, compiler_params=PARAMS, name="halo_to_heads"
    )(x, y)


def far_kernel(*refs):
    out = refs[-1]
    n = refs[0].shape[0]
    for j, piece in enumerate(refs[:-1]):
        for i in range(2):
            out[:, i, j * n : (j + 1) * n] = jnp.swapaxes(piece[:, i], 0, 1)


def far_heads(pieces):
    n, _, h, d = pieces[0].shape
    return pl.pallas_call(
        far_kernel, out_shape=sds(h, 2, n * len(pieces), d), compiler_params=PARAMS, name="far_heads"
    )(*pieces)


def sides_kernel(up, dn, kl, kr, vl, vr, *outs):
    h, d = up.shape[2:]
    n = h // CHUNKS
    for j, (mine, o) in enumerate(((( kl, vl), 0), ((kr, vr), TILE_W - RADIUS))):
        for i in range(2):
            def corner(ref):
                x = ref[:, i].reshape(RADIUS, TILE_W, h, d)[:, o : o + RADIUS]
                return x.reshape(CORNER, h, d)
            x = jnp.concatenate([corner(up), mine[i][...].reshape(SIDE, h, d), corner(dn)], 0)
            for c in range(CHUNKS):
                outs[j * CHUNKS + c][:, i] = x[:, c * n : (c + 1) * n]


def sides(up, dn, k, v):
    h, d = up.shape[2:]
    k = k.reshape(TILE_H, TILE_W, h, d)
    v = v.reshape(TILE_H, TILE_W, h, d)
    block = (TILE_H, RADIUS, h, d)
    first = pl.BlockSpec(block, lambda g: (0, 0, 0, 0))
    last = pl.BlockSpec(block, lambda g: (0, TILE_W // RADIUS - 1, 0, 0))
    whole = pl.BlockSpec(up.shape, lambda g: (0, 0, 0, 0))
    shape = (STRIP, 2, h // CHUNKS, d)
    outs = pl.pallas_call(
        sides_kernel,
        grid=(1,),
        in_specs=[whole, whole, first, last, first, last],
        out_specs=[pl.BlockSpec(shape, lambda g: (0, 0, 0, 0))] * (2 * CHUNKS),
        out_shape=[sds(*shape)] * (2 * CHUNKS),
        compiler_params=PARAMS,
        name="sides",
    )(up, dn, k, k, v, v)
    return outs[:CHUNKS], outs[CHUNKS:]


def to_tokens_kernel(*refs):
    n = (len(refs) - 2) // 2
    for j in range(2):
        x = jnp.concatenate([r[...] for r in refs[j * n : (j + 1) * n]], 0)
        refs[2 * n + j][0] = jnp.swapaxes(x, 0, 1)


def to_tokens(xs, ys):
    h, t, d = xs[0].shape
    return pl.pallas_call(
        to_tokens_kernel,
        out_shape=[sds(1, t, h * len(xs), d)] * 2,
        compiler_params=PARAMS,
        name="to_tokens",
    )(*xs, *ys)


def fold_kernel(gup, gdn, left, right, up, dn):
    for i in range(2):
        for g, o, out in ((gup, 0, up), (gdn, STRIP - CORNER, dn)):
            h, _, t, d = g.shape
            x = jnp.swapaxes(g[:, i], 0, 1).astype(F32).reshape(RADIUS, TILE_W, h, d)
            le, ri = (
                jnp.swapaxes(s[:, i, o : o + CORNER], 0, 1).astype(F32).reshape(RADIUS, RADIUS, h, d)
                for s in (left, right)
            )
            x = jnp.concatenate(
                [x[:, :RADIUS] + le, x[:, RADIUS : TILE_W - RADIUS], x[:, TILE_W - RADIUS :] + ri], 1
            )
            out[:, i] = x.reshape(t, h, d).astype(BF)


def fold(gup, gdn, left, right):
    h, _, t, d = gup.shape
    return pl.pallas_call(
        fold_kernel, out_shape=[sds(t, 2, h, d)] * 2, compiler_params=PARAMS, name="fold"
    )(gup, gdn, left, right)


def premerge_kernel(*refs):
    own, left, right = (refs[c * CHUNKS : (c + 1) * CHUNKS] for c in range(3))
    for i, out in enumerate(refs[3 * CHUNKS :]):
        h, d = out.shape[2:]

        def tokens(parts, rows, *lead):
            x = jnp.concatenate([r[:, i, rows] for r in parts], 0)
            return jnp.swapaxes(x, 0, 1).astype(F32).reshape(*lead, h, d)

        t = tokens(own, slice(0, TOKENS), TILE_H, TILE_W)
        le = tokens(left, slice(CORNER, CORNER + SIDE), TILE_H, RADIUS)
        ri = tokens(right, slice(CORNER, CORNER + SIDE), TILE_H, RADIUS)
        t = jnp.concatenate(
            [t[:, :RADIUS] + le, t[:, RADIUS : TILE_W - RADIUS], t[:, TILE_W - RADIUS :] + ri], 1
        )
        out[0] = t.reshape(TOKENS, h, d).astype(BF)


def premerge(own, left, right):
    h, _, t, d = own[0].shape
    return pl.pallas_call(
        premerge_kernel,
        out_shape=[sds(1, t, h * CHUNKS, d)] * 2,
        compiler_params=PARAMS,
        name="premerge",
    )(*own, *left, *right)


def finish_kernel(*refs):
    sums = refs[:2]
    top, bottom = (refs[2 + c * CHUNKS : 2 + (c + 1) * CHUNKS] for c in range(2))
    outs = refs[2 + 2 * CHUNKS :]
    for g, parts in enumerate((top, bottom)):

        @pl.when(pl.program_id(0) == g)
        def _():
            for i in range(2):
                x = jnp.concatenate([r[:, i] for r in parts], 1).astype(F32)
                outs[i][0] = (sums[i][0].astype(F32) + x).astype(BF)


def finish(dk, dv, top, bottom):
    h, d = dk.shape[2:]
    rows = pl.BlockSpec((1, EDGE, h, d), lambda g: (0, g * (TOKENS // EDGE - 1), 0, 0))
    part = pl.BlockSpec(top[0].shape, lambda g: (0, 0, 0, 0))
    return pl.pallas_call(
        finish_kernel,
        grid=(2,),
        in_specs=[rows, rows] + [part] * (2 * CHUNKS),
        out_specs=[rows, rows],
        out_shape=[sds(*dk.shape)] * 2,
        input_output_aliases={0: 0, 1: 1},
        compiler_params=PARAMS,
        name="finish",
    )(dk, dv, *top, *bottom)


def attend_kernel(
    heads, q, do, kv, up, dn, far, lf, rt, bias, att, dq, own, gup, gdn, glf, grt, strip_lf, strip_rt
):
    @pl.when(pl.program_id(0) == 0)
    def _():
        for src, dst in ((lf, strip_lf), (rt, strip_rt)):
            for i in range(2):
                dst[:, i] = jnp.swapaxes(src[:, i], 0, 1)

    first = pl.program_id(0) * heads
    scale = q.shape[-1] ** -0.5
    half = WIN_ROWS * RADIUS
    mid = WIN_ROWS * TILE_W

    def strips(h, i):
        center = jnp.concatenate([up[h, i], kv[h, i], dn[h, i]], 0)
        return center, strip_lf[first + h, i], strip_rt[first + h, i], far[h, i]

    def window(parts, b):
        c, l, r, f = parts
        o, s = b * BLOCK_ROWS * TILE_W, b * BLOCK_ROWS * RADIUS
        return jnp.concatenate([c[o : o + mid], l[s : s + half], r[s : s + half], f], 0)

    parts = [[strips(h, i) for i in range(2)] for h in range(heads)]
    grads = {}

    def block(h, b):
        rows = slice(b * QUERIES, (b + 1) * QUERIES)
        queries, cots = q[h, rows], do[h, rows]
        keys, values = window(parts[h][0], b), window(parts[h][1], b)
        s = nt(queries, keys)
        dp = nt(cots, values)
        yield
        s = s * (scale * LOG2E)
        s = jnp.concatenate([s[:, :NEAR] + bias[b], s[:, NEAR:]], 1)
        top = jnp.max(s, 1, keepdims=True)
        yield
        e = jnp.exp2(s - top)
        inverse = 1.0 / jnp.sum(e, 1, keepdims=True)
        yield
        p = e * inverse
        rounded = p.astype(BF)
        out = nn(rounded, values).astype(BF)
        dv = tn(rounded[:, :NEAR], cots)
        yield
        att[h, rows] = out
        delta = jnp.sum(out.astype(F32) * cots.astype(F32), 1, keepdims=True)
        ds = (p * (dp - delta) * scale).astype(BF)
        dqs = nn(ds, keys)
        dk = tn(ds[:, :NEAR], queries)
        yield
        dq[h, rows] = dqs.astype(BF)
        grads[h, b] = (dk, dv)

    live = [block(h, b) for h in range(heads) for b in range(BLOCKS)]
    while live:
        for g in list(live):
            try:
                next(g)
            except StopIteration:
                live.remove(g)

    step = BLOCK_ROWS * TILE_W
    for h in range(heads):
        for i in range(2):
            g = [grads[h, b][i] for b in range(BLOCKS)]
            c = [g[0][:step], g[0][step:mid] + g[1][:step], g[1][step:mid] + g[2][:step], g[2][step:mid]]
            c = jnp.concatenate(c, 0)
            gup[h, i] = c[:EDGE].astype(BF)
            own[h, i] = c[EDGE : EDGE + TOKENS].astype(own.dtype)
            gdn[h, i] = c[EDGE + TOKENS :].astype(BF)
            w = BLOCK_ROWS * RADIUS
            for j, out in enumerate((glf, grt)):
                s = [x[mid + j * half : mid + (j + 1) * half] for x in g]
                out[h, i] = jnp.concatenate(
                    [s[0][:w], s[0][w:] + s[1][:w], s[1][w:] + s[2][:w], s[2][w:]], 0
                ).astype(BF)


def attend(chunk, q, do, kv, up, dn, far, lf, rt, bias, heads=2):
    _, t, d = q.shape
    h = lf.shape[2]
    steps = h // heads

    def spec(x, offset=0):
        return pl.BlockSpec((heads,) + x.shape[1:], lambda g: (g + offset,) + (0,) * (len(x.shape) - 1))

    def whole(x):
        return pl.BlockSpec(x.shape, lambda g: (0,) * len(x.shape))

    outs = [sds(h, t, d)] * 2 + [sds(h, 2, n, d) for n in (t, EDGE, EDGE, STRIP, STRIP)]
    flops = h * BLOCKS * QUERIES * (4 * (NEAR + far.shape[2]) + 2 * NEAR) * d * 2
    args = (q, do, kv, up, dn, far)
    return pl.pallas_call(
        functools.partial(attend_kernel, heads),
        grid=(steps,),
        in_specs=[spec(x, chunk * steps) for x in args] + [whole(x) for x in (lf, rt, bias)],
        out_specs=[spec(x) for x in outs],
        out_shape=outs,
        scratch_shapes=[pltpu.VMEM((h, 2, STRIP, d), BF)] * 2,
        compiler_params=PARAMS,
        cost_estimate=pl.CostEstimate(flops=flops, bytes_accessed=12 << 20, transcendentals=0),
        name="attend",
    )(*args, lf, rt, bias)


def near_bias():
    position = lax.axis_index("seq")
    tiles_y = lax.axis_size("seq") // TILES_X
    shape = (BLOCKS, QUERIES, NEAR)
    b = lax.broadcasted_iota(jnp.int32, shape, 0)
    i = lax.broadcasted_iota(jnp.int32, shape, 1)
    k = lax.broadcasted_iota(jnp.int32, shape, 2)
    mid = WIN_ROWS * TILE_W
    half = WIN_ROWS * RADIUS
    k_row = jnp.where(k < mid, k // TILE_W, (k - mid) % half // RADIUS) - RADIUS
    side = jnp.where(k < mid + half, k % RADIUS - RADIUS, k % RADIUS + TILE_W)
    k_col = jnp.where(k < mid, k % TILE_W, side)
    seen = (jnp.abs(k_row - i // TILE_W) <= RADIUS) & (jnp.abs(k_col - i % TILE_W) <= RADIUS)
    row = position // TILES_X * TILE_H + b * BLOCK_ROWS + k_row
    col = position % TILES_X * TILE_W + k_col
    inside = (row >= 0) & (row < tiles_y * TILE_H) & (col >= 0) & (col < TILES_X * TILE_W)
    return jnp.where(seen & inside, 0.0, FLOOR).astype(F32)


def shards(fine_queries, fine_keys, fine_values, coarse_keys, coarse_values, out_grad):
    k, v = fine_keys[0], fine_values[0]
    coarse = widened(jnp.stack([coarse_keys[0], coarse_values[0]], 1), 4)
    first = jnp.stack([k[:EDGE], v[:EDGE]], 1)
    last = jnp.stack([k[TOKENS - EDGE :], v[TOKENS - EDGE :]], 1)
    coarse, first, last = lax.optimization_barrier((coarse, first, last))
    dn = tile_shift(first, -1, 0)
    up = tile_shift(last, 1, 0)
    coarse = widened(coarse, 16)
    coarse, q, do, fk, fv = lax.optimization_barrier((coarse, fine_queries, out_grad, fine_keys, fine_values))
    pieces = [coarse] + [stage_shift(coarse, 1, step) for step in (1, 2, 3)]
    queries, cots = to_heads(q, do)
    kv = pairs_to_heads(fk, fv)
    up, dn, kv, queries, cots = lax.optimization_barrier((up, dn, kv, queries, cots))
    left, right = sides(up, dn, k, v)
    rt = [tile_shift(x, 0, -1) for x in left]
    lf = [tile_shift(x, 0, 1) for x in right]
    up, dn = halo_to_heads(up, dn)
    far = far_heads(pieces)
    bias = near_bias()
    att, dq, own, top, bottom, from_left, from_right = ([] for _ in range(7))
    for c in range(CHUNKS):
        a, b, mine, gup, gdn, glf, grt = attend(c, queries, cots, kv, up, dn, far, lf[c], rt[c], bias)
        from_right.append(tile_shift(glf, 0, -1))
        from_left.append(tile_shift(grt, 0, 1))
        gup, gdn = fold(gup, gdn, from_left[c], from_right[c])
        bottom.append(tile_shift(gup, -1, 0))
        top.append(tile_shift(gdn, 1, 0))
        att.append(a)
        dq.append(b)
        own.append(mine)
    attended, query_grad = to_tokens(att, dq)
    dk, dv = premerge(own, from_left, from_right)
    key_grad, value_grad = finish(dk, dv, top, bottom)
    return (attended, query_grad, key_grad, value_grad)


def solution(mesh):
    spec = P("dp", "seq", "head", None)
    return jax.shard_map(
        shards, mesh=mesh, in_specs=(spec,) * 6, out_specs=(spec,) * 4, check_vma=False
    )
```

```python
import functools

import jax
import jax.numpy as jnp
from jax import lax
from jax.experimental import pallas as pl
from jax.experimental.pallas import tpu as pltpu
from jax.sharding import PartitionSpec as P

TILE_H = 24
TILE_W = 16
RADIUS = 4
TILES_X = 8
TOKENS = TILE_H * TILE_W
EDGE = RADIUS * TILE_W
SIDE = TILE_H * RADIUS
CORNER = RADIUS * RADIUS
STRIP = SIDE + 2 * CORNER
CHUNKS = 2
BLOCK_ROWS = 8
BLOCKS = TILE_H // BLOCK_ROWS
QUERIES = BLOCK_ROWS * TILE_W
WIN_ROWS = BLOCK_ROWS + 2 * RADIUS
NEAR = WIN_ROWS * (TILE_W + 2 * RADIUS)
FLOOR = -1e30
LOG2E = 1.4426950408889634
BF = jnp.bfloat16
F32 = jnp.float32
PARAMS = pltpu.CompilerParams(vmem_limit_bytes=62 << 20)


def nt(a, b):
    return lax.dot_general(a, b, (((1,), (1,)), ((), ())), preferred_element_type=F32)


def tn(a, b):
    return lax.dot_general(a, b, (((0,), (0,)), ((), ())), preferred_element_type=F32)


def nn(a, b):
    return lax.dot_general(a, b, (((1,), (0,)), ((), ())), preferred_element_type=F32)


def sds(*shape):
    return jax.ShapeDtypeStruct(shape, BF)


def tile_shift(value, step_row, step_col):
    count = lax.axis_size("seq")
    rows = count // TILES_X
    pairs = []
    for source in range(count):
        row, col = divmod(source, TILES_X)
        target = (row + step_row) % rows * TILES_X + (col + step_col) % TILES_X
        pairs.append((source, target))
    return lax.ppermute(value, "seq", pairs)


def stage_shift(value, stride, step):
    count = lax.axis_size("seq")
    pairs = []
    for source in range(count):
        digit = source // stride % 4
        pairs.append((source, source + ((digit + step) % 4 - digit) * stride))
    return lax.ppermute(value, "seq", pairs)


def widened(block, stride):
    return jnp.concatenate([block] + [stage_shift(block, stride, step) for step in (1, 2, 3)], 0)


def pairs_to_heads_kernel(k, v, kv):
    for i, x in enumerate((k, v)):
        kv[:, i] = jnp.swapaxes(x[0], 0, 1)


def pairs_to_heads(k, v):
    t, h, d = k.shape[1:]
    return pl.pallas_call(
        pairs_to_heads_kernel, out_shape=sds(h, 2, t, d), compiler_params=PARAMS, name="pairs_to_heads"
    )(k, v)


def to_heads_kernel(x, y, a, b):
    a[...] = jnp.swapaxes(x[0], 0, 1)
    b[...] = jnp.swapaxes(y[0], 0, 1)


def to_heads(x, y):
    t, h, d = x.shape[1:]
    return pl.pallas_call(
        to_heads_kernel, out_shape=[sds(h, t, d)] * 2, compiler_params=PARAMS, name="to_heads"
    )(x, y)


def halo_to_heads_kernel(x, y, a, b):
    for i in range(2):
        a[:, i] = jnp.swapaxes(x[:, i], 0, 1)
        b[:, i] = jnp.swapaxes(y[:, i], 0, 1)


def halo_to_heads(x, y):
    t, _, h, d = x.shape
    return pl.pallas_call(
        halo_to_heads_kernel, out_shape=[sds(h, 2, t, d)] * 2, compiler_params=PARAMS, name="halo_to_heads"
    )(x, y)


def far_kernel(*refs):
    out = refs[-1]
    n = refs[0].shape[0]
    for j, piece in enumerate(refs[:-1]):
        for i in range(2):
            out[:, i, j * n : (j + 1) * n] = jnp.swapaxes(piece[:, i], 0, 1)


def far_heads(pieces):
    n, _, h, d = pieces[0].shape
    return pl.pallas_call(
        far_kernel, out_shape=sds(h, 2, n * len(pieces), d), compiler_params=PARAMS, name="far_heads"
    )(*pieces)


def sides_kernel(up, dn, kl, kr, vl, vr, *outs):
    h, d = up.shape[2:]
    n = h // CHUNKS
    for j, (mine, o) in enumerate(((( kl, vl), 0), ((kr, vr), TILE_W - RADIUS))):
        for i in range(2):
            def corner(ref):
                x = ref[:, i].reshape(RADIUS, TILE_W, h, d)[:, o : o + RADIUS]
                return x.reshape(CORNER, h, d)
            x = jnp.concatenate([corner(up), mine[i][...].reshape(SIDE, h, d), corner(dn)], 0)
            for c in range(CHUNKS):
                outs[j * CHUNKS + c][:, i] = x[:, c * n : (c + 1) * n]


def sides(up, dn, k, v):
    h, d = up.shape[2:]
    k = k.reshape(TILE_H, TILE_W, h, d)
    v = v.reshape(TILE_H, TILE_W, h, d)
    block = (TILE_H, RADIUS, h, d)
    first = pl.BlockSpec(block, lambda g: (0, 0, 0, 0))
    last = pl.BlockSpec(block, lambda g: (0, TILE_W // RADIUS - 1, 0, 0))
    whole = pl.BlockSpec(up.shape, lambda g: (0, 0, 0, 0))
    shape = (STRIP, 2, h // CHUNKS, d)
    outs = pl.pallas_call(
        sides_kernel,
        grid=(1,),
        in_specs=[whole, whole, first, last, first, last],
        out_specs=[pl.BlockSpec(shape, lambda g: (0, 0, 0, 0))] * (2 * CHUNKS),
        out_shape=[sds(*shape)] * (2 * CHUNKS),
        compiler_params=PARAMS,
        name="sides",
    )(up, dn, k, k, v, v)
    return outs[:CHUNKS], outs[CHUNKS:]


def to_tokens_kernel(*refs):
    n = (len(refs) - 2) // 2
    for j in range(2):
        x = jnp.concatenate([r[...] for r in refs[j * n : (j + 1) * n]], 0)
        refs[2 * n + j][0] = jnp.swapaxes(x, 0, 1)


def to_tokens(xs, ys):
    h, t, d = xs[0].shape
    return pl.pallas_call(
        to_tokens_kernel,
        out_shape=[sds(1, t, h * len(xs), d)] * 2,
        compiler_params=PARAMS,
        name="to_tokens",
    )(*xs, *ys)


def fold_kernel(gup, gdn, left, right, up, dn):
    for i in range(2):
        for g, o, out in ((gup, 0, up), (gdn, STRIP - CORNER, dn)):
            h, _, t, d = g.shape
            x = jnp.swapaxes(g[:, i], 0, 1).astype(F32).reshape(RADIUS, TILE_W, h, d)
            le, ri = (
                jnp.swapaxes(s[:, i, o : o + CORNER], 0, 1).astype(F32).reshape(RADIUS, RADIUS, h, d)
                for s in (left, right)
            )
            x = jnp.concatenate(
                [x[:, :RADIUS] + le, x[:, RADIUS : TILE_W - RADIUS], x[:, TILE_W - RADIUS :] + ri], 1
            )
            out[:, i] = x.reshape(t, h, d).astype(BF)


def fold(gup, gdn, left, right):
    h, _, t, d = gup.shape
    return pl.pallas_call(
        fold_kernel, out_shape=[sds(t, 2, h, d)] * 2, compiler_params=PARAMS, name="fold"
    )(gup, gdn, left, right)


def premerge_kernel(*refs):
    own, left, right = (refs[c * CHUNKS : (c + 1) * CHUNKS] for c in range(3))
    for i, out in enumerate(refs[3 * CHUNKS :]):
        h, d = out.shape[2:]

        def tokens(parts, rows, *lead):
            x = jnp.concatenate([r[:, i, rows] for r in parts], 0)
            return jnp.swapaxes(x, 0, 1).astype(F32).reshape(*lead, h, d)

        t = tokens(own, slice(0, TOKENS), TILE_H, TILE_W)
        le = tokens(left, slice(CORNER, CORNER + SIDE), TILE_H, RADIUS)
        ri = tokens(right, slice(CORNER, CORNER + SIDE), TILE_H, RADIUS)
        t = jnp.concatenate(
            [t[:, :RADIUS] + le, t[:, RADIUS : TILE_W - RADIUS], t[:, TILE_W - RADIUS :] + ri], 1
        )
        out[0] = t.reshape(TOKENS, h, d).astype(BF)


def premerge(own, left, right):
    h, _, t, d = own[0].shape
    return pl.pallas_call(
        premerge_kernel,
        out_shape=[sds(1, t, h * CHUNKS, d)] * 2,
        compiler_params=PARAMS,
        name="premerge",
    )(*own, *left, *right)


def finish_kernel(*refs):
    sums = refs[:2]
    top, bottom = (refs[2 + c * CHUNKS : 2 + (c + 1) * CHUNKS] for c in range(2))
    outs = refs[2 + 2 * CHUNKS :]
    for g, parts in enumerate((top, bottom)):

        @pl.when(pl.program_id(0) == g)
        def _():
            for i in range(2):
                x = jnp.concatenate([r[:, i] for r in parts], 1).astype(F32)
                outs[i][0] = (sums[i][0].astype(F32) + x).astype(BF)


def finish(dk, dv, top, bottom):
    h, d = dk.shape[2:]
    rows = pl.BlockSpec((1, EDGE, h, d), lambda g: (0, g * (TOKENS // EDGE - 1), 0, 0))
    part = pl.BlockSpec(top[0].shape, lambda g: (0, 0, 0, 0))
    return pl.pallas_call(
        finish_kernel,
        grid=(2,),
        in_specs=[rows, rows] + [part] * (2 * CHUNKS),
        out_specs=[rows, rows],
        out_shape=[sds(*dk.shape)] * 2,
        input_output_aliases={0: 0, 1: 1},
        compiler_params=PARAMS,
        name="finish",
    )(dk, dv, *top, *bottom)


def attend_kernel(
    heads, q, do, kv, up, dn, far, lf, rt, bias, att, dq, own, gup, gdn, glf, grt, strip_lf, strip_rt
):
    @pl.when(pl.program_id(0) == 0)
    def _():
        for src, dst in ((lf, strip_lf), (rt, strip_rt)):
            for i in range(2):
                dst[:, i] = jnp.swapaxes(src[:, i], 0, 1)

    first = pl.program_id(0) * heads
    scale = q.shape[-1] ** -0.5
    half = WIN_ROWS * RADIUS
    mid = WIN_ROWS * TILE_W

    def strips(h, i):
        center = jnp.concatenate([up[h, i], kv[h, i], dn[h, i]], 0)
        return center, strip_lf[first + h, i], strip_rt[first + h, i], far[h, i]

    def window(parts, b):
        c, l, r, f = parts
        o, s = b * BLOCK_ROWS * TILE_W, b * BLOCK_ROWS * RADIUS
        return jnp.concatenate([c[o : o + mid], l[s : s + half], r[s : s + half], f], 0)

    parts = [[strips(h, i) for i in range(2)] for h in range(heads)]
    grads = {}

    def block(h, b):
        rows = slice(b * QUERIES, (b + 1) * QUERIES)
        queries, cots = q[h, rows], do[h, rows]
        keys, values = window(parts[h][0], b), window(parts[h][1], b)
        s = nt(queries, keys)
        dp = nt(cots, values)
        yield
        s = s * (scale * LOG2E)
        s = jnp.concatenate([s[:, :NEAR] + bias[b], s[:, NEAR:]], 1)
        top = jnp.max(s, 1, keepdims=True)
        yield
        e = jnp.exp2(s - top)
        inverse = 1.0 / jnp.sum(e, 1, keepdims=True)
        yield
        p = e * inverse
        rounded = p.astype(BF)
        out = nn(rounded, values).astype(BF)
        dv = tn(rounded[:, :NEAR], cots)
        yield
        att[h, rows] = out
        delta = jnp.sum(out.astype(F32) * cots.astype(F32), 1, keepdims=True)
        ds = (p * (dp - delta) * scale).astype(BF)
        dqs = nn(ds, keys)
        dk = tn(ds[:, :NEAR], queries)
        yield
        dq[h, rows] = dqs.astype(BF)
        grads[h, b] = (dk, dv)

    live = [block(h, b) for h in range(heads) for b in range(BLOCKS)]
    while live:
        for g in list(live):
            try:
                next(g)
            except StopIteration:
                live.remove(g)

    step = BLOCK_ROWS * TILE_W
    for h in range(heads):
        for i in range(2):
            g = [grads[h, b][i] for b in range(BLOCKS)]
            c = [g[0][:step], g[0][step:mid] + g[1][:step], g[1][step:mid] + g[2][:step], g[2][step:mid]]
            c = jnp.concatenate(c, 0)
            gup[h, i] = c[:EDGE].astype(BF)
            own[h, i] = c[EDGE : EDGE + TOKENS].astype(own.dtype)
            gdn[h, i] = c[EDGE + TOKENS :].astype(BF)
            w = BLOCK_ROWS * RADIUS
            for j, out in enumerate((glf, grt)):
                s = [x[mid + j * half : mid + (j + 1) * half] for x in g]
                out[h, i] = jnp.concatenate(
                    [s[0][:w], s[0][w:] + s[1][:w], s[1][w:] + s[2][:w], s[2][w:]], 0
                ).astype(BF)


def attend(chunk, q, do, kv, up, dn, far, lf, rt, bias, heads=2):
    _, t, d = q.shape
    h = lf.shape[2]
    steps = h // heads

    def spec(x, offset=0):
        return pl.BlockSpec((heads,) + x.shape[1:], lambda g: (g + offset,) + (0,) * (len(x.shape) - 1))

    def whole(x):
        return pl.BlockSpec(x.shape, lambda g: (0,) * len(x.shape))

    outs = [sds(h, t, d)] * 2 + [sds(h, 2, n, d) for n in (t, EDGE, EDGE, STRIP, STRIP)]
    flops = h * BLOCKS * QUERIES * (4 * (NEAR + far.shape[2]) + 2 * NEAR) * d * 2
    args = (q, do, kv, up, dn, far)
    return pl.pallas_call(
        functools.partial(attend_kernel, heads),
        grid=(steps,),
        in_specs=[spec(x, chunk * steps) for x in args] + [whole(x) for x in (lf, rt, bias)],
        out_specs=[spec(x) for x in outs],
        out_shape=outs,
        scratch_shapes=[pltpu.VMEM((h, 2, STRIP, d), BF)] * 2,
        compiler_params=PARAMS,
        cost_estimate=pl.CostEstimate(flops=flops, bytes_accessed=12 << 20, transcendentals=0),
        name="attend",
    )(*args, lf, rt, bias)


def near_bias():
    position = lax.axis_index("seq")
    tiles_y = lax.axis_size("seq") // TILES_X
    shape = (BLOCKS, QUERIES, NEAR)
    b = lax.broadcasted_iota(jnp.int32, shape, 0)
    i = lax.broadcasted_iota(jnp.int32, shape, 1)
    k = lax.broadcasted_iota(jnp.int32, shape, 2)
    mid = WIN_ROWS * TILE_W
    half = WIN_ROWS * RADIUS
    k_row = jnp.where(k < mid, k // TILE_W, (k - mid) % half // RADIUS) - RADIUS
    side = jnp.where(k < mid + half, k % RADIUS - RADIUS, k % RADIUS + TILE_W)
    k_col = jnp.where(k < mid, k % TILE_W, side)
    seen = (jnp.abs(k_row - i // TILE_W) <= RADIUS) & (jnp.abs(k_col - i % TILE_W) <= RADIUS)
    row = position // TILES_X * TILE_H + b * BLOCK_ROWS + k_row
    col = position % TILES_X * TILE_W + k_col
    inside = (row >= 0) & (row < tiles_y * TILE_H) & (col >= 0) & (col < TILES_X * TILE_W)
    return jnp.where(seen & inside, 0.0, FLOOR).astype(F32)


def shards(fine_queries, fine_keys, fine_values, coarse_keys, coarse_values, out_grad):
    k, v = fine_keys[0], fine_values[0]
    coarse = widened(widened(jnp.stack([coarse_keys[0], coarse_values[0]], 1), 16), 4)
    first = jnp.stack([k[:EDGE], v[:EDGE]], 1)
    last = jnp.stack([k[TOKENS - EDGE :], v[TOKENS - EDGE :]], 1)
    coarse, first, last, fine_queries, out_grad, fine_keys, fine_values = lax.optimization_barrier(
        (coarse, first, last, fine_queries, out_grad, fine_keys, fine_values)
    )
    dn = tile_shift(first, -1, 0)
    up = tile_shift(last, 1, 0)
    pieces = [coarse] + [stage_shift(coarse, 1, step) for step in (1, 2, 3)]
    queries, cots = to_heads(fine_queries, out_grad)
    kv = pairs_to_heads(fine_keys, fine_values)
    up, dn, kv, queries, cots = lax.optimization_barrier((up, dn, kv, queries, cots))
    left, right = sides(up, dn, k, v)
    rt = [tile_shift(x, 0, -1) for x in left]
    lf = [tile_shift(x, 0, 1) for x in right]
    up, dn = halo_to_heads(up, dn)
    far = far_heads(pieces)
    bias = near_bias()
    att, dq, own, top, bottom, from_left, from_right = ([] for _ in range(7))
    for c in range(CHUNKS):
        a, b, mine, gup, gdn, glf, grt = attend(c, queries, cots, kv, up, dn, far, lf[c], rt[c], bias)
        from_right.append(tile_shift(glf, 0, -1))
        from_left.append(tile_shift(grt, 0, 1))
        att.append(a)
        dq.append(b)
        own.append(mine)
        if c == CHUNKS - 1:
            attended, query_grad, from_left[c], from_right[c] = lax.optimization_barrier(
                (*to_tokens(att, dq), from_left[c], from_right[c])
            )
        gup, gdn = fold(gup, gdn, from_left[c], from_right[c])
        bottom.append(tile_shift(gup, -1, 0))
        top.append(tile_shift(gdn, 1, 0))
    dk, dv = premerge(own, from_left, from_right)
    key_grad, value_grad = finish(dk, dv, top, bottom)
    return (attended, query_grad, key_grad, value_grad)


def solution(mesh):
    spec = P("dp", "seq", "head", None)
    return jax.shard_map(
        shards, mesh=mesh, in_specs=(spec,) * 6, out_specs=(spec,) * 4, check_vma=False
    )
```

```python
import functools

import jax
import jax.numpy as jnp
from jax import lax
from jax.experimental import pallas as pl
from jax.experimental.pallas import tpu as pltpu
from jax.sharding import PartitionSpec as P

TILE_H = 24
TILE_W = 16
RADIUS = 4
TILES_X = 8
TOKENS = TILE_H * TILE_W
EDGE = RADIUS * TILE_W
SIDE = TILE_H * RADIUS
CORNER = RADIUS * RADIUS
STRIP = SIDE + 2 * CORNER
CHUNKS = 2
BLOCK_ROWS = 8
BLOCKS = TILE_H // BLOCK_ROWS
QUERIES = BLOCK_ROWS * TILE_W
WIN_ROWS = BLOCK_ROWS + 2 * RADIUS
NEAR = WIN_ROWS * (TILE_W + 2 * RADIUS)
FLOOR = -1e30
LOG2E = 1.4426950408889634
BF = jnp.bfloat16
F32 = jnp.float32
PARAMS = pltpu.CompilerParams(vmem_limit_bytes=62 << 20)


def nt(a, b):
    return lax.dot_general(a, b, (((1,), (1,)), ((), ())), preferred_element_type=F32)


def tn(a, b):
    return lax.dot_general(a, b, (((0,), (0,)), ((), ())), preferred_element_type=F32)


def nn(a, b):
    return lax.dot_general(a, b, (((1,), (0,)), ((), ())), preferred_element_type=F32)


def sds(*shape):
    return jax.ShapeDtypeStruct(shape, BF)


def tile_shift(value, step_row, step_col):
    count = lax.axis_size("seq")
    rows = count // TILES_X
    pairs = []
    for source in range(count):
        row, col = source // TILES_X + step_row, source % TILES_X + step_col
        if 0 <= row < rows and 0 <= col < TILES_X:
            pairs.append((source, row * TILES_X + col))
    return lax.ppermute(value, "seq", pairs)


def stage_shift(value, stride, step):
    count = lax.axis_size("seq")
    pairs = []
    for source in range(count):
        digit = source // stride % 4
        pairs.append((source, source + ((digit + step) % 4 - digit) * stride))
    return lax.ppermute(value, "seq", pairs)


def widened(block, stride):
    return jnp.concatenate([block] + [stage_shift(block, stride, step) for step in (1, 2, 3)], 0)


def pairs_to_heads_kernel(k, v, kv):
    for i, x in enumerate((k, v)):
        kv[:, i] = jnp.swapaxes(x[0], 0, 1)


def pairs_to_heads(k, v):
    t, h, d = k.shape[1:]
    return pl.pallas_call(
        pairs_to_heads_kernel, out_shape=sds(h, 2, t, d), compiler_params=PARAMS, name="pairs_to_heads"
    )(k, v)


def to_heads_kernel(x, y, a, b):
    a[...] = jnp.swapaxes(x[0], 0, 1)
    b[...] = jnp.swapaxes(y[0], 0, 1)


def to_heads(x, y):
    t, h, d = x.shape[1:]
    return pl.pallas_call(
        to_heads_kernel, out_shape=[sds(h, t, d)] * 2, compiler_params=PARAMS, name="to_heads"
    )(x, y)


def halo_to_heads_kernel(x, y, a, b):
    for i in range(2):
        a[:, i] = jnp.swapaxes(x[:, i], 0, 1)
        b[:, i] = jnp.swapaxes(y[:, i], 0, 1)


def halo_to_heads(x, y):
    t, _, h, d = x.shape
    return pl.pallas_call(
        halo_to_heads_kernel, out_shape=[sds(h, 2, t, d)] * 2, compiler_params=PARAMS, name="halo_to_heads"
    )(x, y)


def far_kernel(*refs):
    out = refs[-1]
    n = refs[0].shape[0]
    for j, piece in enumerate(refs[:-1]):
        for i in range(2):
            out[:, i, j * n : (j + 1) * n] = jnp.swapaxes(piece[:, i], 0, 1)


def far_heads(pieces):
    n, _, h, d = pieces[0].shape
    return pl.pallas_call(
        far_kernel, out_shape=sds(h, 2, n * len(pieces), d), compiler_params=PARAMS, name="far_heads"
    )(*pieces)


def columns_kernel(kl, kr, vl, vr, *outs):
    h, d = kl.shape[2:]
    n = h // CHUNKS
    for j, mine in enumerate(((kl, vl), (kr, vr))):
        for i in range(2):
            x = mine[i][...].reshape(SIDE, h, d)
            for c in range(CHUNKS):
                outs[j * CHUNKS + c][CORNER : CORNER + SIDE, i] = x[:, c * n : (c + 1) * n]


def columns(k, v):
    h, d = k.shape[1:]
    k = k.reshape(TILE_H, TILE_W, h, d)
    v = v.reshape(TILE_H, TILE_W, h, d)
    block = (TILE_H, RADIUS, h, d)
    first = pl.BlockSpec(block, lambda g: (0, 0, 0, 0))
    last = pl.BlockSpec(block, lambda g: (0, TILE_W // RADIUS - 1, 0, 0))
    shape = (STRIP, 2, h // CHUNKS, d)
    return pl.pallas_call(
        columns_kernel,
        grid=(1,),
        in_specs=[first, last, first, last],
        out_specs=[pl.BlockSpec(shape, lambda g: (0, 0, 0, 0))] * (2 * CHUNKS),
        out_shape=[sds(*shape)] * (2 * CHUNKS),
        compiler_params=PARAMS,
        name="columns",
    )(k, k, v, v)


def corners_kernel(up, dn, *refs):
    outs = refs[len(refs) // 2 :]
    h, d = up.shape[2:]
    n = h // CHUNKS
    for g, rows in enumerate((up, dn)):

        @pl.when(pl.program_id(0) == g)
        def _():
            for j, o in enumerate((0, TILE_W - RADIUS)):
                for i in range(2):
                    x = rows[:, i].reshape(RADIUS, TILE_W, h, d)[:, o : o + RADIUS]
                    x = x.reshape(CORNER, h, d)
                    for c in range(CHUNKS):
                        outs[j * CHUNKS + c][:, i] = x[:, c * n : (c + 1) * n]


def corners(up, dn, strips):
    whole = pl.BlockSpec(up.shape, lambda g: (0, 0, 0, 0))
    end = pl.BlockSpec((CORNER,) + strips[0].shape[1:], lambda g: (g * (STRIP // CORNER - 1), 0, 0, 0))
    outs = pl.pallas_call(
        corners_kernel,
        grid=(2,),
        in_specs=[whole, whole] + [pl.BlockSpec(memory_space=pl.ANY)] * len(strips),
        out_specs=[end] * len(strips),
        out_shape=[sds(*x.shape) for x in strips],
        input_output_aliases={2 + i: i for i in range(len(strips))},
        compiler_params=PARAMS,
        name="corners",
    )(up, dn, *strips)
    return outs[:CHUNKS], outs[CHUNKS:]


def to_tokens_kernel(*refs):
    n = (len(refs) - 2) // 2
    for j in range(2):
        x = jnp.concatenate([r[...] for r in refs[j * n : (j + 1) * n]], 0)
        refs[2 * n + j][0] = jnp.swapaxes(x, 0, 1)


def to_tokens(xs, ys):
    h, t, d = xs[0].shape
    return pl.pallas_call(
        to_tokens_kernel,
        out_shape=[sds(1, t, h * len(xs), d)] * 2,
        compiler_params=PARAMS,
        name="to_tokens",
    )(*xs, *ys)


def fold_kernel(gup, gdn, left, right, up, dn):
    for i in range(2):
        for g, o, out in ((gup, 0, up), (gdn, STRIP - CORNER, dn)):
            h, _, t, d = g.shape
            x = jnp.swapaxes(g[:, i], 0, 1).astype(F32).reshape(RADIUS, TILE_W, h, d)
            le, ri = (
                jnp.swapaxes(s[:, i, o : o + CORNER], 0, 1).astype(F32).reshape(RADIUS, RADIUS, h, d)
                for s in (left, right)
            )
            x = jnp.concatenate(
                [x[:, :RADIUS] + le, x[:, RADIUS : TILE_W - RADIUS], x[:, TILE_W - RADIUS :] + ri], 1
            )
            out[:, i] = x.reshape(t, h, d).astype(BF)


def fold(gup, gdn, left, right):
    h, _, t, d = gup.shape
    return pl.pallas_call(
        fold_kernel, out_shape=[sds(t, 2, h, d)] * 2, compiler_params=PARAMS, name="fold"
    )(gup, gdn, left, right)


def premerge_kernel(*refs):
    own, left, right = (refs[c * CHUNKS : (c + 1) * CHUNKS] for c in range(3))
    for i, out in enumerate(refs[3 * CHUNKS :]):
        h, d = out.shape[2:]

        def tokens(parts, rows, *lead):
            x = jnp.concatenate([r[:, i, rows] for r in parts], 0)
            return jnp.swapaxes(x, 0, 1).astype(F32).reshape(*lead, h, d)

        t = tokens(own, slice(0, TOKENS), TILE_H, TILE_W)
        le = tokens(left, slice(CORNER, CORNER + SIDE), TILE_H, RADIUS)
        ri = tokens(right, slice(CORNER, CORNER + SIDE), TILE_H, RADIUS)
        t = jnp.concatenate(
            [t[:, :RADIUS] + le, t[:, RADIUS : TILE_W - RADIUS], t[:, TILE_W - RADIUS :] + ri], 1
        )
        out[0] = t.reshape(TOKENS, h, d).astype(BF)


def premerge(own, left, right):
    h, _, t, d = own[0].shape
    return pl.pallas_call(
        premerge_kernel,
        out_shape=[sds(1, t, h * CHUNKS, d)] * 2,
        compiler_params=PARAMS,
        name="premerge",
    )(*own, *left, *right)


def finish_kernel(*refs):
    sums = refs[:2]
    top, bottom = (refs[2 + c * CHUNKS : 2 + (c + 1) * CHUNKS] for c in range(2))
    outs = refs[2 + 2 * CHUNKS :]
    for g, parts in enumerate((top, bottom)):

        @pl.when(pl.program_id(0) == g)
        def _():
            for i in range(2):
                x = jnp.concatenate([r[:, i] for r in parts], 1).astype(F32)
                outs[i][0] = (sums[i][0].astype(F32) + x).astype(BF)


def finish(dk, dv, top, bottom):
    h, d = dk.shape[2:]
    rows = pl.BlockSpec((1, EDGE, h, d), lambda g: (0, g * (TOKENS // EDGE - 1), 0, 0))
    part = pl.BlockSpec(top[0].shape, lambda g: (0, 0, 0, 0))
    return pl.pallas_call(
        finish_kernel,
        grid=(2,),
        in_specs=[rows, rows] + [part] * (2 * CHUNKS),
        out_specs=[rows, rows],
        out_shape=[sds(*dk.shape)] * 2,
        input_output_aliases={0: 0, 1: 1},
        compiler_params=PARAMS,
        name="finish",
    )(dk, dv, *top, *bottom)


def attend_kernel(
    heads, q, do, kv, up, dn, far, lf, rt, bias, att, dq, own, gup, gdn, glf, grt, strip_lf, strip_rt
):
    @pl.when(pl.program_id(0) == 0)
    def _():
        for src, dst in ((lf, strip_lf), (rt, strip_rt)):
            for i in range(2):
                dst[:, i] = jnp.swapaxes(src[:, i], 0, 1)

    first = pl.program_id(0) * heads
    scale = q.shape[-1] ** -0.5
    half = WIN_ROWS * RADIUS
    mid = WIN_ROWS * TILE_W

    def strips(h, i):
        center = jnp.concatenate([up[h, i], kv[h, i], dn[h, i]], 0)
        return center, strip_lf[first + h, i], strip_rt[first + h, i], far[h, i]

    def window(parts, b):
        c, l, r, f = parts
        o, s = b * BLOCK_ROWS * TILE_W, b * BLOCK_ROWS * RADIUS
        return jnp.concatenate([c[o : o + mid], l[s : s + half], r[s : s + half], f], 0)

    parts = [[strips(h, i) for i in range(2)] for h in range(heads)]
    grads = {}

    def block(h, b):
        rows = slice(b * QUERIES, (b + 1) * QUERIES)
        queries, cots = q[h, rows], do[h, rows]
        keys, values = window(parts[h][0], b), window(parts[h][1], b)
        s = nt(queries, keys)
        dp = nt(cots, values)
        yield
        s = s * (scale * LOG2E)
        s = jnp.concatenate([s[:, :NEAR] + bias[b], s[:, NEAR:]], 1)
        top = jnp.max(s, 1, keepdims=True)
        yield
        e = jnp.exp2(s - top)
        inverse = 1.0 / jnp.sum(e, 1, keepdims=True)
        yield
        p = e * inverse
        rounded = p.astype(BF)
        out = nn(rounded, values).astype(BF)
        dv = tn(rounded[:, :NEAR], cots)
        yield
        att[h, rows] = out
        delta = jnp.sum(out.astype(F32) * cots.astype(F32), 1, keepdims=True)
        ds = (p * (dp - delta) * scale).astype(BF)
        dqs = nn(ds, keys)
        dk = tn(ds[:, :NEAR], queries)
        yield
        dq[h, rows] = dqs.astype(BF)
        grads[h, b] = (dk, dv)

    live = [block(h, b) for h in range(heads) for b in range(BLOCKS)]
    while live:
        for g in list(live):
            try:
                next(g)
            except StopIteration:
                live.remove(g)

    step = BLOCK_ROWS * TILE_W
    for h in range(heads):
        for i in range(2):
            g = [grads[h, b][i] for b in range(BLOCKS)]
            c = [g[0][:step], g[0][step:mid] + g[1][:step], g[1][step:mid] + g[2][:step], g[2][step:mid]]
            c = jnp.concatenate(c, 0)
            gup[h, i] = c[:EDGE].astype(BF)
            own[h, i] = c[EDGE : EDGE + TOKENS].astype(own.dtype)
            gdn[h, i] = c[EDGE + TOKENS :].astype(BF)
            w = BLOCK_ROWS * RADIUS
            for j, out in enumerate((glf, grt)):
                s = [x[mid + j * half : mid + (j + 1) * half] for x in g]
                out[h, i] = jnp.concatenate(
                    [s[0][:w], s[0][w:] + s[1][:w], s[1][w:] + s[2][:w], s[2][w:]], 0
                ).astype(BF)


def attend(chunk, q, do, kv, up, dn, far, lf, rt, bias, heads=2):
    _, t, d = q.shape
    h = lf.shape[2]
    steps = h // heads

    def spec(x, offset=0):
        return pl.BlockSpec((heads,) + x.shape[1:], lambda g: (g + offset,) + (0,) * (len(x.shape) - 1))

    def whole(x):
        return pl.BlockSpec(x.shape, lambda g: (0,) * len(x.shape))

    outs = [sds(h, t, d)] * 2 + [sds(h, 2, n, d) for n in (t, EDGE, EDGE, STRIP, STRIP)]
    flops = h * BLOCKS * QUERIES * (4 * (NEAR + far.shape[2]) + 2 * NEAR) * d * 2
    args = (q, do, kv, up, dn, far)
    return pl.pallas_call(
        functools.partial(attend_kernel, heads),
        grid=(steps,),
        in_specs=[spec(x, chunk * steps) for x in args] + [whole(x) for x in (lf, rt, bias)],
        out_specs=[spec(x) for x in outs],
        out_shape=outs,
        scratch_shapes=[pltpu.VMEM((h, 2, STRIP, d), BF)] * 2,
        compiler_params=PARAMS,
        cost_estimate=pl.CostEstimate(flops=flops, bytes_accessed=12 << 20, transcendentals=0),
        name="attend",
    )(*args, lf, rt, bias)


def near_bias():
    position = lax.axis_index("seq")
    tiles_y = lax.axis_size("seq") // TILES_X
    shape = (BLOCKS, QUERIES, NEAR)
    b = lax.broadcasted_iota(jnp.int32, shape, 0)
    i = lax.broadcasted_iota(jnp.int32, shape, 1)
    k = lax.broadcasted_iota(jnp.int32, shape, 2)
    mid = WIN_ROWS * TILE_W
    half = WIN_ROWS * RADIUS
    k_row = jnp.where(k < mid, k // TILE_W, (k - mid) % half // RADIUS) - RADIUS
    side = jnp.where(k < mid + half, k % RADIUS - RADIUS, k % RADIUS + TILE_W)
    k_col = jnp.where(k < mid, k % TILE_W, side)
    seen = (jnp.abs(k_row - i // TILE_W) <= RADIUS) & (jnp.abs(k_col - i % TILE_W) <= RADIUS)
    row = position // TILES_X * TILE_H + b * BLOCK_ROWS + k_row
    col = position % TILES_X * TILE_W + k_col
    inside = (row >= 0) & (row < tiles_y * TILE_H) & (col >= 0) & (col < TILES_X * TILE_W)
    return jnp.where(seen & inside, 0.0, FLOOR).astype(F32)


def shards(fine_queries, fine_keys, fine_values, coarse_keys, coarse_values, out_grad):
    k, v = fine_keys[0], fine_values[0]
    coarse = widened(jnp.stack([coarse_keys[0], coarse_values[0]], 1), 4)
    first = jnp.stack([k[:EDGE], v[:EDGE]], 1)
    last = jnp.stack([k[TOKENS - EDGE :], v[TOKENS - EDGE :]], 1)
    coarse, first, last = lax.optimization_barrier((coarse, first, last))
    dn = tile_shift(first, -1, 0)
    up = tile_shift(last, 1, 0)
    coarse = widened(coarse, 16)
    coarse, fine_queries, out_grad, fine_keys, fine_values = lax.optimization_barrier(
        (coarse, fine_queries, out_grad, fine_keys, fine_values)
    )
    pieces = [coarse] + [stage_shift(coarse, 1, step) for step in (1, 2, 3)]
    strips = columns(fine_keys[0], fine_values[0])
    queries, cots = to_heads(fine_queries, out_grad)
    kv = pairs_to_heads(fine_keys, fine_values)
    up, dn, kv, queries, cots, *strips = lax.optimization_barrier((up, dn, kv, queries, cots, *strips))
    left, right = corners(up, dn, strips)
    rt = [tile_shift(x, 0, -1) for x in left]
    lf = [tile_shift(x, 0, 1) for x in right]
    up, dn = halo_to_heads(up, dn)
    far = far_heads(pieces)
    bias = near_bias()
    att, dq, own, top, bottom, from_left, from_right = ([] for _ in range(7))
    for c in range(CHUNKS):
        a, b, mine, gup, gdn, glf, grt = attend(c, queries, cots, kv, up, dn, far, lf[c], rt[c], bias)
        from_right.append(tile_shift(glf, 0, -1))
        from_left.append(tile_shift(grt, 0, 1))
        att.append(a)
        dq.append(b)
        own.append(mine)
        gup, gdn = fold(gup, gdn, from_left[c], from_right[c])
        bottom.append(tile_shift(gup, -1, 0))
        top.append(tile_shift(gdn, 1, 0))
    attended, query_grad = to_tokens(att, dq)
    dk, dv = premerge(own, from_left, from_right)
    key_grad, value_grad = finish(dk, dv, top, bottom)
    return (attended, query_grad, key_grad, value_grad)


def solution(mesh):
    spec = P("dp", "seq", "head", None)
    return jax.shard_map(
        shards, mesh=mesh, in_specs=(spec,) * 6, out_specs=(spec,) * 4, check_vma=False
    )
```

```python
import functools

import jax
import jax.numpy as jnp
from jax import lax
from jax.experimental import pallas as pl
from jax.experimental.pallas import tpu as pltpu
from jax.sharding import PartitionSpec as P

TILE_H = 24
TILE_W = 16
RADIUS = 4
TILES_X = 8
TOKENS = TILE_H * TILE_W
EDGE = RADIUS * TILE_W
SIDE = TILE_H * RADIUS
CORNER = RADIUS * RADIUS
STRIP = SIDE + 2 * CORNER
CHUNKS = 2
BLOCK_ROWS = 8
BLOCKS = TILE_H // BLOCK_ROWS
QUERIES = BLOCK_ROWS * TILE_W
WIN_ROWS = BLOCK_ROWS + 2 * RADIUS
NEAR = WIN_ROWS * (TILE_W + 2 * RADIUS)
FLOOR = -1e30
LOG2E = 1.4426950408889634
BF = jnp.bfloat16
F32 = jnp.float32
SMEM = pl.BlockSpec(memory_space=pltpu.SMEM)
VMEM = pl.BlockSpec(memory_space=pltpu.VMEM)
PARAMS = pltpu.CompilerParams(vmem_limit_bytes=62 << 20)


def nt(a, b):
    return lax.dot_general(a, b, (((1,), (1,)), ((), ())), preferred_element_type=F32)


def tn(a, b):
    return lax.dot_general(a, b, (((0,), (0,)), ((), ())), preferred_element_type=F32)


def nn(a, b):
    return lax.dot_general(a, b, (((1,), (0,)), ((), ())), preferred_element_type=F32)


def sds(*shape):
    return jax.ShapeDtypeStruct(shape, BF)


def exchange(value, rows, which):
    count = lax.axis_size("seq")
    pairs = []
    for source in range(count):
        row, col = divmod(source, TILES_X)
        place, extent = (row, count // TILES_X) if rows else (col, TILES_X)
        target = ((place + which) ^ 1) - which
        if not 0 <= target < extent:
            target = place
        pairs.append((source, target * TILES_X + col if rows else row * TILES_X + target))
    return lax.ppermute(value, "seq", pairs)


def widened(block, stride):
    count = lax.axis_size("seq")

    def swapped(mask):
        pairs = [(source, source ^ (mask * stride)) for source in range(count)]
        return lax.ppermute(block, "seq", pairs)

    return [block] + [swapped(mask) for mask in (1, 2, 3)]


def pairs_to_heads_kernel(k, v, kv):
    for i, x in enumerate((k, v)):
        kv[:, i] = jnp.swapaxes(x[0], 0, 1)


def pairs_to_heads(k, v):
    t, h, d = k.shape[1:]
    return pl.pallas_call(
        pairs_to_heads_kernel, out_shape=sds(h, 2, t, d), compiler_params=PARAMS, name="pairs_to_heads"
    )(k, v)


def to_heads_kernel(x, y, a, b):
    a[...] = jnp.swapaxes(x[0], 0, 1)
    b[...] = jnp.swapaxes(y[0], 0, 1)


def to_heads(x, y):
    t, h, d = x.shape[1:]
    return pl.pallas_call(
        to_heads_kernel, out_shape=[sds(h, t, d)] * 2, compiler_params=PARAMS, name="to_heads"
    )(x, y)


def halo_to_heads_kernel(even, x, y, up, dn):
    for i in range(2):
        a = jnp.swapaxes(x[:, i], 0, 1)
        b = jnp.swapaxes(y[:, i], 0, 1)
        up[:, i] = lax.select(even[0] == 1, b, a)
        dn[:, i] = lax.select(even[0] == 1, a, b)


def halo_to_heads(even, x, y):
    t, _, h, d = x.shape
    return pl.pallas_call(
        halo_to_heads_kernel,
        in_specs=[SMEM, VMEM, VMEM],
        out_shape=[sds(h, 2, t, d)] * 2,
        compiler_params=PARAMS,
        name="halo_to_heads",
    )(even, x, y)


def far_kernel(*refs):
    out = refs[-1]
    n = refs[0].shape[0]
    for j, piece in enumerate(refs[:-1]):
        for i in range(2):
            out[:, i, j * n : (j + 1) * n] = jnp.swapaxes(piece[:, i], 0, 1)


def far_heads(pieces):
    n, _, h, d = pieces[0].shape
    return pl.pallas_call(
        far_kernel, out_shape=sds(h, 2, n * len(pieces), d), compiler_params=PARAMS, name="far_heads"
    )(*pieces)


def columns_kernel(even, ka, kb, va, vb, *outs):
    h, d = ka.shape[2:]
    n = h // CHUNKS
    for j, mine in enumerate(((ka, va), (kb, vb))):
        for i in range(2):
            x = mine[i][...].reshape(SIDE, h, d)
            for c in range(CHUNKS):
                outs[j * CHUNKS + c][CORNER : CORNER + SIDE, i] = x[:, c * n : (c + 1) * n]


def columns(even, k, v):
    h, d = k.shape[1:]
    k = k.reshape(TILE_H, TILE_W, h, d)
    v = v.reshape(TILE_H, TILE_W, h, d)
    block = (TILE_H, RADIUS, h, d)
    last = TILE_W // RADIUS - 1
    side_a = pl.BlockSpec(block, lambda g, e: (0, last * e[1], 0, 0))
    side_b = pl.BlockSpec(block, lambda g, e: (0, last * (1 - e[1]), 0, 0))
    shape = (STRIP, 2, h // CHUNKS, d)
    return pl.pallas_call(
        columns_kernel,
        grid_spec=pltpu.PrefetchScalarGridSpec(
            num_scalar_prefetch=1,
            grid=(1,),
            in_specs=[side_a, side_b, side_a, side_b],
            out_specs=[pl.BlockSpec(shape, lambda g, e: (0, 0, 0, 0))] * (2 * CHUNKS),
        ),
        out_shape=[sds(*shape)] * (2 * CHUNKS),
        compiler_params=PARAMS,
        name="columns",
    )(even, k, k, v, v)


def corners_kernel(even, a, b, *refs):
    outs = refs[len(refs) // 2 :]
    h = a.shape[2]
    n = h // CHUNKS
    for g, rows in enumerate((a, b)):

        @pl.when(pl.program_id(0) == g)
        def _():
            for j, e in enumerate((even[1], 1 - even[1])):
                for r in range(RADIUS):
                    start = r * TILE_W + (TILE_W - RADIUS) * e
                    for i in range(2):
                        x = rows[pl.ds(start, RADIUS), i]
                        for c in range(CHUNKS):
                            out = outs[j * CHUNKS + c]
                            out[r * RADIUS : (r + 1) * RADIUS, i] = x[:, c * n : (c + 1) * n]


def corners(even, a, b, strips):
    whole = pl.BlockSpec(a.shape, lambda g, e: (0, 0, 0, 0))
    last = STRIP // CORNER - 1
    end = pl.BlockSpec((CORNER,) + strips[0].shape[1:], lambda g, e: (last * (g ^ e[0]), 0, 0, 0))
    outs = pl.pallas_call(
        corners_kernel,
        grid_spec=pltpu.PrefetchScalarGridSpec(
            num_scalar_prefetch=1,
            grid=(2,),
            in_specs=[whole, whole] + [pl.BlockSpec(memory_space=pl.ANY)] * len(strips),
            out_specs=[end] * len(strips),
        ),
        out_shape=[sds(*x.shape) for x in strips],
        input_output_aliases={3 + i: i for i in range(len(strips))},
        compiler_params=PARAMS,
        name="corners",
    )(even, a, b, *strips)
    return outs[:CHUNKS], outs[CHUNKS:]


def to_tokens_kernel(*refs):
    n = (len(refs) - 2) // 2
    for j in range(2):
        x = jnp.concatenate([r[...] for r in refs[j * n : (j + 1) * n]], 0)
        refs[2 * n + j][0] = jnp.swapaxes(x, 0, 1)


def to_tokens(xs, ys):
    h, t, d = xs[0].shape
    return pl.pallas_call(
        to_tokens_kernel,
        out_shape=[sds(1, t, h * len(xs), d)] * 2,
        compiler_params=PARAMS,
        name="to_tokens",
    )(*xs, *ys)


def fold_kernel(even, gup, gdn, from_a, from_b, a, b):
    h, _, t, d = gup.shape
    for i in range(2):
        folded = []
        for g, o in ((gup, 0), (gdn, STRIP - CORNER)):
            x = jnp.swapaxes(g[:, i], 0, 1).astype(F32).reshape(RADIUS, TILE_W, h, d)
            sa, sb = (
                jnp.swapaxes(s[:, i, o : o + CORNER], 0, 1).astype(F32).reshape(RADIUS, RADIUS, h, d)
                for s in (from_a, from_b)
            )
            left = lax.select(even[1] == 1, sb, sa)
            right = lax.select(even[1] == 1, sa, sb)
            x = jnp.concatenate(
                [x[:, :RADIUS] + left, x[:, RADIUS : TILE_W - RADIUS], x[:, TILE_W - RADIUS :] + right], 1
            )
            folded.append(x.reshape(t, h, d).astype(BF))
        a[:, i] = lax.select(even[0] == 1, folded[1], folded[0])
        b[:, i] = lax.select(even[0] == 1, folded[0], folded[1])


def fold(even, gup, gdn, from_a, from_b):
    h, _, t, d = gup.shape
    return pl.pallas_call(
        fold_kernel,
        in_specs=[SMEM] + [VMEM] * 4,
        out_shape=[sds(t, 2, h, d)] * 2,
        compiler_params=PARAMS,
        name="fold",
    )(even, gup, gdn, from_a, from_b)


def premerge_kernel(even, *refs):
    own, from_a, from_b = (refs[c * CHUNKS : (c + 1) * CHUNKS] for c in range(3))
    for i, out in enumerate(refs[3 * CHUNKS :]):
        h, d = out.shape[2:]

        def tokens(parts, rows, *lead):
            x = jnp.concatenate([r[:, i, rows] for r in parts], 0)
            return jnp.swapaxes(x, 0, 1).astype(F32).reshape(*lead, h, d)

        t = tokens(own, slice(0, TOKENS), TILE_H, TILE_W)
        sa = tokens(from_a, slice(CORNER, CORNER + SIDE), TILE_H, RADIUS)
        sb = tokens(from_b, slice(CORNER, CORNER + SIDE), TILE_H, RADIUS)
        le = lax.select(even[1] == 1, sb, sa)
        ri = lax.select(even[1] == 1, sa, sb)
        t = jnp.concatenate(
            [t[:, :RADIUS] + le, t[:, RADIUS : TILE_W - RADIUS], t[:, TILE_W - RADIUS :] + ri], 1
        )
        out[0] = t.reshape(TOKENS, h, d).astype(BF)


def premerge(even, own, from_a, from_b):
    h, _, t, d = own[0].shape
    return pl.pallas_call(
        premerge_kernel,
        in_specs=[SMEM] + [VMEM] * (3 * CHUNKS),
        out_shape=[sds(1, t, h * CHUNKS, d)] * 2,
        compiler_params=PARAMS,
        name="premerge",
    )(even, *own, *from_a, *from_b)


def finish_kernel(even, *refs):
    sums = refs[:2]
    parts = [refs[2 + c * CHUNKS : 2 + (c + 1) * CHUNKS] for c in range(2)]
    outs = refs[2 + 2 * CHUNKS :]
    for g in range(2):

        @pl.when(pl.program_id(0) == g)
        def _():
            for i in range(2):
                x = jnp.concatenate([r[:, i] for r in parts[g]], 1).astype(F32)
                outs[i][0] = (sums[i][0].astype(F32) + x).astype(BF)


def finish(even, dk, dv, from_a, from_b):
    h, d = dk.shape[2:]
    last = TOKENS // EDGE - 1
    rows = pl.BlockSpec((1, EDGE, h, d), lambda g, e: (0, last * (g ^ e[0]), 0, 0))
    part = pl.BlockSpec(from_a[0].shape, lambda g, e: (0, 0, 0, 0))
    return pl.pallas_call(
        finish_kernel,
        grid_spec=pltpu.PrefetchScalarGridSpec(
            num_scalar_prefetch=1,
            grid=(2,),
            in_specs=[rows, rows] + [part] * (2 * CHUNKS),
            out_specs=[rows, rows],
        ),
        out_shape=[sds(*dk.shape)] * 2,
        input_output_aliases={1: 0, 2: 1},
        compiler_params=PARAMS,
        name="finish",
    )(even, dk, dv, *from_a, *from_b)


def attend_kernel(
    heads, q, do, kv, up, dn, far, sa, sb, bias, even, att, dq, own, gup, gdn, ga, gb, strips_lr
):
    @pl.when(pl.program_id(0) == 0)
    def _():
        for src, side in ((sa, even[1]), (sb, 1 - even[1])):
            for i in range(2):
                strips_lr[side, :, i] = jnp.swapaxes(src[:, i], 0, 1)

    first = pl.program_id(0) * heads
    scale = q.shape[-1] ** -0.5
    half = WIN_ROWS * RADIUS
    mid = WIN_ROWS * TILE_W

    def strips(h, i):
        center = jnp.concatenate([up[h, i], kv[h, i], dn[h, i]], 0)
        return center, strips_lr[0, first + h, i], strips_lr[1, first + h, i], far[h, i]

    def window(parts, b):
        c, l, r, f = parts
        o, s = b * BLOCK_ROWS * TILE_W, b * BLOCK_ROWS * RADIUS
        return jnp.concatenate([c[o : o + mid], l[s : s + half], r[s : s + half], f], 0)

    parts = [[strips(h, i) for i in range(2)] for h in range(heads)]
    grads = {}

    def block(h, b):
        rows = slice(b * QUERIES, (b + 1) * QUERIES)
        queries, cots = q[h, rows], do[h, rows]
        keys, values = window(parts[h][0], b), window(parts[h][1], b)
        s = nt(queries, keys)
        dp = nt(cots, values)
        yield
        s = s * (scale * LOG2E)
        s = jnp.concatenate([s[:, :NEAR] + bias[b], s[:, NEAR:]], 1)
        top = jnp.max(s, 1, keepdims=True)
        yield
        e = jnp.exp2(s - top)
        inverse = 1.0 / jnp.sum(e, 1, keepdims=True)
        yield
        p = e * inverse
        rounded = p.astype(BF)
        out = nn(rounded, values).astype(BF)
        dv = tn(rounded[:, :NEAR], cots)
        yield
        att[h, rows] = out
        delta = jnp.sum(out.astype(F32) * cots.astype(F32), 1, keepdims=True)
        ds = (p * (dp - delta) * scale).astype(BF)
        dqs = nn(ds, keys)
        dk = tn(ds[:, :NEAR], queries)
        yield
        dq[h, rows] = dqs.astype(BF)
        grads[h, b] = (dk, dv)

    live = [block(h, b) for h in range(heads) for b in range(BLOCKS)]
    while live:
        for g in list(live):
            try:
                next(g)
            except StopIteration:
                live.remove(g)

    step = BLOCK_ROWS * TILE_W
    for h in range(heads):
        for i in range(2):
            g = [grads[h, b][i] for b in range(BLOCKS)]
            c = [g[0][:step], g[0][step:mid] + g[1][:step], g[1][step:mid] + g[2][:step], g[2][step:mid]]
            c = jnp.concatenate(c, 0)
            gup[h, i] = c[:EDGE].astype(BF)
            own[h, i] = c[EDGE : EDGE + TOKENS].astype(own.dtype)
            gdn[h, i] = c[EDGE + TOKENS :].astype(BF)
            w = BLOCK_ROWS * RADIUS
            sides = []
            for j in range(2):
                s = [x[mid + j * half : mid + (j + 1) * half] for x in g]
                s = jnp.concatenate([s[0][:w], s[0][w:] + s[1][:w], s[1][w:] + s[2][:w], s[2][w:]], 0)
                sides.append(s.astype(BF))
            ga[h, i] = lax.select(even[1] == 1, sides[1], sides[0])
            gb[h, i] = lax.select(even[1] == 1, sides[0], sides[1])


def attend(chunk, even, q, do, kv, up, dn, far, sa, sb, bias, heads=2):
    _, t, d = q.shape
    h = sa.shape[2]
    steps = h // heads

    def spec(x, offset=0):
        return pl.BlockSpec((heads,) + x.shape[1:], lambda g: (g + offset,) + (0,) * (len(x.shape) - 1))

    def whole(x):
        return pl.BlockSpec(x.shape, lambda g: (0,) * len(x.shape))

    outs = [sds(h, t, d)] * 2 + [sds(h, 2, n, d) for n in (t, EDGE, EDGE, STRIP, STRIP)]
    flops = h * BLOCKS * QUERIES * (4 * (NEAR + far.shape[2]) + 2 * NEAR) * d * 2
    args = (q, do, kv, up, dn, far)
    return pl.pallas_call(
        functools.partial(attend_kernel, heads),
        grid=(steps,),
        in_specs=[spec(x, chunk * steps) for x in args] + [whole(x) for x in (sa, sb, bias)] + [SMEM],
        out_specs=[spec(x) for x in outs],
        out_shape=outs,
        scratch_shapes=[pltpu.VMEM((2, h, 2, STRIP, d), BF)],
        compiler_params=PARAMS,
        cost_estimate=pl.CostEstimate(flops=flops, bytes_accessed=12 << 20, transcendentals=0),
        name="attend",
    )(*args, sa, sb, bias, even)


def near_bias():
    position = lax.axis_index("seq")
    tiles_y = lax.axis_size("seq") // TILES_X
    shape = (BLOCKS, QUERIES, NEAR)
    b = lax.broadcasted_iota(jnp.int32, shape, 0)
    i = lax.broadcasted_iota(jnp.int32, shape, 1)
    k = lax.broadcasted_iota(jnp.int32, shape, 2)
    mid = WIN_ROWS * TILE_W
    half = WIN_ROWS * RADIUS
    k_row = jnp.where(k < mid, k // TILE_W, (k - mid) % half // RADIUS) - RADIUS
    side = jnp.where(k < mid + half, k % RADIUS - RADIUS, k % RADIUS + TILE_W)
    k_col = jnp.where(k < mid, k % TILE_W, side)
    seen = (jnp.abs(k_row - i // TILE_W) <= RADIUS) & (jnp.abs(k_col - i % TILE_W) <= RADIUS)
    row = position // TILES_X * TILE_H + b * BLOCK_ROWS + k_row
    col = position % TILES_X * TILE_W + k_col
    inside = (row >= 0) & (row < tiles_y * TILE_H) & (col >= 0) & (col < TILES_X * TILE_W)
    return jnp.where(seen & inside, 0.0, FLOOR).astype(F32)


def shards(fine_queries, fine_keys, fine_values, coarse_keys, coarse_values, out_grad):
    position = lax.axis_index("seq")
    even = jnp.stack([1 - position // TILES_X % 2, 1 - position % TILES_X % 2]).astype(jnp.int32)
    coarse = jnp.concatenate(widened(jnp.stack([coarse_keys[0], coarse_values[0]], 1), 4), 0)
    start = even[0] * (TOKENS - EDGE)
    rows = [
        jnp.stack([lax.dynamic_slice_in_dim(x[0], o, EDGE, 0) for x in (fine_keys, fine_values)], 1)
        for o in (start, TOKENS - EDGE - start)
    ]
    coarse, *rows = lax.optimization_barrier((coarse, *rows))
    row_a, row_b = (exchange(x, True, which) for which, x in enumerate(rows))
    coarse = jnp.concatenate(widened(coarse, 16), 0)
    coarse, fine_queries, out_grad, fine_keys, fine_values = lax.optimization_barrier(
        (coarse, fine_queries, out_grad, fine_keys, fine_values)
    )
    pieces = widened(coarse, 1)
    strips = columns(even, fine_keys[0], fine_values[0])
    queries, cots = to_heads(fine_queries, out_grad)
    kv = pairs_to_heads(fine_keys, fine_values)
    row_a, row_b, kv, queries, cots, *strips = lax.optimization_barrier(
        (row_a, row_b, kv, queries, cots, *strips)
    )
    sides = corners(even, row_a, row_b, strips)
    side_a, side_b = ([exchange(x, False, which) for x in xs] for which, xs in enumerate(sides))
    up, dn = halo_to_heads(even, row_a, row_b)
    far = far_heads(pieces)
    bias = near_bias()
    att, dq, own, to_a, to_b, from_a, from_b = ([] for _ in range(7))
    for c in range(CHUNKS):
        a, b, mine, gup, gdn, ga, gb = attend(
            c, even, queries, cots, kv, up, dn, far, side_a[c], side_b[c], bias
        )
        from_a.append(exchange(ga, False, 0))
        from_b.append(exchange(gb, False, 1))
        att.append(a)
        dq.append(b)
        own.append(mine)
        ra, rb = fold(even, gup, gdn, from_a[c], from_b[c])
        to_a.append(exchange(ra, True, 0))
        to_b.append(exchange(rb, True, 1))
    attended, query_grad = to_tokens(att, dq)
    dk, dv = premerge(even, own, from_a, from_b)
    key_grad, value_grad = finish(even, dk, dv, to_a, to_b)
    return (attended, query_grad, key_grad, value_grad)


def solution(mesh):
    spec = P("dp", "seq", "head", None)
    return jax.shard_map(
        shards, mesh=mesh, in_specs=(spec,) * 6, out_specs=(spec,) * 4, check_vma=False
    )
```

```python
import functools

import jax
import jax.numpy as jnp
from jax import lax
from jax.experimental import pallas as pl
from jax.experimental.pallas import tpu as pltpu
from jax.sharding import PartitionSpec as P

TILE_H = 24
TILE_W = 16
RADIUS = 4
TILES_X = 8
TOKENS = TILE_H * TILE_W
EDGE = RADIUS * TILE_W
SIDE = TILE_H * RADIUS
CORNER = RADIUS * RADIUS
STRIP = SIDE + 2 * CORNER
CHUNKS = 2
BLOCK_ROWS = 8
BLOCKS = TILE_H // BLOCK_ROWS
QUERIES = BLOCK_ROWS * TILE_W
WIN_ROWS = BLOCK_ROWS + 2 * RADIUS
NEAR = WIN_ROWS * (TILE_W + 2 * RADIUS)
FLOOR = -1e30
LOG2E = 1.4426950408889634
BF = jnp.bfloat16
F32 = jnp.float32
SMEM = pl.BlockSpec(memory_space=pltpu.SMEM)
VMEM = pl.BlockSpec(memory_space=pltpu.VMEM)
PARAMS = pltpu.CompilerParams(vmem_limit_bytes=62 << 20)


def nt(a, b):
    return lax.dot_general(a, b, (((1,), (1,)), ((), ())), preferred_element_type=F32)


def tn(a, b):
    return lax.dot_general(a, b, (((0,), (0,)), ((), ())), preferred_element_type=F32)


def nn(a, b):
    return lax.dot_general(a, b, (((1,), (0,)), ((), ())), preferred_element_type=F32)


def sds(*shape):
    return jax.ShapeDtypeStruct(shape, BF)


def exchange(value, rows, which):
    count = lax.axis_size("seq")
    pairs = []
    for source in range(count):
        row, col = divmod(source, TILES_X)
        place, extent = (row, count // TILES_X) if rows else (col, TILES_X)
        target = ((place + which) ^ 1) - which
        if not 0 <= target < extent:
            target = place
        pairs.append((source, target * TILES_X + col if rows else row * TILES_X + target))
    return lax.ppermute(value, "seq", pairs)


def widened(block, stride):
    count = lax.axis_size("seq")

    def swapped(mask):
        pairs = [(source, source ^ (mask * stride)) for source in range(count)]
        return lax.ppermute(block, "seq", pairs)

    return [block] + [swapped(mask) for mask in (1, 2, 3)]


def pairs_to_heads_kernel(k, v, kv):
    for i, x in enumerate((k, v)):
        kv[:, i] = jnp.swapaxes(x[0], 0, 1)


def pairs_to_heads(k, v):
    t, h, d = k.shape[1:]
    n = t // BLOCKS
    tokens = pl.BlockSpec((1, n, h, d), lambda g: (0, g, 0, 0))
    return pl.pallas_call(
        pairs_to_heads_kernel,
        grid=(BLOCKS,),
        in_specs=[tokens, tokens],
        out_specs=pl.BlockSpec((h, 2, n, d), lambda g: (0, 0, g, 0)),
        out_shape=sds(h, 2, t, d),
        compiler_params=PARAMS,
        name="pairs_to_heads",
    )(k, v)


def to_heads_kernel(x, y, a, b):
    a[...] = jnp.swapaxes(x[0], 0, 1)
    b[...] = jnp.swapaxes(y[0], 0, 1)


def to_heads(x, y):
    t, h, d = x.shape[1:]
    n = t // BLOCKS
    tokens = pl.BlockSpec((1, n, h, d), lambda g: (0, g, 0, 0))
    heads = pl.BlockSpec((h, n, d), lambda g: (0, g, 0))
    return pl.pallas_call(
        to_heads_kernel,
        grid=(BLOCKS,),
        in_specs=[tokens, tokens],
        out_specs=[heads, heads],
        out_shape=[sds(h, t, d)] * 2,
        compiler_params=PARAMS,
        name="to_heads",
    )(x, y)


def halo_to_heads_kernel(even, x, y, up, dn):
    a = jnp.swapaxes(x[:, 0], 0, 1)
    b = jnp.swapaxes(y[:, 0], 0, 1)
    up[:, 0] = lax.select(even[0] == 1, b, a)
    dn[:, 0] = lax.select(even[0] == 1, a, b)


def halo_to_heads(even, x, y):
    t, _, h, d = x.shape
    tokens = pl.BlockSpec((t, 1, h, d), lambda g: (0, g, 0, 0))
    heads = pl.BlockSpec((h, 1, t, d), lambda g: (0, g, 0, 0))
    return pl.pallas_call(
        halo_to_heads_kernel,
        grid=(2,),
        in_specs=[SMEM, tokens, tokens],
        out_specs=[heads, heads],
        out_shape=[sds(h, 2, t, d)] * 2,
        compiler_params=PARAMS,
        name="halo_to_heads",
    )(even, x, y)


def far_kernel(*refs):
    out = refs[-1]
    n = refs[0].shape[0]
    for j, piece in enumerate(refs[:-1]):
        out[:, 0, j * n : (j + 1) * n] = jnp.swapaxes(piece[:, 0], 0, 1)


def far_heads(pieces):
    n, _, h, d = pieces[0].shape
    t = n * len(pieces)
    return pl.pallas_call(
        far_kernel,
        grid=(2,),
        in_specs=[pl.BlockSpec((n, 1, h, d), lambda g: (0, g, 0, 0))] * len(pieces),
        out_specs=pl.BlockSpec((h, 1, t, d), lambda g: (0, g, 0, 0)),
        out_shape=sds(h, 2, t, d),
        compiler_params=PARAMS,
        name="far_heads",
    )(*pieces)


def sides_kernel(even, a, b, ka, kb, va, vb, *outs):
    h, d = a.shape[2:]
    n = h // CHUNKS
    for j, (mine, e) in enumerate((((ka, va), even[1]), ((kb, vb), 1 - even[1]))):
        for i in range(2):
            x = mine[i][...].reshape(SIDE, h, d)
            for c in range(CHUNKS):
                outs[j * CHUNKS + c][CORNER : CORNER + SIDE, i] = x[:, c * n : (c + 1) * n]
            for g, rows in enumerate((a, b)):
                end = (STRIP - CORNER) * (g ^ even[0])
                for r in range(RADIUS):
                    x = rows[pl.ds(r * TILE_W + (TILE_W - RADIUS) * e, RADIUS), i]
                    for c in range(CHUNKS):
                        outs[j * CHUNKS + c][pl.ds(end + r * RADIUS, RADIUS), i] = x[:, c * n : (c + 1) * n]


def sides(even, a, b, k, v):
    h, d = a.shape[2:]
    k = k.reshape(TILE_H, TILE_W, h, d)
    v = v.reshape(TILE_H, TILE_W, h, d)
    block = (TILE_H, RADIUS, h, d)
    last = TILE_W // RADIUS - 1
    whole = pl.BlockSpec(a.shape, lambda g, e: (0, 0, 0, 0))
    side_a = pl.BlockSpec(block, lambda g, e: (0, last * e[1], 0, 0))
    side_b = pl.BlockSpec(block, lambda g, e: (0, last * (1 - e[1]), 0, 0))
    shape = (STRIP, 2, h // CHUNKS, d)
    outs = pl.pallas_call(
        sides_kernel,
        grid_spec=pltpu.PrefetchScalarGridSpec(
            num_scalar_prefetch=1,
            grid=(1,),
            in_specs=[whole, whole, side_a, side_b, side_a, side_b],
            out_specs=[pl.BlockSpec(shape, lambda g, e: (0, 0, 0, 0))] * (2 * CHUNKS),
        ),
        out_shape=[sds(*shape)] * (2 * CHUNKS),
        compiler_params=PARAMS,
        name="sides",
    )(even, a, b, k, k, v, v)
    return outs[:CHUNKS], outs[CHUNKS:]


def to_tokens_kernel(*refs):
    n = (len(refs) - 2) // 2
    for j in range(2):
        x = jnp.concatenate([r[...] for r in refs[j * n : (j + 1) * n]], 0)
        refs[2 * n + j][0] = jnp.swapaxes(x, 0, 1)


def to_tokens(xs, ys):
    h, t, d = xs[0].shape
    n = t // BLOCKS
    return pl.pallas_call(
        to_tokens_kernel,
        grid=(BLOCKS,),
        in_specs=[pl.BlockSpec((h, n, d), lambda g: (0, g, 0))] * (2 * len(xs)),
        out_specs=[pl.BlockSpec((1, n, h * len(xs), d), lambda g: (0, g, 0, 0))] * 2,
        out_shape=[sds(1, t, h * len(xs), d)] * 2,
        compiler_params=PARAMS,
        name="to_tokens",
    )(*xs, *ys)


def fold_kernel(even, *refs):
    gup, gdn, from_a, from_b = (refs[c * CHUNKS : (c + 1) * CHUNKS] for c in range(4))
    a, b = refs[4 * CHUNKS :]
    t, _, h, d = a.shape

    def tokens(parts, rows, cols):
        x = jnp.concatenate([r[:, 0, rows] for r in parts], 0)
        return jnp.swapaxes(x, 0, 1).astype(F32).reshape(RADIUS, cols, h, d)

    folded = []
    for g, o in ((gup, 0), (gdn, STRIP - CORNER)):
        x = tokens(g, slice(0, t), TILE_W)
        sa, sb = (tokens(s, slice(o, o + CORNER), RADIUS) for s in (from_a, from_b))
        left = lax.select(even[1] == 1, sb, sa)
        right = lax.select(even[1] == 1, sa, sb)
        x = jnp.concatenate(
            [x[:, :RADIUS] + left, x[:, RADIUS : TILE_W - RADIUS], x[:, TILE_W - RADIUS :] + right], 1
        )
        folded.append(x.reshape(t, h, d).astype(BF))
    a[:, 0] = lax.select(even[0] == 1, folded[1], folded[0])
    b[:, 0] = lax.select(even[0] == 1, folded[0], folded[1])


def fold(even, gup, gdn, from_a, from_b):
    args = (*gup, *gdn, *from_a, *from_b)
    h, _, t, d = gup[0].shape
    h *= CHUNKS
    return pl.pallas_call(
        fold_kernel,
        grid=(2,),
        in_specs=[SMEM]
        + [pl.BlockSpec((x.shape[0], 1) + x.shape[2:], lambda g: (0, g, 0, 0)) for x in args],
        out_specs=[pl.BlockSpec((t, 1, h, d), lambda g: (0, g, 0, 0))] * 2,
        out_shape=[sds(t, 2, h, d)] * 2,
        compiler_params=PARAMS,
        name="fold",
    )(even, *args)


def premerge_kernel(even, *refs):
    own, from_a, from_b = (refs[c * CHUNKS : (c + 1) * CHUNKS] for c in range(3))
    for i, out in enumerate(refs[3 * CHUNKS :]):
        h, d = out.shape[2:]

        def tokens(parts, rows, *lead):
            x = jnp.concatenate([r[:, i, rows] for r in parts], 0)
            return jnp.swapaxes(x, 0, 1).astype(F32).reshape(*lead, h, d)

        t = tokens(own, slice(0, TOKENS), TILE_H, TILE_W)
        sa = tokens(from_a, slice(CORNER, CORNER + SIDE), TILE_H, RADIUS)
        sb = tokens(from_b, slice(CORNER, CORNER + SIDE), TILE_H, RADIUS)
        le = lax.select(even[1] == 1, sb, sa)
        ri = lax.select(even[1] == 1, sa, sb)
        t = jnp.concatenate(
            [t[:, :RADIUS] + le, t[:, RADIUS : TILE_W - RADIUS], t[:, TILE_W - RADIUS :] + ri], 1
        )
        out[0] = t.reshape(TOKENS, h, d).astype(BF)


def premerge(even, own, from_a, from_b):
    h, _, t, d = own[0].shape
    return pl.pallas_call(
        premerge_kernel,
        in_specs=[SMEM] + [VMEM] * (3 * CHUNKS),
        out_shape=[sds(1, t, h * CHUNKS, d)] * 2,
        compiler_params=PARAMS,
        name="premerge",
    )(even, *own, *from_a, *from_b)


def finish_kernel(even, dk, dv, from_a, from_b, dk_out, dv_out):
    for g, part in enumerate((from_a, from_b)):

        @pl.when(pl.program_id(0) == g)
        def _():
            for i, (x, out) in enumerate(((dk, dk_out), (dv, dv_out))):
                out[0] = (x[0].astype(F32) + part[:, i].astype(F32)).astype(BF)


def finish(even, dk, dv, from_a, from_b):
    h, d = dk.shape[2:]
    last = TOKENS // EDGE - 1
    rows = pl.BlockSpec((1, EDGE, h, d), lambda g, e: (0, last * (g ^ e[0]), 0, 0))
    part = pl.BlockSpec(from_a.shape, lambda g, e: (0, 0, 0, 0))
    return pl.pallas_call(
        finish_kernel,
        grid_spec=pltpu.PrefetchScalarGridSpec(
            num_scalar_prefetch=1,
            grid=(2,),
            in_specs=[rows, rows, part, part],
            out_specs=[rows, rows],
        ),
        out_shape=[sds(*dk.shape)] * 2,
        input_output_aliases={1: 0, 2: 1},
        compiler_params=PARAMS,
        name="finish",
    )(even, dk, dv, from_a, from_b)


def attend_kernel(
    heads, q, do, kv, up, dn, far, sa, sb, bias, even, att, dq, own, gup, gdn, ga, gb, strips_lr
):
    @pl.when(pl.program_id(0) == 0)
    def _():
        for src, side in ((sa, even[1]), (sb, 1 - even[1])):
            for i in range(2):
                strips_lr[side, :, i] = jnp.swapaxes(src[:, i], 0, 1)

    first = pl.program_id(0) * heads
    scale = q.shape[-1] ** -0.5
    half = WIN_ROWS * RADIUS
    mid = WIN_ROWS * TILE_W

    def strips(h, i):
        center = jnp.concatenate([up[h, i], kv[h, i], dn[h, i]], 0)
        return center, strips_lr[0, first + h, i], strips_lr[1, first + h, i], far[h, i]

    def window(parts, b):
        c, l, r, f = parts
        o, s = b * BLOCK_ROWS * TILE_W, b * BLOCK_ROWS * RADIUS
        return jnp.concatenate([c[o : o + mid], l[s : s + half], r[s : s + half], f], 0)

    parts = [[strips(h, i) for i in range(2)] for h in range(heads)]
    grads = {}

    def block(h, b):
        rows = slice(b * QUERIES, (b + 1) * QUERIES)
        queries, cots = q[h, rows], do[h, rows]
        keys, values = window(parts[h][0], b), window(parts[h][1], b)
        s = nt(queries, keys)
        dp = nt(cots, values)
        yield
        s = s * (scale * LOG2E)
        s = jnp.concatenate([s[:, :NEAR] + bias[b], s[:, NEAR:]], 1)
        top = jnp.max(s, 1, keepdims=True)
        yield
        e = jnp.exp2(s - top)
        inverse = 1.0 / jnp.sum(e, 1, keepdims=True)
        yield
        p = e * inverse
        rounded = p.astype(BF)
        out = nn(rounded, values).astype(BF)
        dv = tn(rounded[:, :NEAR], cots)
        yield
        att[h, rows] = out
        delta = jnp.sum(out.astype(F32) * cots.astype(F32), 1, keepdims=True)
        ds = (p * (dp - delta) * scale).astype(BF)
        dqs = nn(ds, keys)
        dk = tn(ds[:, :NEAR], queries)
        yield
        dq[h, rows] = dqs.astype(BF)
        grads[h, b] = (dk, dv)

    live = [block(h, b) for h in range(heads) for b in range(BLOCKS)]
    while live:
        for g in list(live):
            try:
                next(g)
            except StopIteration:
                live.remove(g)

    step = BLOCK_ROWS * TILE_W
    for h in range(heads):
        for i in range(2):
            g = [grads[h, b][i] for b in range(BLOCKS)]
            c = [g[0][:step], g[0][step:mid] + g[1][:step], g[1][step:mid] + g[2][:step], g[2][step:mid]]
            c = jnp.concatenate(c, 0)
            gup[h, i] = c[:EDGE].astype(BF)
            own[h, i] = c[EDGE : EDGE + TOKENS].astype(own.dtype)
            gdn[h, i] = c[EDGE + TOKENS :].astype(BF)
            w = BLOCK_ROWS * RADIUS
            sides = []
            for j in range(2):
                s = [x[mid + j * half : mid + (j + 1) * half] for x in g]
                s = jnp.concatenate([s[0][:w], s[0][w:] + s[1][:w], s[1][w:] + s[2][:w], s[2][w:]], 0)
                sides.append(s.astype(BF))
            ga[h, i] = lax.select(even[1] == 1, sides[1], sides[0])
            gb[h, i] = lax.select(even[1] == 1, sides[0], sides[1])


def attend(chunk, even, q, do, kv, up, dn, far, sa, sb, bias, heads=2):
    _, t, d = q.shape
    h = sa.shape[2]
    steps = h // heads

    def spec(x, offset=0):
        return pl.BlockSpec((heads,) + x.shape[1:], lambda g: (g + offset,) + (0,) * (len(x.shape) - 1))

    def whole(x):
        return pl.BlockSpec(x.shape, lambda g: (0,) * len(x.shape))

    outs = [sds(h, t, d)] * 2 + [sds(h, 2, n, d) for n in (t, EDGE, EDGE, STRIP, STRIP)]
    flops = h * BLOCKS * QUERIES * (4 * (NEAR + far.shape[2]) + 2 * NEAR) * d * 2
    args = (q, do, kv, up, dn, far)
    return pl.pallas_call(
        functools.partial(attend_kernel, heads),
        grid=(steps,),
        in_specs=[spec(x, chunk * steps) for x in args] + [whole(x) for x in (sa, sb, bias)] + [SMEM],
        out_specs=[spec(x) for x in outs],
        out_shape=outs,
        scratch_shapes=[pltpu.VMEM((2, h, 2, STRIP, d), BF)],
        compiler_params=PARAMS,
        cost_estimate=pl.CostEstimate(flops=flops, bytes_accessed=12 << 20, transcendentals=0),
        name="attend",
    )(*args, sa, sb, bias, even)


def near_bias():
    position = lax.axis_index("seq")
    tiles_y = lax.axis_size("seq") // TILES_X
    shape = (BLOCKS, QUERIES, NEAR)
    b = lax.broadcasted_iota(jnp.int32, shape, 0)
    i = lax.broadcasted_iota(jnp.int32, shape, 1)
    k = lax.broadcasted_iota(jnp.int32, shape, 2)
    mid = WIN_ROWS * TILE_W
    half = WIN_ROWS * RADIUS
    k_row = jnp.where(k < mid, k // TILE_W, (k - mid) % half // RADIUS) - RADIUS
    side = jnp.where(k < mid + half, k % RADIUS - RADIUS, k % RADIUS + TILE_W)
    k_col = jnp.where(k < mid, k % TILE_W, side)
    seen = (jnp.abs(k_row - i // TILE_W) <= RADIUS) & (jnp.abs(k_col - i % TILE_W) <= RADIUS)
    row = position // TILES_X * TILE_H + b * BLOCK_ROWS + k_row
    col = position % TILES_X * TILE_W + k_col
    inside = (row >= 0) & (row < tiles_y * TILE_H) & (col >= 0) & (col < TILES_X * TILE_W)
    return jnp.where(seen & inside, 0.0, FLOOR).astype(F32)


def shards(fine_queries, fine_keys, fine_values, coarse_keys, coarse_values, out_grad):
    position = lax.axis_index("seq")
    even = jnp.stack([1 - position // TILES_X % 2, 1 - position % TILES_X % 2]).astype(jnp.int32)
    coarse = jnp.concatenate(widened(jnp.stack([coarse_keys[0], coarse_values[0]], 1), 4), 0)
    start = even[0] * (TOKENS - EDGE)
    rows = [
        jnp.stack([lax.dynamic_slice_in_dim(x[0], o, EDGE, 0) for x in (fine_keys, fine_values)], 1)
        for o in (start, TOKENS - EDGE - start)
    ]
    coarse, *rows = lax.optimization_barrier((coarse, *rows))
    row_a, row_b = (exchange(x, True, which) for which, x in enumerate(rows))
    coarse = jnp.concatenate(widened(coarse, 16), 0)
    coarse, fine_queries, out_grad, fine_keys, fine_values = lax.optimization_barrier(
        (coarse, fine_queries, out_grad, fine_keys, fine_values)
    )
    pieces = widened(coarse, 1)
    queries, cots = to_heads(fine_queries, out_grad)
    kv = pairs_to_heads(fine_keys, fine_values)
    bias = near_bias()
    row_a, row_b, kv, queries, cots, bias = lax.optimization_barrier((row_a, row_b, kv, queries, cots, bias))
    strips = sides(even, row_a, row_b, fine_keys[0], fine_values[0])
    side_a, side_b = ([exchange(x, False, which) for x in xs] for which, xs in enumerate(strips))
    up, dn = halo_to_heads(even, row_a, row_b)
    far = far_heads(pieces)
    att, dq, own, gup, gdn, from_a, from_b = ([] for _ in range(7))
    for c in range(CHUNKS):
        a, b, mine, u, n, ga, gb = attend(
            c, even, queries, cots, kv, up, dn, far, side_a[c], side_b[c], bias
        )
        from_a.append(exchange(ga, False, 0))
        from_b.append(exchange(gb, False, 1))
        for xs, x in ((att, a), (dq, b), (own, mine), (gup, u), (gdn, n)):
            xs.append(x)
    to_a, to_b = fold(even, gup, gdn, from_a, from_b)
    to_a, to_b = exchange(to_a, True, 0), exchange(to_b, True, 1)
    attended, query_grad = to_tokens(att, dq)
    dk, dv = premerge(even, own, from_a, from_b)
    key_grad, value_grad = finish(even, dk, dv, to_a, to_b)
    return (attended, query_grad, key_grad, value_grad)


def solution(mesh):
    spec = P("dp", "seq", "head", None)
    return jax.shard_map(
        shards, mesh=mesh, in_specs=(spec,) * 6, out_specs=(spec,) * 4, check_vma=False
    )
```

```python
import functools

import jax
import jax.numpy as jnp
from jax import lax
from jax.experimental import pallas as pl
from jax.experimental.pallas import tpu as pltpu
from jax.sharding import PartitionSpec as P

TILE_H = 24
TILE_W = 16
RADIUS = 4
TILES_X = 8
TOKENS = TILE_H * TILE_W
EDGE = RADIUS * TILE_W
SIDE = TILE_H * RADIUS
CORNER = RADIUS * RADIUS
STRIP = SIDE + 2 * CORNER
CHUNKS = 2
BLOCK_ROWS = 8
BLOCKS = TILE_H // BLOCK_ROWS
QUERIES = BLOCK_ROWS * TILE_W
WIN_ROWS = BLOCK_ROWS + 2 * RADIUS
NEAR = WIN_ROWS * (TILE_W + 2 * RADIUS)
FLOOR = -1e30
LOG2E = 1.4426950408889634
BF = jnp.bfloat16
F32 = jnp.float32
SMEM = pl.BlockSpec(memory_space=pltpu.SMEM)
VMEM = pl.BlockSpec(memory_space=pltpu.VMEM)
PARAMS = pltpu.CompilerParams(vmem_limit_bytes=63 << 20)


def nt(a, b):
    return lax.dot_general(a, b, (((1,), (1,)), ((), ())), preferred_element_type=F32)


def tn(a, b):
    return lax.dot_general(a, b, (((0,), (0,)), ((), ())), preferred_element_type=F32)


def nn(a, b):
    return lax.dot_general(a, b, (((1,), (0,)), ((), ())), preferred_element_type=F32)


def sds(*shape):
    return jax.ShapeDtypeStruct(shape, BF)


def exchange(value, rows, which):
    count = lax.axis_size("seq")
    pairs = []
    for source in range(count):
        row, col = divmod(source, TILES_X)
        place, extent = (row, count // TILES_X) if rows else (col, TILES_X)
        target = ((place + which) ^ 1) - which
        if not 0 <= target < extent:
            pairs.append((source, source ^ (TILES_X // 2) if rows else source ^ (2 * TILES_X)))
        else:
            pairs.append((source, target * TILES_X + col if rows else row * TILES_X + target))
    return lax.ppermute(value, "seq", pairs)


def widened(block, stride):
    count = lax.axis_size("seq")

    def swapped(mask):
        pairs = [(source, source ^ (mask * stride)) for source in range(count)]
        return lax.ppermute(block, "seq", pairs)

    return [block] + [swapped(mask) for mask in (1, 2, 3)]


def pairs_to_heads_kernel(k, v, kv):
    for i, x in enumerate((k, v)):
        kv[:, i] = jnp.swapaxes(x[0], 0, 1)


def pairs_to_heads(k, v):
    t, h, d = k.shape[1:]
    return pl.pallas_call(
        pairs_to_heads_kernel,
        out_shape=sds(h, 2, t, d),
        compiler_params=PARAMS,
        name="pairs_to_heads",
    )(k, v)


def to_heads_kernel(x, y, a, b):
    a[...] = jnp.swapaxes(x[0], 0, 1)
    b[...] = jnp.swapaxes(y[0], 0, 1)


def to_heads(x, y):
    t, h, d = x.shape[1:]
    return pl.pallas_call(
        to_heads_kernel,
        out_shape=[sds(h, t, d)] * 2,
        compiler_params=PARAMS,
        name="to_heads",
    )(x, y)


def halo_to_heads_kernel(even, x, y, up, dn):
    a = jnp.swapaxes(x[:, 0], 0, 1)
    b = jnp.swapaxes(y[:, 0], 0, 1)
    up[:, 0] = lax.select(even[0] == 1, b, a)
    dn[:, 0] = lax.select(even[0] == 1, a, b)


def halo_to_heads(even, x, y):
    t, _, h, d = x.shape
    tokens = pl.BlockSpec((t, 1, h, d), lambda g: (0, g, 0, 0))
    heads = pl.BlockSpec((h, 1, t, d), lambda g: (0, g, 0, 0))
    return pl.pallas_call(
        halo_to_heads_kernel,
        grid=(2,),
        in_specs=[SMEM, tokens, tokens],
        out_specs=[heads, heads],
        out_shape=[sds(h, 2, t, d)] * 2,
        compiler_params=PARAMS,
        name="halo_to_heads",
    )(even, x, y)


def far_kernel(*refs):
    out = refs[-1]
    n = refs[0].shape[0]
    for j, piece in enumerate(refs[:-1]):
        out[:, 0, j * n : (j + 1) * n] = jnp.swapaxes(piece[:, 0], 0, 1)


def far_heads(pieces):
    n, _, h, d = pieces[0].shape
    t = n * len(pieces)
    return pl.pallas_call(
        far_kernel,
        grid=(2,),
        in_specs=[pl.BlockSpec((n, 1, h, d), lambda g: (0, g, 0, 0))] * len(pieces),
        out_specs=pl.BlockSpec((h, 1, t, d), lambda g: (0, g, 0, 0)),
        out_shape=sds(h, 2, t, d),
        compiler_params=PARAMS,
        name="far_heads",
    )(*pieces)


def sides_kernel(even, a, b, ka, kb, va, vb, *outs):
    h, d = a.shape[2:]
    n = h // CHUNKS
    for j, (mine, e) in enumerate((((ka, va), even[1]), ((kb, vb), 1 - even[1]))):
        for i in range(2):
            x = mine[i][...].reshape(SIDE, h, d)
            for c in range(CHUNKS):
                outs[j * CHUNKS + c][CORNER : CORNER + SIDE, i] = x[:, c * n : (c + 1) * n]
            for g, rows in enumerate((a, b)):
                end = (STRIP - CORNER) * (g ^ even[0])
                for r in range(RADIUS):
                    x = rows[pl.ds(r * TILE_W + (TILE_W - RADIUS) * e, RADIUS), i]
                    for c in range(CHUNKS):
                        outs[j * CHUNKS + c][pl.ds(end + r * RADIUS, RADIUS), i] = x[:, c * n : (c + 1) * n]


def sides(even, a, b, k, v):
    h, d = a.shape[2:]
    k = k.reshape(TILE_H, TILE_W, h, d)
    v = v.reshape(TILE_H, TILE_W, h, d)
    block = (TILE_H, RADIUS, h, d)
    last = TILE_W // RADIUS - 1
    whole = pl.BlockSpec(a.shape, lambda g, e: (0, 0, 0, 0))
    side_a = pl.BlockSpec(block, lambda g, e: (0, last * e[1], 0, 0))
    side_b = pl.BlockSpec(block, lambda g, e: (0, last * (1 - e[1]), 0, 0))
    shape = (STRIP, 2, h // CHUNKS, d)
    outs = pl.pallas_call(
        sides_kernel,
        grid_spec=pltpu.PrefetchScalarGridSpec(
            num_scalar_prefetch=1,
            grid=(1,),
            in_specs=[whole, whole, side_a, side_b, side_a, side_b],
            out_specs=[pl.BlockSpec(shape, lambda g, e: (0, 0, 0, 0))] * (2 * CHUNKS),
        ),
        out_shape=[sds(*shape)] * (2 * CHUNKS),
        compiler_params=PARAMS,
        name="sides",
    )(even, a, b, k, k, v, v)
    return outs[:CHUNKS], outs[CHUNKS:]


def to_tokens_kernel(*refs):
    n = (len(refs) - 2) // 2
    for j in range(2):
        x = jnp.concatenate([r[...] for r in refs[j * n : (j + 1) * n]], 0)
        refs[2 * n + j][0] = jnp.swapaxes(x, 0, 1)


def to_tokens(xs, ys):
    h, t, d = xs[0].shape
    return pl.pallas_call(
        to_tokens_kernel,
        out_shape=[sds(1, t, h * len(xs), d)] * 2,
        compiler_params=PARAMS,
        name="to_tokens",
    )(*xs, *ys)


def fold_kernel(even, *refs):
    gup, gdn, from_a, from_b = (refs[c * CHUNKS : (c + 1) * CHUNKS] for c in range(4))
    a, b = refs[4 * CHUNKS :]
    t, _, h, d = a.shape

    def tokens(parts, rows, cols):
        x = jnp.concatenate([r[:, 0, rows] for r in parts], 0)
        return jnp.swapaxes(x, 0, 1).astype(F32).reshape(RADIUS, cols, h, d)

    folded = []
    for g, o in ((gup, 0), (gdn, STRIP - CORNER)):
        x = tokens(g, slice(0, t), TILE_W)
        sa, sb = (tokens(s, slice(o, o + CORNER), RADIUS) for s in (from_a, from_b))
        left = lax.select(even[1] == 1, sb, sa)
        right = lax.select(even[1] == 1, sa, sb)
        x = jnp.concatenate(
            [x[:, :RADIUS] + left, x[:, RADIUS : TILE_W - RADIUS], x[:, TILE_W - RADIUS :] + right], 1
        )
        folded.append(x.reshape(t, h, d).astype(BF))
    a[:, 0] = lax.select(even[0] == 1, folded[1], folded[0])
    b[:, 0] = lax.select(even[0] == 1, folded[0], folded[1])


def fold(even, gup, gdn, from_a, from_b):
    args = (*gup, *gdn, *from_a, *from_b)
    h, _, t, d = gup[0].shape
    h *= CHUNKS
    return pl.pallas_call(
        fold_kernel,
        grid=(2,),
        in_specs=[SMEM]
        + [pl.BlockSpec((x.shape[0], 1) + x.shape[2:], lambda g: (0, g, 0, 0)) for x in args],
        out_specs=[pl.BlockSpec((t, 1, h, d), lambda g: (0, g, 0, 0))] * 2,
        out_shape=[sds(t, 2, h, d)] * 2,
        compiler_params=PARAMS,
        name="fold",
    )(even, *args)


def premerge_kernel(even, *refs):
    own, from_a, from_b = (refs[c * CHUNKS : (c + 1) * CHUNKS] for c in range(3))
    for i, out in enumerate(refs[3 * CHUNKS :]):
        h, d = out.shape[2:]

        def tokens(parts, rows, *lead):
            x = jnp.concatenate([r[:, i, rows] for r in parts], 0)
            return jnp.swapaxes(x, 0, 1).astype(F32).reshape(*lead, h, d)

        t = tokens(own, slice(0, TOKENS), TILE_H, TILE_W)
        sa = tokens(from_a, slice(CORNER, CORNER + SIDE), TILE_H, RADIUS)
        sb = tokens(from_b, slice(CORNER, CORNER + SIDE), TILE_H, RADIUS)
        le = lax.select(even[1] == 1, sb, sa)
        ri = lax.select(even[1] == 1, sa, sb)
        t = jnp.concatenate(
            [t[:, :RADIUS] + le, t[:, RADIUS : TILE_W - RADIUS], t[:, TILE_W - RADIUS :] + ri], 1
        )
        out[0] = t.reshape(TOKENS, h, d).astype(BF)


def premerge(even, own, from_a, from_b):
    h, _, t, d = own[0].shape
    return pl.pallas_call(
        premerge_kernel,
        in_specs=[SMEM] + [VMEM] * (3 * CHUNKS),
        out_shape=[sds(1, t, h * CHUNKS, d)] * 2,
        compiler_params=PARAMS,
        name="premerge",
    )(even, *own, *from_a, *from_b)


def finish_kernel(even, dk, dv, from_a, from_b, dk_out, dv_out):
    for g, part in enumerate((from_a, from_b)):

        @pl.when(pl.program_id(0) == g)
        def _():
            for i, (x, out) in enumerate(((dk, dk_out), (dv, dv_out))):
                out[0] = (x[0].astype(F32) + part[:, i].astype(F32)).astype(BF)


def finish(even, dk, dv, from_a, from_b):
    h, d = dk.shape[2:]
    last = TOKENS // EDGE - 1
    rows = pl.BlockSpec((1, EDGE, h, d), lambda g, e: (0, last * (g ^ e[0]), 0, 0))
    part = pl.BlockSpec(from_a.shape, lambda g, e: (0, 0, 0, 0))
    return pl.pallas_call(
        finish_kernel,
        grid_spec=pltpu.PrefetchScalarGridSpec(
            num_scalar_prefetch=1,
            grid=(2,),
            in_specs=[rows, rows, part, part],
            out_specs=[rows, rows],
        ),
        out_shape=[sds(*dk.shape)] * 2,
        input_output_aliases={1: 0, 2: 1},
        compiler_params=PARAMS,
        name="finish",
    )(even, dk, dv, from_a, from_b)


def attend_kernel(
    heads, q, do, kv, up, dn, far, sa, sb, bias, even, att, dq, own, gup, gdn, ga, gb, strips_lr
):
    @pl.when(pl.program_id(0) == 0)
    def _():
        for src, side in ((sa, even[1]), (sb, 1 - even[1])):
            for i in range(2):
                strips_lr[side, :, i] = jnp.swapaxes(src[:, i], 0, 1)

    first = pl.program_id(0) * heads
    scale = q.shape[-1] ** -0.5
    half = WIN_ROWS * RADIUS
    mid = WIN_ROWS * TILE_W

    def strips(h, i):
        center = jnp.concatenate([up[h, i], kv[h, i], dn[h, i]], 0)
        return center, strips_lr[0, first + h, i], strips_lr[1, first + h, i], far[h, i]

    def window(parts, b):
        c, l, r, f = parts
        o, s = b * BLOCK_ROWS * TILE_W, b * BLOCK_ROWS * RADIUS
        return jnp.concatenate([c[o : o + mid], l[s : s + half], r[s : s + half], f], 0)

    parts = [[strips(h, i) for i in range(2)] for h in range(heads)]
    grads = {}

    def block(h, b):
        rows = slice(b * QUERIES, (b + 1) * QUERIES)
        queries, cots = q[h, rows], do[h, rows]
        keys, values = window(parts[h][0], b), window(parts[h][1], b)
        s = nt(queries, keys)
        dp = nt(cots, values)
        yield
        s = s * (scale * LOG2E)
        s = jnp.concatenate([s[:, :NEAR] + bias[b], s[:, NEAR:]], 1)
        top = jnp.max(s, 1, keepdims=True)
        yield
        e = jnp.exp2(s - top)
        inverse = 1.0 / jnp.sum(e, 1, keepdims=True)
        yield
        p = e * inverse
        rounded = p.astype(BF)
        out = nn(rounded, values).astype(BF)
        dv = tn(rounded[:, :NEAR], cots)
        yield
        att[h, rows] = out
        delta = jnp.sum(out.astype(F32) * cots.astype(F32), 1, keepdims=True)
        ds = (p * (dp - delta) * scale).astype(BF)
        dqs = nn(ds, keys)
        dk = tn(ds[:, :NEAR], queries)
        yield
        dq[h, rows] = dqs.astype(BF)
        grads[h, b] = (dk, dv)

    live = [block(h, b) for h in range(heads) for b in range(BLOCKS)]
    while live:
        for g in list(live):
            try:
                next(g)
            except StopIteration:
                live.remove(g)

    step = BLOCK_ROWS * TILE_W
    for h in range(heads):
        for i in range(2):
            g = [grads[h, b][i] for b in range(BLOCKS)]
            c = [g[0][:step], g[0][step:mid] + g[1][:step], g[1][step:mid] + g[2][:step], g[2][step:mid]]
            c = jnp.concatenate(c, 0)
            gup[h, i] = c[:EDGE].astype(BF)
            own[h, i] = c[EDGE : EDGE + TOKENS].astype(own.dtype)
            gdn[h, i] = c[EDGE + TOKENS :].astype(BF)
            w = BLOCK_ROWS * RADIUS
            sides = []
            for j in range(2):
                s = [x[mid + j * half : mid + (j + 1) * half] for x in g]
                s = jnp.concatenate([s[0][:w], s[0][w:] + s[1][:w], s[1][w:] + s[2][:w], s[2][w:]], 0)
                sides.append(s.astype(BF))
            ga[h, i] = lax.select(even[1] == 1, sides[1], sides[0])
            gb[h, i] = lax.select(even[1] == 1, sides[0], sides[1])


def attend(chunk, even, q, do, kv, up, dn, far, sa, sb, bias, heads=2):
    _, t, d = q.shape
    h = sa.shape[2]
    steps = h // heads

    def spec(x, offset=0):
        return pl.BlockSpec((heads,) + x.shape[1:], lambda g: (g + offset,) + (0,) * (len(x.shape) - 1))

    def whole(x):
        return pl.BlockSpec(x.shape, lambda g: (0,) * len(x.shape))

    outs = [sds(h, t, d)] * 2 + [sds(h, 2, n, d) for n in (t, EDGE, EDGE, STRIP, STRIP)]
    flops = h * BLOCKS * QUERIES * (4 * (NEAR + far.shape[2]) + 2 * NEAR) * d * 2
    args = (q, do, kv, up, dn, far)
    return pl.pallas_call(
        functools.partial(attend_kernel, heads),
        grid=(steps,),
        in_specs=[spec(x, chunk * steps) for x in args] + [whole(x) for x in (sa, sb, bias)] + [SMEM],
        out_specs=[spec(x) for x in outs],
        out_shape=outs,
        scratch_shapes=[pltpu.VMEM((2, h, 2, STRIP, d), BF)],
        compiler_params=PARAMS,
        cost_estimate=pl.CostEstimate(flops=flops, bytes_accessed=12 << 20, transcendentals=0),
        name="attend",
    )(*args, sa, sb, bias, even)


def near_bias():
    position = lax.axis_index("seq")
    tiles_y = lax.axis_size("seq") // TILES_X
    shape = (BLOCKS, QUERIES, NEAR)
    b = lax.broadcasted_iota(jnp.int32, shape, 0)
    i = lax.broadcasted_iota(jnp.int32, shape, 1)
    k = lax.broadcasted_iota(jnp.int32, shape, 2)
    mid = WIN_ROWS * TILE_W
    half = WIN_ROWS * RADIUS
    k_row = jnp.where(k < mid, k // TILE_W, (k - mid) % half // RADIUS) - RADIUS
    side = jnp.where(k < mid + half, k % RADIUS - RADIUS, k % RADIUS + TILE_W)
    k_col = jnp.where(k < mid, k % TILE_W, side)
    seen = (jnp.abs(k_row - i // TILE_W) <= RADIUS) & (jnp.abs(k_col - i % TILE_W) <= RADIUS)
    row = position // TILES_X * TILE_H + b * BLOCK_ROWS + k_row
    col = position % TILES_X * TILE_W + k_col
    inside = (row >= 0) & (row < tiles_y * TILE_H) & (col >= 0) & (col < TILES_X * TILE_W)
    return jnp.where(seen & inside, 0.0, FLOOR).astype(F32)


def shards(fine_queries, fine_keys, fine_values, coarse_keys, coarse_values, out_grad):
    position = lax.axis_index("seq")
    even = jnp.stack([1 - position // TILES_X % 2, 1 - position % TILES_X % 2]).astype(jnp.int32)
    coarse = jnp.concatenate(widened(jnp.stack([coarse_keys[0], coarse_values[0]], 1), 4), 0)
    start = even[0] * (TOKENS - EDGE)
    rows = [
        jnp.stack([lax.dynamic_slice_in_dim(x[0], o, EDGE, 0) for x in (fine_keys, fine_values)], 1)
        for o in (start, TOKENS - EDGE - start)
    ]
    coarse, *rows = lax.optimization_barrier((coarse, *rows))
    row_a, row_b = (exchange(x, True, which) for which, x in enumerate(rows))
    coarse = jnp.concatenate(widened(coarse, 16), 0)
    coarse, fine_queries, out_grad, fine_keys, fine_values = lax.optimization_barrier(
        (coarse, fine_queries, out_grad, fine_keys, fine_values)
    )
    pieces = widened(coarse, 1)
    queries, cots = to_heads(fine_queries, out_grad)
    kv = pairs_to_heads(fine_keys, fine_values)
    bias = near_bias()
    row_a, row_b, kv, queries, cots, bias = lax.optimization_barrier((row_a, row_b, kv, queries, cots, bias))
    strips = sides(even, row_a, row_b, fine_keys[0], fine_values[0])
    side_a, side_b = ([exchange(x, False, which) for x in xs] for which, xs in enumerate(strips))
    up, dn = halo_to_heads(even, row_a, row_b)
    far = far_heads(pieces)
    att, dq, own, gup, gdn, from_a, from_b = ([] for _ in range(7))
    for c in range(CHUNKS):
        a, b, mine, u, n, ga, gb = attend(
            c, even, queries, cots, kv, up, dn, far, side_a[c], side_b[c], bias
        )
        from_a.append(exchange(ga, False, 0))
        from_b.append(exchange(gb, False, 1))
        for xs, x in ((att, a), (dq, b), (own, mine), (gup, u), (gdn, n)):
            xs.append(x)
    to_a, to_b = fold(even, gup, gdn, from_a, from_b)
    to_a, to_b = exchange(to_a, True, 0), exchange(to_b, True, 1)
    attended, query_grad = to_tokens(att, dq)
    dk, dv = premerge(even, own, from_a, from_b)
    key_grad, value_grad = finish(even, dk, dv, to_a, to_b)
    return (attended, query_grad, key_grad, value_grad)


def solution(mesh):
    spec = P("dp", "seq", "head", None)
    return jax.shard_map(
        shards, mesh=mesh, in_specs=(spec,) * 6, out_specs=(spec,) * 4, check_vma=False
    )
```

```python
import functools

import jax
import jax.numpy as jnp
from jax import lax
from jax.experimental import pallas as pl
from jax.experimental.pallas import tpu as pltpu
from jax.sharding import PartitionSpec as P

TILE_H = 24
TILE_W = 16
RADIUS = 4
TILES_X = 8
TOKENS = TILE_H * TILE_W
EDGE = RADIUS * TILE_W
SIDE = TILE_H * RADIUS
CORNER = RADIUS * RADIUS
STRIP = SIDE + 2 * CORNER
CHUNKS = 2
BLOCK_ROWS = 8
BLOCKS = TILE_H // BLOCK_ROWS
QUERIES = BLOCK_ROWS * TILE_W
WIN_ROWS = BLOCK_ROWS + 2 * RADIUS
NEAR = WIN_ROWS * (TILE_W + 2 * RADIUS)
FLOOR = -1e30
LOG2E = 1.4426950408889634
BF = jnp.bfloat16
F32 = jnp.float32
SMEM = pl.BlockSpec(memory_space=pltpu.SMEM)
VMEM = pl.BlockSpec(memory_space=pltpu.VMEM)
PARAMS = pltpu.CompilerParams(vmem_limit_bytes=63 << 20)


def nt(a, b):
    return lax.dot_general(a, b, (((1,), (1,)), ((), ())), preferred_element_type=F32)


def tn(a, b):
    return lax.dot_general(a, b, (((0,), (0,)), ((), ())), preferred_element_type=F32)


def nn(a, b):
    return lax.dot_general(a, b, (((1,), (0,)), ((), ())), preferred_element_type=F32)


def sds(*shape):
    return jax.ShapeDtypeStruct(shape, BF)


def exchange(value, rows, which):
    count = lax.axis_size("seq")
    pairs = []
    for source in range(count):
        row, col = divmod(source, TILES_X)
        place, extent = (row, count // TILES_X) if rows else (col, TILES_X)
        target = ((place + which) ^ 1) - which
        if not 0 <= target < extent:
            pairs.append((source, source ^ 1 if rows else source ^ (2 * TILES_X)))
        else:
            pairs.append((source, target * TILES_X + col if rows else row * TILES_X + target))
    return lax.ppermute(value, "seq", pairs)


def widened(block, stride):
    count = lax.axis_size("seq")

    def swapped(mask):
        pairs = [(source, source ^ (mask * stride)) for source in range(count)]
        return lax.ppermute(block, "seq", pairs)

    return [block] + [swapped(mask) for mask in (1, 2, 3)]


def pairs_to_heads_kernel(k, v, kv):
    for i, x in enumerate((k, v)):
        kv[:, i] = jnp.swapaxes(x[0], 0, 1)


def pairs_to_heads(k, v):
    t, h, d = k.shape[1:]
    return pl.pallas_call(
        pairs_to_heads_kernel,
        out_shape=sds(h, 2, t, d),
        compiler_params=PARAMS,
        name="pairs_to_heads",
    )(k, v)


def to_heads_kernel(x, y, a, b):
    a[...] = jnp.swapaxes(x[0], 0, 1)
    b[...] = jnp.swapaxes(y[0], 0, 1)


def to_heads(x, y):
    t, h, d = x.shape[1:]
    return pl.pallas_call(
        to_heads_kernel,
        out_shape=[sds(h, t, d)] * 2,
        compiler_params=PARAMS,
        name="to_heads",
    )(x, y)


def halo_to_heads_kernel(even, x, y, up, dn):
    a = jnp.swapaxes(x[:, 0], 0, 1)
    b = jnp.swapaxes(y[:, 0], 0, 1)
    up[:, 0] = lax.select(even[0] == 1, b, a)
    dn[:, 0] = lax.select(even[0] == 1, a, b)


def halo_to_heads(even, x, y):
    t, _, h, d = x.shape
    tokens = pl.BlockSpec((t, 1, h, d), lambda g: (0, g, 0, 0))
    heads = pl.BlockSpec((h, 1, t, d), lambda g: (0, g, 0, 0))
    return pl.pallas_call(
        halo_to_heads_kernel,
        grid=(2,),
        in_specs=[SMEM, tokens, tokens],
        out_specs=[heads, heads],
        out_shape=[sds(h, 2, t, d)] * 2,
        compiler_params=PARAMS,
        name="halo_to_heads",
    )(even, x, y)


def far_kernel(*refs):
    out = refs[-1]
    n = refs[0].shape[0]
    for j, piece in enumerate(refs[:-1]):
        out[:, 0, j * n : (j + 1) * n] = jnp.swapaxes(piece[:, 0], 0, 1)


def far_heads(pieces):
    n, _, h, d = pieces[0].shape
    t = n * len(pieces)
    return pl.pallas_call(
        far_kernel,
        grid=(2,),
        in_specs=[pl.BlockSpec((n, 1, h, d), lambda g: (0, g, 0, 0))] * len(pieces),
        out_specs=pl.BlockSpec((h, 1, t, d), lambda g: (0, g, 0, 0)),
        out_shape=sds(h, 2, t, d),
        compiler_params=PARAMS,
        name="far_heads",
    )(*pieces)


def sides_kernel(even, a, b, ka, kb, va, vb, *outs):
    h, d = a.shape[2:]
    n = h // CHUNKS
    for j, (mine, e) in enumerate((((ka, va), even[1]), ((kb, vb), 1 - even[1]))):
        for i in range(2):
            x = mine[i][...].reshape(SIDE, h, d)
            for c in range(CHUNKS):
                outs[j * CHUNKS + c][CORNER : CORNER + SIDE, i] = x[:, c * n : (c + 1) * n]
            for g, rows in enumerate((a, b)):
                end = (STRIP - CORNER) * (g ^ even[0])
                for r in range(RADIUS):
                    x = rows[pl.ds(r * TILE_W + (TILE_W - RADIUS) * e, RADIUS), i]
                    for c in range(CHUNKS):
                        outs[j * CHUNKS + c][pl.ds(end + r * RADIUS, RADIUS), i] = x[:, c * n : (c + 1) * n]


def sides(even, a, b, k, v):
    h, d = a.shape[2:]
    k = k.reshape(TILE_H, TILE_W, h, d)
    v = v.reshape(TILE_H, TILE_W, h, d)
    block = (TILE_H, RADIUS, h, d)
    last = TILE_W // RADIUS - 1
    whole = pl.BlockSpec(a.shape, lambda g, e: (0, 0, 0, 0))
    side_a = pl.BlockSpec(block, lambda g, e: (0, last * e[1], 0, 0))
    side_b = pl.BlockSpec(block, lambda g, e: (0, last * (1 - e[1]), 0, 0))
    shape = (STRIP, 2, h // CHUNKS, d)
    outs = pl.pallas_call(
        sides_kernel,
        grid_spec=pltpu.PrefetchScalarGridSpec(
            num_scalar_prefetch=1,
            grid=(1,),
            in_specs=[whole, whole, side_a, side_b, side_a, side_b],
            out_specs=[pl.BlockSpec(shape, lambda g, e: (0, 0, 0, 0))] * (2 * CHUNKS),
        ),
        out_shape=[sds(*shape)] * (2 * CHUNKS),
        compiler_params=PARAMS,
        name="sides",
    )(even, a, b, k, k, v, v)
    return outs[:CHUNKS], outs[CHUNKS:]


def to_tokens_kernel(*refs):
    n = (len(refs) - 2) // 2
    for j in range(2):
        x = jnp.concatenate([r[...] for r in refs[j * n : (j + 1) * n]], 0)
        refs[2 * n + j][0] = jnp.swapaxes(x, 0, 1)


def to_tokens(xs, ys):
    h, t, d = xs[0].shape
    return pl.pallas_call(
        to_tokens_kernel,
        out_shape=[sds(1, t, h * len(xs), d)] * 2,
        compiler_params=PARAMS,
        name="to_tokens",
    )(*xs, *ys)


def fold_kernel(even, *refs):
    gup, gdn, from_a, from_b = (refs[c * CHUNKS : (c + 1) * CHUNKS] for c in range(4))
    a, b = refs[4 * CHUNKS :]
    t, _, h, d = a.shape

    def tokens(parts, rows, cols):
        x = jnp.concatenate([r[:, 0, rows] for r in parts], 0)
        return jnp.swapaxes(x, 0, 1).astype(F32).reshape(RADIUS, cols, h, d)

    folded = []
    for g, o in ((gup, 0), (gdn, STRIP - CORNER)):
        x = tokens(g, slice(0, t), TILE_W)
        sa, sb = (tokens(s, slice(o, o + CORNER), RADIUS) for s in (from_a, from_b))
        left = lax.select(even[1] == 1, sb, sa)
        right = lax.select(even[1] == 1, sa, sb)
        x = jnp.concatenate(
            [x[:, :RADIUS] + left, x[:, RADIUS : TILE_W - RADIUS], x[:, TILE_W - RADIUS :] + right], 1
        )
        folded.append(x.reshape(t, h, d).astype(BF))
    a[:, 0] = lax.select(even[0] == 1, folded[1], folded[0])
    b[:, 0] = lax.select(even[0] == 1, folded[0], folded[1])


def fold(even, gup, gdn, from_a, from_b):
    args = (*gup, *gdn, *from_a, *from_b)
    h, _, t, d = gup[0].shape
    h *= CHUNKS
    return pl.pallas_call(
        fold_kernel,
        grid=(2,),
        in_specs=[SMEM]
        + [pl.BlockSpec((x.shape[0], 1) + x.shape[2:], lambda g: (0, g, 0, 0)) for x in args],
        out_specs=[pl.BlockSpec((t, 1, h, d), lambda g: (0, g, 0, 0))] * 2,
        out_shape=[sds(t, 2, h, d)] * 2,
        compiler_params=PARAMS,
        name="fold",
    )(even, *args)


def premerge_kernel(even, *refs):
    own, from_a, from_b = (refs[c * CHUNKS : (c + 1) * CHUNKS] for c in range(3))
    for i, out in enumerate(refs[3 * CHUNKS :]):
        h, d = out.shape[2:]

        def tokens(parts, rows, *lead):
            x = jnp.concatenate([r[:, i, rows] for r in parts], 0)
            return jnp.swapaxes(x, 0, 1).astype(F32).reshape(*lead, h, d)

        t = tokens(own, slice(0, TOKENS), TILE_H, TILE_W)
        sa = tokens(from_a, slice(CORNER, CORNER + SIDE), TILE_H, RADIUS)
        sb = tokens(from_b, slice(CORNER, CORNER + SIDE), TILE_H, RADIUS)
        le = lax.select(even[1] == 1, sb, sa)
        ri = lax.select(even[1] == 1, sa, sb)
        t = jnp.concatenate(
            [t[:, :RADIUS] + le, t[:, RADIUS : TILE_W - RADIUS], t[:, TILE_W - RADIUS :] + ri], 1
        )
        out[0] = t.reshape(TOKENS, h, d).astype(BF)


def premerge(even, own, from_a, from_b):
    h, _, t, d = own[0].shape
    return pl.pallas_call(
        premerge_kernel,
        in_specs=[SMEM] + [VMEM] * (3 * CHUNKS),
        out_shape=[sds(1, t, h * CHUNKS, d)] * 2,
        compiler_params=PARAMS,
        name="premerge",
    )(even, *own, *from_a, *from_b)


def finish_kernel(even, dk, dv, from_a, from_b, dk_out, dv_out):
    for g, part in enumerate((from_a, from_b)):

        @pl.when(pl.program_id(0) == g)
        def _():
            for i, (x, out) in enumerate(((dk, dk_out), (dv, dv_out))):
                out[0] = (x[0].astype(F32) + part[:, i].astype(F32)).astype(BF)


def finish(even, dk, dv, from_a, from_b):
    h, d = dk.shape[2:]
    last = TOKENS // EDGE - 1
    rows = pl.BlockSpec((1, EDGE, h, d), lambda g, e: (0, last * (g ^ e[0]), 0, 0))
    part = pl.BlockSpec(from_a.shape, lambda g, e: (0, 0, 0, 0))
    return pl.pallas_call(
        finish_kernel,
        grid_spec=pltpu.PrefetchScalarGridSpec(
            num_scalar_prefetch=1,
            grid=(2,),
            in_specs=[rows, rows, part, part],
            out_specs=[rows, rows],
        ),
        out_shape=[sds(*dk.shape)] * 2,
        input_output_aliases={1: 0, 2: 1},
        compiler_params=PARAMS,
        name="finish",
    )(even, dk, dv, from_a, from_b)


def attend_kernel(
    heads, q, do, kv, up, dn, far, sa, sb, bias, even, att, dq, own, gup, gdn, ga, gb, strips_lr
):
    @pl.when(pl.program_id(0) == 0)
    def _():
        for src, side in ((sa, even[1]), (sb, 1 - even[1])):
            for i in range(2):
                strips_lr[side, :, i] = jnp.swapaxes(src[:, i], 0, 1)

    first = pl.program_id(0) * heads
    scale = q.shape[-1] ** -0.5
    half = WIN_ROWS * RADIUS
    mid = WIN_ROWS * TILE_W

    def strips(h, i):
        center = jnp.concatenate([up[h, i], kv[h, i], dn[h, i]], 0)
        return center, strips_lr[0, first + h, i], strips_lr[1, first + h, i], far[h, i]

    def window(parts, b):
        c, l, r, f = parts
        o, s = b * BLOCK_ROWS * TILE_W, b * BLOCK_ROWS * RADIUS
        return jnp.concatenate([c[o : o + mid], l[s : s + half], r[s : s + half], f], 0)

    parts = [[strips(h, i) for i in range(2)] for h in range(heads)]
    grads = {}

    def block(h, b):
        rows = slice(b * QUERIES, (b + 1) * QUERIES)
        queries, cots = q[h, rows], do[h, rows]
        keys, values = window(parts[h][0], b), window(parts[h][1], b)
        s = nt(queries, keys)
        dp = nt(cots, values)
        yield
        s = s * (scale * LOG2E)
        s = jnp.concatenate([s[:, :NEAR] + bias[b], s[:, NEAR:]], 1)
        top = jnp.max(s, 1, keepdims=True)
        yield
        e = jnp.exp2(s - top)
        inverse = 1.0 / jnp.sum(e, 1, keepdims=True)
        yield
        p = e * inverse
        rounded = p.astype(BF)
        out = nn(rounded, values).astype(BF)
        dv = tn(rounded[:, :NEAR], cots)
        yield
        att[h, rows] = out
        delta = jnp.sum(out.astype(F32) * cots.astype(F32), 1, keepdims=True)
        ds = (p * (dp - delta) * scale).astype(BF)
        dqs = nn(ds, keys)
        dk = tn(ds[:, :NEAR], queries)
        yield
        dq[h, rows] = dqs.astype(BF)
        grads[h, b] = (dk, dv)

    live = [block(h, b) for h in range(heads) for b in range(BLOCKS)]
    while live:
        for g in list(live):
            try:
                next(g)
            except StopIteration:
                live.remove(g)

    step = BLOCK_ROWS * TILE_W
    for h in range(heads):
        for i in range(2):
            g = [grads[h, b][i] for b in range(BLOCKS)]
            c = [g[0][:step], g[0][step:mid] + g[1][:step], g[1][step:mid] + g[2][:step], g[2][step:mid]]
            c = jnp.concatenate(c, 0)
            gup[h, i] = c[:EDGE].astype(BF)
            own[h, i] = c[EDGE : EDGE + TOKENS].astype(own.dtype)
            gdn[h, i] = c[EDGE + TOKENS :].astype(BF)
            w = BLOCK_ROWS * RADIUS
            sides = []
            for j in range(2):
                s = [x[mid + j * half : mid + (j + 1) * half] for x in g]
                s = jnp.concatenate([s[0][:w], s[0][w:] + s[1][:w], s[1][w:] + s[2][:w], s[2][w:]], 0)
                sides.append(s.astype(BF))
            ga[h, i] = lax.select(even[1] == 1, sides[1], sides[0])
            gb[h, i] = lax.select(even[1] == 1, sides[0], sides[1])


def attend(chunk, even, q, do, kv, up, dn, far, sa, sb, bias, heads=2):
    _, t, d = q.shape
    h = sa.shape[2]
    steps = h // heads

    def spec(x, offset=0):
        return pl.BlockSpec((heads,) + x.shape[1:], lambda g: (g + offset,) + (0,) * (len(x.shape) - 1))

    def whole(x):
        return pl.BlockSpec(x.shape, lambda g: (0,) * len(x.shape))

    outs = [sds(h, t, d)] * 2 + [sds(h, 2, n, d) for n in (t, EDGE, EDGE, STRIP, STRIP)]
    flops = h * BLOCKS * QUERIES * (4 * (NEAR + far.shape[2]) + 2 * NEAR) * d * 2
    args = (q, do, kv, up, dn, far)
    return pl.pallas_call(
        functools.partial(attend_kernel, heads),
        grid=(steps,),
        in_specs=[spec(x, chunk * steps) for x in args] + [whole(x) for x in (sa, sb, bias)] + [SMEM],
        out_specs=[spec(x) for x in outs],
        out_shape=outs,
        scratch_shapes=[pltpu.VMEM((2, h, 2, STRIP, d), BF)],
        compiler_params=PARAMS,
        cost_estimate=pl.CostEstimate(flops=flops, bytes_accessed=12 << 20, transcendentals=0),
        name="attend",
    )(*args, sa, sb, bias, even)


def near_bias():
    position = lax.axis_index("seq")
    tiles_y = lax.axis_size("seq") // TILES_X
    shape = (BLOCKS, QUERIES, NEAR)
    b = lax.broadcasted_iota(jnp.int32, shape, 0)
    i = lax.broadcasted_iota(jnp.int32, shape, 1)
    k = lax.broadcasted_iota(jnp.int32, shape, 2)
    mid = WIN_ROWS * TILE_W
    half = WIN_ROWS * RADIUS
    k_row = jnp.where(k < mid, k // TILE_W, (k - mid) % half // RADIUS) - RADIUS
    side = jnp.where(k < mid + half, k % RADIUS - RADIUS, k % RADIUS + TILE_W)
    k_col = jnp.where(k < mid, k % TILE_W, side)
    seen = (jnp.abs(k_row - i // TILE_W) <= RADIUS) & (jnp.abs(k_col - i % TILE_W) <= RADIUS)
    row = position // TILES_X * TILE_H + b * BLOCK_ROWS + k_row
    col = position % TILES_X * TILE_W + k_col
    inside = (row >= 0) & (row < tiles_y * TILE_H) & (col >= 0) & (col < TILES_X * TILE_W)
    return jnp.where(seen & inside, 0.0, FLOOR).astype(F32)


def shards(fine_queries, fine_keys, fine_values, coarse_keys, coarse_values, out_grad):
    position = lax.axis_index("seq")
    even = jnp.stack([1 - position // TILES_X % 2, 1 - position % TILES_X % 2]).astype(jnp.int32)
    coarse = jnp.concatenate(widened(jnp.stack([coarse_keys[0], coarse_values[0]], 1), 4), 0)
    start = even[0] * (TOKENS - EDGE)
    rows = [
        jnp.stack([lax.dynamic_slice_in_dim(x[0], o, EDGE, 0) for x in (fine_keys, fine_values)], 1)
        for o in (start, TOKENS - EDGE - start)
    ]
    coarse, *rows = lax.optimization_barrier((coarse, *rows))
    row_a, row_b = (exchange(x, True, which) for which, x in enumerate(rows))
    coarse = jnp.concatenate(widened(coarse, 16), 0)
    coarse, fine_queries, out_grad, fine_keys, fine_values = lax.optimization_barrier(
        (coarse, fine_queries, out_grad, fine_keys, fine_values)
    )
    pieces = widened(coarse, 1)
    queries, cots = to_heads(fine_queries, out_grad)
    kv = pairs_to_heads(fine_keys, fine_values)
    bias = near_bias()
    row_a, row_b, kv, queries, cots, bias = lax.optimization_barrier((row_a, row_b, kv, queries, cots, bias))
    strips = sides(even, row_a, row_b, fine_keys[0], fine_values[0])
    side_a, side_b = ([exchange(x, False, which) for x in xs] for which, xs in enumerate(strips))
    up, dn = halo_to_heads(even, row_a, row_b)
    far = far_heads(pieces)
    att, dq, own, gup, gdn, from_a, from_b = ([] for _ in range(7))
    for c in range(CHUNKS):
        a, b, mine, u, n, ga, gb = attend(
            c, even, queries, cots, kv, up, dn, far, side_a[c], side_b[c], bias
        )
        from_a.append(exchange(ga, False, 0))
        from_b.append(exchange(gb, False, 1))
        for xs, x in ((att, a), (dq, b), (own, mine), (gup, u), (gdn, n)):
            xs.append(x)
    to_a, to_b = fold(even, gup, gdn, from_a, from_b)
    to_a, to_b = exchange(to_a, True, 0), exchange(to_b, True, 1)
    attended, query_grad = to_tokens(att, dq)
    dk, dv = premerge(even, own, from_a, from_b)
    key_grad, value_grad = finish(even, dk, dv, to_a, to_b)
    return (attended, query_grad, key_grad, value_grad)


def solution(mesh):
    spec = P("dp", "seq", "head", None)
    return jax.shard_map(
        shards, mesh=mesh, in_specs=(spec,) * 6, out_specs=(spec,) * 4, check_vma=False
    )
```

```python
import functools

import jax
import jax.numpy as jnp
from jax import lax
from jax.experimental import pallas as pl
from jax.experimental.pallas import tpu as pltpu
from jax.sharding import PartitionSpec as P

TILE_H = 24
TILE_W = 16
RADIUS = 4
TILES_X = 8
TOKENS = TILE_H * TILE_W
EDGE = RADIUS * TILE_W
SIDE = TILE_H * RADIUS
CORNER = RADIUS * RADIUS
STRIP = SIDE + 2 * CORNER
CHUNKS = 2
BLOCK_ROWS = 8
BLOCKS = TILE_H // BLOCK_ROWS
QUERIES = BLOCK_ROWS * TILE_W
WIN_ROWS = BLOCK_ROWS + 2 * RADIUS
NEAR = WIN_ROWS * (TILE_W + 2 * RADIUS)
FLOOR = -1e30
LOG2E = 1.4426950408889634
BF = jnp.bfloat16
F32 = jnp.float32
SMEM = pl.BlockSpec(memory_space=pltpu.SMEM)
VMEM = pl.BlockSpec(memory_space=pltpu.VMEM)
PARAMS = pltpu.CompilerParams(vmem_limit_bytes=63 << 20)


def nt(a, b):
    return lax.dot_general(a, b, (((1,), (1,)), ((), ())), preferred_element_type=F32)


def tn(a, b):
    return lax.dot_general(a, b, (((0,), (0,)), ((), ())), preferred_element_type=F32)


def nn(a, b):
    return lax.dot_general(a, b, (((1,), (0,)), ((), ())), preferred_element_type=F32)


def sds(*shape):
    return jax.ShapeDtypeStruct(shape, BF)


def exchange(value, rows, which):
    count = lax.axis_size("seq")
    pairs = []
    for source in range(count):
        row, col = divmod(source, TILES_X)
        place, extent = (row, count // TILES_X) if rows else (col, TILES_X)
        target = ((place + which) ^ 1) - which
        if not 0 <= target < extent:
            pairs.append((source, source if rows else source ^ (2 * TILES_X)))
        else:
            pairs.append((source, target * TILES_X + col if rows else row * TILES_X + target))
    return lax.ppermute(value, "seq", pairs)


def widened(block, stride):
    count = lax.axis_size("seq")

    def swapped(mask):
        pairs = [(source, source ^ (mask * stride)) for source in range(count)]
        return lax.ppermute(block, "seq", pairs)

    return [block] + [swapped(mask) for mask in (1, 2, 3)]


def pairs_to_heads_kernel(k, v, kv):
    for i, x in enumerate((k, v)):
        kv[:, i] = jnp.swapaxes(x[0], 0, 1)


def pairs_to_heads(k, v):
    t, h, d = k.shape[1:]
    return pl.pallas_call(
        pairs_to_heads_kernel,
        out_shape=sds(h, 2, t, d),
        compiler_params=PARAMS,
        name="pairs_to_heads",
    )(k, v)


def to_heads_kernel(x, y, a, b):
    a[...] = jnp.swapaxes(x[0], 0, 1)
    b[...] = jnp.swapaxes(y[0], 0, 1)


def to_heads(x, y):
    t, h, d = x.shape[1:]
    return pl.pallas_call(
        to_heads_kernel,
        out_shape=[sds(h, t, d)] * 2,
        compiler_params=PARAMS,
        name="to_heads",
    )(x, y)


def halo_to_heads_kernel(even, x, y, up, dn):
    a = jnp.swapaxes(x[:, 0], 0, 1)
    b = jnp.swapaxes(y[:, 0], 0, 1)
    up[:, 0] = lax.select(even[0] == 1, b, a)
    dn[:, 0] = lax.select(even[0] == 1, a, b)


def halo_to_heads(even, x, y):
    t, _, h, d = x.shape
    tokens = pl.BlockSpec((t, 1, h, d), lambda g: (0, g, 0, 0))
    heads = pl.BlockSpec((h, 1, t, d), lambda g: (0, g, 0, 0))
    return pl.pallas_call(
        halo_to_heads_kernel,
        grid=(2,),
        in_specs=[SMEM, tokens, tokens],
        out_specs=[heads, heads],
        out_shape=[sds(h, 2, t, d)] * 2,
        compiler_params=PARAMS,
        name="halo_to_heads",
    )(even, x, y)


def far_kernel(*refs):
    out = refs[-1]
    n = refs[0].shape[0]
    for j, piece in enumerate(refs[:-1]):
        out[:, 0, j * n : (j + 1) * n] = jnp.swapaxes(piece[:, 0], 0, 1)


def far_heads(pieces):
    n, _, h, d = pieces[0].shape
    t = n * len(pieces)
    return pl.pallas_call(
        far_kernel,
        grid=(2,),
        in_specs=[pl.BlockSpec((n, 1, h, d), lambda g: (0, g, 0, 0))] * len(pieces),
        out_specs=pl.BlockSpec((h, 1, t, d), lambda g: (0, g, 0, 0)),
        out_shape=sds(h, 2, t, d),
        compiler_params=PARAMS,
        name="far_heads",
    )(*pieces)


def sides_kernel(even, a, b, ka, kb, va, vb, *outs):
    h, d = a.shape[2:]
    n = h // CHUNKS
    for j, (mine, e) in enumerate((((ka, va), even[1]), ((kb, vb), 1 - even[1]))):
        for i in range(2):
            x = mine[i][...].reshape(SIDE, h, d)
            for c in range(CHUNKS):
                outs[j * CHUNKS + c][CORNER : CORNER + SIDE, i] = x[:, c * n : (c + 1) * n]
            for g, rows in enumerate((a, b)):
                end = (STRIP - CORNER) * (g ^ even[0])
                for r in range(RADIUS):
                    x = rows[pl.ds(r * TILE_W + (TILE_W - RADIUS) * e, RADIUS), i]
                    for c in range(CHUNKS):
                        outs[j * CHUNKS + c][pl.ds(end + r * RADIUS, RADIUS), i] = x[:, c * n : (c + 1) * n]


def sides(even, a, b, k, v):
    h, d = a.shape[2:]
    k = k.reshape(TILE_H, TILE_W, h, d)
    v = v.reshape(TILE_H, TILE_W, h, d)
    block = (TILE_H, RADIUS, h, d)
    last = TILE_W // RADIUS - 1
    whole = pl.BlockSpec(a.shape, lambda g, e: (0, 0, 0, 0))
    side_a = pl.BlockSpec(block, lambda g, e: (0, last * e[1], 0, 0))
    side_b = pl.BlockSpec(block, lambda g, e: (0, last * (1 - e[1]), 0, 0))
    shape = (STRIP, 2, h // CHUNKS, d)
    outs = pl.pallas_call(
        sides_kernel,
        grid_spec=pltpu.PrefetchScalarGridSpec(
            num_scalar_prefetch=1,
            grid=(1,),
            in_specs=[whole, whole, side_a, side_b, side_a, side_b],
            out_specs=[pl.BlockSpec(shape, lambda g, e: (0, 0, 0, 0))] * (2 * CHUNKS),
        ),
        out_shape=[sds(*shape)] * (2 * CHUNKS),
        compiler_params=PARAMS,
        name="sides",
    )(even, a, b, k, k, v, v)
    return outs[:CHUNKS], outs[CHUNKS:]


def to_tokens_kernel(*refs):
    n = (len(refs) - 2) // 2
    for j in range(2):
        x = jnp.concatenate([r[...] for r in refs[j * n : (j + 1) * n]], 0)
        refs[2 * n + j][0] = jnp.swapaxes(x, 0, 1)


def to_tokens(xs, ys):
    h, t, d = xs[0].shape
    return pl.pallas_call(
        to_tokens_kernel,
        out_shape=[sds(1, t, h * len(xs), d)] * 2,
        compiler_params=PARAMS,
        name="to_tokens",
    )(*xs, *ys)


def fold_kernel(even, *refs):
    gup, gdn, from_a, from_b = (refs[c * CHUNKS : (c + 1) * CHUNKS] for c in range(4))
    a, b = refs[4 * CHUNKS :]
    t, _, h, d = a.shape

    def tokens(parts, rows, cols):
        x = jnp.concatenate([r[:, 0, rows] for r in parts], 0)
        return jnp.swapaxes(x, 0, 1).astype(F32).reshape(RADIUS, cols, h, d)

    folded = []
    for g, o in ((gup, 0), (gdn, STRIP - CORNER)):
        x = tokens(g, slice(0, t), TILE_W)
        sa, sb = (tokens(s, slice(o, o + CORNER), RADIUS) for s in (from_a, from_b))
        left = lax.select(even[1] == 1, sb, sa)
        right = lax.select(even[1] == 1, sa, sb)
        x = jnp.concatenate(
            [x[:, :RADIUS] + left, x[:, RADIUS : TILE_W - RADIUS], x[:, TILE_W - RADIUS :] + right], 1
        )
        folded.append(x.reshape(t, h, d).astype(BF))
    a[:, 0] = lax.select(even[0] == 1, folded[1], folded[0])
    b[:, 0] = lax.select(even[0] == 1, folded[0], folded[1])


def fold(even, gup, gdn, from_a, from_b):
    args = (*gup, *gdn, *from_a, *from_b)
    h, _, t, d = gup[0].shape
    h *= CHUNKS
    return pl.pallas_call(
        fold_kernel,
        grid=(2,),
        in_specs=[SMEM]
        + [pl.BlockSpec((x.shape[0], 1) + x.shape[2:], lambda g: (0, g, 0, 0)) for x in args],
        out_specs=[pl.BlockSpec((t, 1, h, d), lambda g: (0, g, 0, 0))] * 2,
        out_shape=[sds(t, 2, h, d)] * 2,
        compiler_params=PARAMS,
        name="fold",
    )(even, *args)


def premerge_kernel(even, *refs):
    own, from_a, from_b = (refs[c * CHUNKS : (c + 1) * CHUNKS] for c in range(3))
    for i, out in enumerate(refs[3 * CHUNKS :]):
        h, d = out.shape[2:]

        def tokens(parts, rows, *lead):
            x = jnp.concatenate([r[:, i, rows] for r in parts], 0)
            return jnp.swapaxes(x, 0, 1).astype(F32).reshape(*lead, h, d)

        t = tokens(own, slice(0, TOKENS), TILE_H, TILE_W)
        sa = tokens(from_a, slice(CORNER, CORNER + SIDE), TILE_H, RADIUS)
        sb = tokens(from_b, slice(CORNER, CORNER + SIDE), TILE_H, RADIUS)
        le = lax.select(even[1] == 1, sb, sa)
        ri = lax.select(even[1] == 1, sa, sb)
        t = jnp.concatenate(
            [t[:, :RADIUS] + le, t[:, RADIUS : TILE_W - RADIUS], t[:, TILE_W - RADIUS :] + ri], 1
        )
        out[0] = t.reshape(TOKENS, h, d).astype(BF)


def premerge(even, own, from_a, from_b):
    h, _, t, d = own[0].shape
    return pl.pallas_call(
        premerge_kernel,
        in_specs=[SMEM] + [VMEM] * (3 * CHUNKS),
        out_shape=[sds(1, t, h * CHUNKS, d)] * 2,
        compiler_params=PARAMS,
        name="premerge",
    )(even, *own, *from_a, *from_b)


def finish_kernel(even, dk, dv, from_a, from_b, dk_out, dv_out):
    for g, part in enumerate((from_a, from_b)):

        @pl.when(pl.program_id(0) == g)
        def _():
            for i, (x, out) in enumerate(((dk, dk_out), (dv, dv_out))):
                out[0] = (x[0].astype(F32) + part[:, i].astype(F32)).astype(BF)


def finish(even, dk, dv, from_a, from_b):
    h, d = dk.shape[2:]
    last = TOKENS // EDGE - 1
    rows = pl.BlockSpec((1, EDGE, h, d), lambda g, e: (0, last * (g ^ e[0]), 0, 0))
    part = pl.BlockSpec(from_a.shape, lambda g, e: (0, 0, 0, 0))
    return pl.pallas_call(
        finish_kernel,
        grid_spec=pltpu.PrefetchScalarGridSpec(
            num_scalar_prefetch=1,
            grid=(2,),
            in_specs=[rows, rows, part, part],
            out_specs=[rows, rows],
        ),
        out_shape=[sds(*dk.shape)] * 2,
        input_output_aliases={1: 0, 2: 1},
        compiler_params=PARAMS,
        name="finish",
    )(even, dk, dv, from_a, from_b)


def attend_kernel(
    heads, q, do, kv, up, dn, far, sa, sb, bias, even, att, dq, own, gup, gdn, ga, gb, strips_lr
):
    @pl.when(pl.program_id(0) == 0)
    def _():
        for src, side in ((sa, even[1]), (sb, 1 - even[1])):
            for i in range(2):
                strips_lr[side, :, i] = jnp.swapaxes(src[:, i], 0, 1)

    first = pl.program_id(0) * heads
    scale = q.shape[-1] ** -0.5
    half = WIN_ROWS * RADIUS
    mid = WIN_ROWS * TILE_W

    def strips(h, i):
        center = jnp.concatenate([up[h, i], kv[h, i], dn[h, i]], 0)
        return center, strips_lr[0, first + h, i], strips_lr[1, first + h, i], far[h, i]

    def window(parts, b):
        c, l, r, f = parts
        o, s = b * BLOCK_ROWS * TILE_W, b * BLOCK_ROWS * RADIUS
        return jnp.concatenate([c[o : o + mid], l[s : s + half], r[s : s + half], f], 0)

    parts = [[strips(h, i) for i in range(2)] for h in range(heads)]
    grads = {}

    def block(h, b):
        rows = slice(b * QUERIES, (b + 1) * QUERIES)
        queries, cots = q[h, rows], do[h, rows]
        keys, values = window(parts[h][0], b), window(parts[h][1], b)
        s = nt(queries, keys)
        dp = nt(cots, values)
        yield
        s = s * (scale * LOG2E)
        s = jnp.concatenate([s[:, :NEAR] + bias[b], s[:, NEAR:]], 1)
        top = jnp.max(s, 1, keepdims=True)
        yield
        e = jnp.exp2(s - top)
        inverse = 1.0 / jnp.sum(e, 1, keepdims=True)
        yield
        p = e * inverse
        rounded = p.astype(BF)
        out = nn(rounded, values).astype(BF)
        dv = tn(rounded[:, :NEAR], cots)
        yield
        att[h, rows] = out
        delta = jnp.sum(out.astype(F32) * cots.astype(F32), 1, keepdims=True)
        ds = (p * (dp - delta) * scale).astype(BF)
        dqs = nn(ds, keys)
        dk = tn(ds[:, :NEAR], queries)
        yield
        dq[h, rows] = dqs.astype(BF)
        grads[h, b] = (dk, dv)

    live = [block(h, b) for h in range(heads) for b in range(BLOCKS)]
    while live:
        for g in list(live):
            try:
                next(g)
            except StopIteration:
                live.remove(g)

    step = BLOCK_ROWS * TILE_W
    for h in range(heads):
        for i in range(2):
            g = [grads[h, b][i] for b in range(BLOCKS)]
            c = [g[0][:step], g[0][step:mid] + g[1][:step], g[1][step:mid] + g[2][:step], g[2][step:mid]]
            c = jnp.concatenate(c, 0)
            gup[h, i] = c[:EDGE].astype(BF)
            own[h, i] = c[EDGE : EDGE + TOKENS].astype(own.dtype)
            gdn[h, i] = c[EDGE + TOKENS :].astype(BF)
            w = BLOCK_ROWS * RADIUS
            sides = []
            for j in range(2):
                s = [x[mid + j * half : mid + (j + 1) * half] for x in g]
                s = jnp.concatenate([s[0][:w], s[0][w:] + s[1][:w], s[1][w:] + s[2][:w], s[2][w:]], 0)
                sides.append(s.astype(BF))
            ga[h, i] = lax.select(even[1] == 1, sides[1], sides[0])
            gb[h, i] = lax.select(even[1] == 1, sides[0], sides[1])


def attend(chunk, even, q, do, kv, up, dn, far, sa, sb, bias, heads=2):
    _, t, d = q.shape
    h = sa.shape[2]
    steps = h // heads

    def spec(x, offset=0):
        return pl.BlockSpec((heads,) + x.shape[1:], lambda g: (g + offset,) + (0,) * (len(x.shape) - 1))

    def whole(x):
        return pl.BlockSpec(x.shape, lambda g: (0,) * len(x.shape))

    outs = [sds(h, t, d)] * 2 + [sds(h, 2, n, d) for n in (t, EDGE, EDGE, STRIP, STRIP)]
    flops = h * BLOCKS * QUERIES * (4 * (NEAR + far.shape[2]) + 2 * NEAR) * d * 2
    args = (q, do, kv, up, dn, far)
    return pl.pallas_call(
        functools.partial(attend_kernel, heads),
        grid=(steps,),
        in_specs=[spec(x, chunk * steps) for x in args] + [whole(x) for x in (sa, sb, bias)] + [SMEM],
        out_specs=[spec(x) for x in outs],
        out_shape=outs,
        scratch_shapes=[pltpu.VMEM((2, h, 2, STRIP, d), BF)],
        compiler_params=PARAMS,
        cost_estimate=pl.CostEstimate(flops=flops, bytes_accessed=12 << 20, transcendentals=0),
        name="attend",
    )(*args, sa, sb, bias, even)


def near_bias():
    position = lax.axis_index("seq")
    tiles_y = lax.axis_size("seq") // TILES_X
    shape = (BLOCKS, QUERIES, NEAR)
    b = lax.broadcasted_iota(jnp.int32, shape, 0)
    i = lax.broadcasted_iota(jnp.int32, shape, 1)
    k = lax.broadcasted_iota(jnp.int32, shape, 2)
    mid = WIN_ROWS * TILE_W
    half = WIN_ROWS * RADIUS
    k_row = jnp.where(k < mid, k // TILE_W, (k - mid) % half // RADIUS) - RADIUS
    side = jnp.where(k < mid + half, k % RADIUS - RADIUS, k % RADIUS + TILE_W)
    k_col = jnp.where(k < mid, k % TILE_W, side)
    seen = (jnp.abs(k_row - i // TILE_W) <= RADIUS) & (jnp.abs(k_col - i % TILE_W) <= RADIUS)
    row = position // TILES_X * TILE_H + b * BLOCK_ROWS + k_row
    col = position % TILES_X * TILE_W + k_col
    inside = (row >= 0) & (row < tiles_y * TILE_H) & (col >= 0) & (col < TILES_X * TILE_W)
    return jnp.where(seen & inside, 0.0, FLOOR).astype(F32)


def shards(fine_queries, fine_keys, fine_values, coarse_keys, coarse_values, out_grad):
    position = lax.axis_index("seq")
    even = jnp.stack([1 - position // TILES_X % 2, 1 - position % TILES_X % 2]).astype(jnp.int32)
    coarse = jnp.concatenate(widened(jnp.stack([coarse_keys[0], coarse_values[0]], 1), 4), 0)
    start = even[0] * (TOKENS - EDGE)
    rows = [
        jnp.stack([lax.dynamic_slice_in_dim(x[0], o, EDGE, 0) for x in (fine_keys, fine_values)], 1)
        for o in (start, TOKENS - EDGE - start)
    ]
    coarse, *rows = lax.optimization_barrier((coarse, *rows))
    row_a, row_b = (exchange(x, True, which) for which, x in enumerate(rows))
    coarse = jnp.concatenate(widened(coarse, 16), 0)
    coarse, fine_queries, out_grad, fine_keys, fine_values = lax.optimization_barrier(
        (coarse, fine_queries, out_grad, fine_keys, fine_values)
    )
    pieces = widened(coarse, 1)
    queries, cots = to_heads(fine_queries, out_grad)
    kv = pairs_to_heads(fine_keys, fine_values)
    bias = near_bias()
    row_a, row_b, kv, queries, cots, bias = lax.optimization_barrier((row_a, row_b, kv, queries, cots, bias))
    strips = sides(even, row_a, row_b, fine_keys[0], fine_values[0])
    side_a, side_b = ([exchange(x, False, which) for x in xs] for which, xs in enumerate(strips))
    up, dn = halo_to_heads(even, row_a, row_b)
    far = far_heads(pieces)
    att, dq, own, gup, gdn, from_a, from_b = ([] for _ in range(7))
    for c in range(CHUNKS):
        a, b, mine, u, n, ga, gb = attend(
            c, even, queries, cots, kv, up, dn, far, side_a[c], side_b[c], bias
        )
        from_a.append(exchange(ga, False, 0))
        from_b.append(exchange(gb, False, 1))
        for xs, x in ((att, a), (dq, b), (own, mine), (gup, u), (gdn, n)):
            xs.append(x)
    to_a, to_b = fold(even, gup, gdn, from_a, from_b)
    to_a, to_b = exchange(to_a, True, 0), exchange(to_b, True, 1)
    attended, query_grad = to_tokens(att, dq)
    dk, dv = premerge(even, own, from_a, from_b)
    key_grad, value_grad = finish(even, dk, dv, to_a, to_b)
    return (attended, query_grad, key_grad, value_grad)


def solution(mesh):
    spec = P("dp", "seq", "head", None)
    return jax.shard_map(
        shards, mesh=mesh, in_specs=(spec,) * 6, out_specs=(spec,) * 4, check_vma=False
    )
```

```python
import functools

import jax
import jax.numpy as jnp
from jax import lax
from jax.experimental import pallas as pl
from jax.experimental.pallas import tpu as pltpu
from jax.sharding import PartitionSpec as P

TILE_H = 24
TILE_W = 16
RADIUS = 4
TILES_X = 8
TOKENS = TILE_H * TILE_W
EDGE = RADIUS * TILE_W
SIDE = TILE_H * RADIUS
CORNER = RADIUS * RADIUS
STRIP = SIDE + 2 * CORNER
CHUNKS = 2
BLOCK_ROWS = 8
BLOCKS = TILE_H // BLOCK_ROWS
QUERIES = BLOCK_ROWS * TILE_W
WIN_ROWS = BLOCK_ROWS + 2 * RADIUS
NEAR = WIN_ROWS * (TILE_W + 2 * RADIUS)
FLOOR = -1e30
LOG2E = 1.4426950408889634
BF = jnp.bfloat16
F32 = jnp.float32
SMEM = pl.BlockSpec(memory_space=pltpu.SMEM)
VMEM = pl.BlockSpec(memory_space=pltpu.VMEM)
PARAMS = pltpu.CompilerParams(vmem_limit_bytes=63 << 20)


def nt(a, b):
    return lax.dot_general(a, b, (((1,), (1,)), ((), ())), preferred_element_type=F32)


def tn(a, b):
    return lax.dot_general(a, b, (((0,), (0,)), ((), ())), preferred_element_type=F32)


def nn(a, b):
    return lax.dot_general(a, b, (((1,), (0,)), ((), ())), preferred_element_type=F32)


def sds(*shape):
    return jax.ShapeDtypeStruct(shape, BF)


def exchange(value, rows, which):
    count = lax.axis_size("seq")
    pairs = []
    for source in range(count):
        row, col = divmod(source, TILES_X)
        place, extent = (row, count // TILES_X) if rows else (col, TILES_X)
        target = ((place + which) ^ 1) - which
        if not 0 <= target < extent:
            pairs.append((source, source))
        else:
            pairs.append((source, target * TILES_X + col if rows else row * TILES_X + target))
    return lax.ppermute(value, "seq", pairs)


def widened(block, stride):
    count = lax.axis_size("seq")

    def swapped(mask):
        pairs = [(source, source ^ (mask * stride)) for source in range(count)]
        return lax.ppermute(block, "seq", pairs)

    return [block] + [swapped(mask) for mask in (1, 2, 3)]


def pairs_to_heads_kernel(k, v, kv):
    for i, x in enumerate((k, v)):
        kv[:, i] = jnp.swapaxes(x[0], 0, 1)


def pairs_to_heads(k, v):
    t, h, d = k.shape[1:]
    return pl.pallas_call(
        pairs_to_heads_kernel,
        out_shape=sds(h, 2, t, d),
        compiler_params=PARAMS,
        name="pairs_to_heads",
    )(k, v)


def to_heads_kernel(x, y, a, b):
    a[...] = jnp.swapaxes(x[0], 0, 1)
    b[...] = jnp.swapaxes(y[0], 0, 1)


def to_heads(x, y):
    t, h, d = x.shape[1:]
    return pl.pallas_call(
        to_heads_kernel,
        out_shape=[sds(h, t, d)] * 2,
        compiler_params=PARAMS,
        name="to_heads",
    )(x, y)


def halo_to_heads_kernel(even, x, y, up, dn):
    a = jnp.swapaxes(x[:, 0], 0, 1)
    b = jnp.swapaxes(y[:, 0], 0, 1)
    up[:, 0] = lax.select(even[0] == 1, b, a)
    dn[:, 0] = lax.select(even[0] == 1, a, b)


def halo_to_heads(even, x, y):
    t, _, h, d = x.shape
    tokens = pl.BlockSpec((t, 1, h, d), lambda g: (0, g, 0, 0))
    heads = pl.BlockSpec((h, 1, t, d), lambda g: (0, g, 0, 0))
    return pl.pallas_call(
        halo_to_heads_kernel,
        grid=(2,),
        in_specs=[SMEM, tokens, tokens],
        out_specs=[heads, heads],
        out_shape=[sds(h, 2, t, d)] * 2,
        compiler_params=PARAMS,
        name="halo_to_heads",
    )(even, x, y)


def far_kernel(*refs):
    out = refs[-1]
    n = refs[0].shape[0]
    for j, piece in enumerate(refs[:-1]):
        out[:, 0, j * n : (j + 1) * n] = jnp.swapaxes(piece[:, 0], 0, 1)


def far_heads(pieces):
    n, _, h, d = pieces[0].shape
    t = n * len(pieces)
    return pl.pallas_call(
        far_kernel,
        grid=(2,),
        in_specs=[pl.BlockSpec((n, 1, h, d), lambda g: (0, g, 0, 0))] * len(pieces),
        out_specs=pl.BlockSpec((h, 1, t, d), lambda g: (0, g, 0, 0)),
        out_shape=sds(h, 2, t, d),
        compiler_params=PARAMS,
        name="far_heads",
    )(*pieces)


def sides_kernel(even, a, b, ka, kb, va, vb, *outs):
    h, d = a.shape[2:]
    n = h // CHUNKS
    for j, (mine, e) in enumerate((((ka, va), even[1]), ((kb, vb), 1 - even[1]))):
        for i in range(2):
            x = mine[i][...].reshape(SIDE, h, d)
            for c in range(CHUNKS):
                outs[j * CHUNKS + c][CORNER : CORNER + SIDE, i] = x[:, c * n : (c + 1) * n]
            for g, rows in enumerate((a, b)):
                end = (STRIP - CORNER) * (g ^ even[0])
                for r in range(RADIUS):
                    x = rows[pl.ds(r * TILE_W + (TILE_W - RADIUS) * e, RADIUS), i]
                    for c in range(CHUNKS):
                        outs[j * CHUNKS + c][pl.ds(end + r * RADIUS, RADIUS), i] = x[:, c * n : (c + 1) * n]


def sides(even, a, b, k, v):
    h, d = a.shape[2:]
    k = k.reshape(TILE_H, TILE_W, h, d)
    v = v.reshape(TILE_H, TILE_W, h, d)
    block = (TILE_H, RADIUS, h, d)
    last = TILE_W // RADIUS - 1
    whole = pl.BlockSpec(a.shape, lambda g, e: (0, 0, 0, 0))
    side_a = pl.BlockSpec(block, lambda g, e: (0, last * e[1], 0, 0))
    side_b = pl.BlockSpec(block, lambda g, e: (0, last * (1 - e[1]), 0, 0))
    shape = (STRIP, 2, h // CHUNKS, d)
    outs = pl.pallas_call(
        sides_kernel,
        grid_spec=pltpu.PrefetchScalarGridSpec(
            num_scalar_prefetch=1,
            grid=(1,),
            in_specs=[whole, whole, side_a, side_b, side_a, side_b],
            out_specs=[pl.BlockSpec(shape, lambda g, e: (0, 0, 0, 0))] * (2 * CHUNKS),
        ),
        out_shape=[sds(*shape)] * (2 * CHUNKS),
        compiler_params=PARAMS,
        name="sides",
    )(even, a, b, k, k, v, v)
    return outs[:CHUNKS], outs[CHUNKS:]


def to_tokens_kernel(*refs):
    n = (len(refs) - 2) // 2
    for j in range(2):
        x = jnp.concatenate([r[...] for r in refs[j * n : (j + 1) * n]], 0)
        refs[2 * n + j][0] = jnp.swapaxes(x, 0, 1)


def to_tokens(xs, ys):
    h, t, d = xs[0].shape
    return pl.pallas_call(
        to_tokens_kernel,
        out_shape=[sds(1, t, h * len(xs), d)] * 2,
        compiler_params=PARAMS,
        name="to_tokens",
    )(*xs, *ys)


def fold_kernel(even, *refs):
    gup, gdn, from_a, from_b = (refs[c * CHUNKS : (c + 1) * CHUNKS] for c in range(4))
    a, b = refs[4 * CHUNKS :]
    t, _, h, d = a.shape

    def tokens(parts, rows, cols):
        x = jnp.concatenate([r[:, 0, rows] for r in parts], 0)
        return jnp.swapaxes(x, 0, 1).astype(F32).reshape(RADIUS, cols, h, d)

    folded = []
    for g, o in ((gup, 0), (gdn, STRIP - CORNER)):
        x = tokens(g, slice(0, t), TILE_W)
        sa, sb = (tokens(s, slice(o, o + CORNER), RADIUS) for s in (from_a, from_b))
        left = lax.select(even[1] == 1, sb, sa)
        right = lax.select(even[1] == 1, sa, sb)
        x = jnp.concatenate(
            [x[:, :RADIUS] + left, x[:, RADIUS : TILE_W - RADIUS], x[:, TILE_W - RADIUS :] + right], 1
        )
        folded.append(x.reshape(t, h, d).astype(BF))
    a[:, 0] = lax.select(even[0] == 1, folded[1], folded[0])
    b[:, 0] = lax.select(even[0] == 1, folded[0], folded[1])


def fold(even, gup, gdn, from_a, from_b):
    args = (*gup, *gdn, *from_a, *from_b)
    h, _, t, d = gup[0].shape
    h *= CHUNKS
    return pl.pallas_call(
        fold_kernel,
        grid=(2,),
        in_specs=[SMEM]
        + [pl.BlockSpec((x.shape[0], 1) + x.shape[2:], lambda g: (0, g, 0, 0)) for x in args],
        out_specs=[pl.BlockSpec((t, 1, h, d), lambda g: (0, g, 0, 0))] * 2,
        out_shape=[sds(t, 2, h, d)] * 2,
        compiler_params=PARAMS,
        name="fold",
    )(even, *args)


def premerge_kernel(even, *refs):
    own, from_a, from_b = (refs[c * CHUNKS : (c + 1) * CHUNKS] for c in range(3))
    for i, out in enumerate(refs[3 * CHUNKS :]):
        h, d = out.shape[2:]

        def tokens(parts, rows, *lead):
            x = jnp.concatenate([r[:, i, rows] for r in parts], 0)
            return jnp.swapaxes(x, 0, 1).astype(F32).reshape(*lead, h, d)

        t = tokens(own, slice(0, TOKENS), TILE_H, TILE_W)
        sa = tokens(from_a, slice(CORNER, CORNER + SIDE), TILE_H, RADIUS)
        sb = tokens(from_b, slice(CORNER, CORNER + SIDE), TILE_H, RADIUS)
        le = lax.select(even[1] == 1, sb, sa)
        ri = lax.select(even[1] == 1, sa, sb)
        t = jnp.concatenate(
            [t[:, :RADIUS] + le, t[:, RADIUS : TILE_W - RADIUS], t[:, TILE_W - RADIUS :] + ri], 1
        )
        out[0] = t.reshape(TOKENS, h, d).astype(BF)


def premerge(even, own, from_a, from_b):
    h, _, t, d = own[0].shape
    return pl.pallas_call(
        premerge_kernel,
        in_specs=[SMEM] + [VMEM] * (3 * CHUNKS),
        out_shape=[sds(1, t, h * CHUNKS, d)] * 2,
        compiler_params=PARAMS,
        name="premerge",
    )(even, *own, *from_a, *from_b)


def finish_kernel(even, dk, dv, from_a, from_b, dk_out, dv_out):
    for g, part in enumerate((from_a, from_b)):

        @pl.when(pl.program_id(0) == g)
        def _():
            for i, (x, out) in enumerate(((dk, dk_out), (dv, dv_out))):
                out[0] = (x[0].astype(F32) + part[:, i].astype(F32)).astype(BF)


def finish(even, dk, dv, from_a, from_b):
    h, d = dk.shape[2:]
    last = TOKENS // EDGE - 1
    rows = pl.BlockSpec((1, EDGE, h, d), lambda g, e: (0, last * (g ^ e[0]), 0, 0))
    part = pl.BlockSpec(from_a.shape, lambda g, e: (0, 0, 0, 0))
    return pl.pallas_call(
        finish_kernel,
        grid_spec=pltpu.PrefetchScalarGridSpec(
            num_scalar_prefetch=1,
            grid=(2,),
            in_specs=[rows, rows, part, part],
            out_specs=[rows, rows],
        ),
        out_shape=[sds(*dk.shape)] * 2,
        input_output_aliases={1: 0, 2: 1},
        compiler_params=PARAMS,
        name="finish",
    )(even, dk, dv, from_a, from_b)


def attend_kernel(
    heads, q, do, kv, up, dn, far, sa, sb, bias, even, att, dq, own, gup, gdn, ga, gb, strips_lr
):
    @pl.when(pl.program_id(0) == 0)
    def _():
        for src, side in ((sa, even[1]), (sb, 1 - even[1])):
            for i in range(2):
                strips_lr[side, :, i] = jnp.swapaxes(src[:, i], 0, 1)

    first = pl.program_id(0) * heads
    scale = q.shape[-1] ** -0.5
    half = WIN_ROWS * RADIUS
    mid = WIN_ROWS * TILE_W

    def strips(h, i):
        center = jnp.concatenate([up[h, i], kv[h, i], dn[h, i]], 0)
        return center, strips_lr[0, first + h, i], strips_lr[1, first + h, i], far[h, i]

    def window(parts, b):
        c, l, r, f = parts
        o, s = b * BLOCK_ROWS * TILE_W, b * BLOCK_ROWS * RADIUS
        return jnp.concatenate([c[o : o + mid], l[s : s + half], r[s : s + half], f], 0)

    parts = [[strips(h, i) for i in range(2)] for h in range(heads)]
    grads = {}

    def block(h, b):
        rows = slice(b * QUERIES, (b + 1) * QUERIES)
        queries, cots = q[h, rows], do[h, rows]
        keys, values = window(parts[h][0], b), window(parts[h][1], b)
        s = nt(queries, keys)
        dp = nt(cots, values)
        yield
        s = s * (scale * LOG2E)
        s = jnp.concatenate([s[:, :NEAR] + bias[b], s[:, NEAR:]], 1)
        top = jnp.max(s, 1, keepdims=True)
        yield
        e = jnp.exp2(s - top)
        inverse = 1.0 / jnp.sum(e, 1, keepdims=True)
        yield
        p = e * inverse
        rounded = p.astype(BF)
        out = nn(rounded, values).astype(BF)
        dv = tn(rounded[:, :NEAR], cots)
        yield
        att[h, rows] = out
        delta = jnp.sum(out.astype(F32) * cots.astype(F32), 1, keepdims=True)
        ds = (p * (dp - delta) * scale).astype(BF)
        dqs = nn(ds, keys)
        dk = tn(ds[:, :NEAR], queries)
        yield
        dq[h, rows] = dqs.astype(BF)
        grads[h, b] = (dk, dv)

    live = [block(h, b) for h in range(heads) for b in range(BLOCKS)]
    while live:
        for g in list(live):
            try:
                next(g)
            except StopIteration:
                live.remove(g)

    step = BLOCK_ROWS * TILE_W
    for h in range(heads):
        for i in range(2):
            g = [grads[h, b][i] for b in range(BLOCKS)]
            c = [g[0][:step], g[0][step:mid] + g[1][:step], g[1][step:mid] + g[2][:step], g[2][step:mid]]
            c = jnp.concatenate(c, 0)
            gup[h, i] = c[:EDGE].astype(BF)
            own[h, i] = c[EDGE : EDGE + TOKENS].astype(own.dtype)
            gdn[h, i] = c[EDGE + TOKENS :].astype(BF)
            w = BLOCK_ROWS * RADIUS
            sides = []
            for j in range(2):
                s = [x[mid + j * half : mid + (j + 1) * half] for x in g]
                s = jnp.concatenate([s[0][:w], s[0][w:] + s[1][:w], s[1][w:] + s[2][:w], s[2][w:]], 0)
                sides.append(s.astype(BF))
            ga[h, i] = lax.select(even[1] == 1, sides[1], sides[0])
            gb[h, i] = lax.select(even[1] == 1, sides[0], sides[1])


def attend(chunk, even, q, do, kv, up, dn, far, sa, sb, bias, heads=2):
    _, t, d = q.shape
    h = sa.shape[2]
    steps = h // heads

    def spec(x, offset=0):
        return pl.BlockSpec((heads,) + x.shape[1:], lambda g: (g + offset,) + (0,) * (len(x.shape) - 1))

    def whole(x):
        return pl.BlockSpec(x.shape, lambda g: (0,) * len(x.shape))

    outs = [sds(h, t, d)] * 2 + [sds(h, 2, n, d) for n in (t, EDGE, EDGE, STRIP, STRIP)]
    flops = h * BLOCKS * QUERIES * (4 * (NEAR + far.shape[2]) + 2 * NEAR) * d * 2
    args = (q, do, kv, up, dn, far)
    return pl.pallas_call(
        functools.partial(attend_kernel, heads),
        grid=(steps,),
        in_specs=[spec(x, chunk * steps) for x in args] + [whole(x) for x in (sa, sb, bias)] + [SMEM],
        out_specs=[spec(x) for x in outs],
        out_shape=outs,
        scratch_shapes=[pltpu.VMEM((2, h, 2, STRIP, d), BF)],
        compiler_params=PARAMS,
        cost_estimate=pl.CostEstimate(flops=flops, bytes_accessed=12 << 20, transcendentals=0),
        name="attend",
    )(*args, sa, sb, bias, even)


def near_bias():
    position = lax.axis_index("seq")
    tiles_y = lax.axis_size("seq") // TILES_X
    shape = (BLOCKS, QUERIES, NEAR)
    b = lax.broadcasted_iota(jnp.int32, shape, 0)
    i = lax.broadcasted_iota(jnp.int32, shape, 1)
    k = lax.broadcasted_iota(jnp.int32, shape, 2)
    mid = WIN_ROWS * TILE_W
    half = WIN_ROWS * RADIUS
    k_row = jnp.where(k < mid, k // TILE_W, (k - mid) % half // RADIUS) - RADIUS
    side = jnp.where(k < mid + half, k % RADIUS - RADIUS, k % RADIUS + TILE_W)
    k_col = jnp.where(k < mid, k % TILE_W, side)
    seen = (jnp.abs(k_row - i // TILE_W) <= RADIUS) & (jnp.abs(k_col - i % TILE_W) <= RADIUS)
    row = position // TILES_X * TILE_H + b * BLOCK_ROWS + k_row
    col = position % TILES_X * TILE_W + k_col
    inside = (row >= 0) & (row < tiles_y * TILE_H) & (col >= 0) & (col < TILES_X * TILE_W)
    return jnp.where(seen & inside, 0.0, FLOOR).astype(F32)


def shards(fine_queries, fine_keys, fine_values, coarse_keys, coarse_values, out_grad):
    position = lax.axis_index("seq")
    even = jnp.stack([1 - position // TILES_X % 2, 1 - position % TILES_X % 2]).astype(jnp.int32)
    coarse = jnp.concatenate(widened(jnp.stack([coarse_keys[0], coarse_values[0]], 1), 4), 0)
    start = even[0] * (TOKENS - EDGE)
    rows = [
        jnp.stack([lax.dynamic_slice_in_dim(x[0], o, EDGE, 0) for x in (fine_keys, fine_values)], 1)
        for o in (start, TOKENS - EDGE - start)
    ]
    coarse, *rows = lax.optimization_barrier((coarse, *rows))
    row_a, row_b = (exchange(x, True, which) for which, x in enumerate(rows))
    coarse = jnp.concatenate(widened(coarse, 16), 0)
    coarse, fine_queries, out_grad, fine_keys, fine_values = lax.optimization_barrier(
        (coarse, fine_queries, out_grad, fine_keys, fine_values)
    )
    pieces = widened(coarse, 1)
    queries, cots = to_heads(fine_queries, out_grad)
    kv = pairs_to_heads(fine_keys, fine_values)
    bias = near_bias()
    row_a, row_b, kv, queries, cots, bias = lax.optimization_barrier((row_a, row_b, kv, queries, cots, bias))
    strips = sides(even, row_a, row_b, fine_keys[0], fine_values[0])
    side_a, side_b = ([exchange(x, False, which) for x in xs] for which, xs in enumerate(strips))
    up, dn = halo_to_heads(even, row_a, row_b)
    far = far_heads(pieces)
    att, dq, own, gup, gdn, from_a, from_b = ([] for _ in range(7))
    for c in range(CHUNKS):
        a, b, mine, u, n, ga, gb = attend(
            c, even, queries, cots, kv, up, dn, far, side_a[c], side_b[c], bias
        )
        from_a.append(exchange(ga, False, 0))
        from_b.append(exchange(gb, False, 1))
        for xs, x in ((att, a), (dq, b), (own, mine), (gup, u), (gdn, n)):
            xs.append(x)
    to_a, to_b = fold(even, gup, gdn, from_a, from_b)
    to_a, to_b = exchange(to_a, True, 0), exchange(to_b, True, 1)
    attended, query_grad = to_tokens(att, dq)
    dk, dv = premerge(even, own, from_a, from_b)
    key_grad, value_grad = finish(even, dk, dv, to_a, to_b)
    return (attended, query_grad, key_grad, value_grad)


def solution(mesh):
    spec = P("dp", "seq", "head", None)
    return jax.shard_map(
        shards, mesh=mesh, in_specs=(spec,) * 6, out_specs=(spec,) * 4, check_vma=False
    )
```

```python
import functools

import jax
import jax.numpy as jnp
from jax import lax
from jax.experimental import pallas as pl
from jax.experimental.pallas import tpu as pltpu
from jax.sharding import PartitionSpec as P

TILE_H = 24
TILE_W = 16
RADIUS = 4
TILES_X = 8
TOKENS = TILE_H * TILE_W
EDGE = RADIUS * TILE_W
SIDE = TILE_H * RADIUS
CORNER = RADIUS * RADIUS
STRIP = SIDE + 2 * CORNER
CHUNKS = 2
BLOCK_ROWS = 8
BLOCKS = TILE_H // BLOCK_ROWS
QUERIES = BLOCK_ROWS * TILE_W
WIN_ROWS = BLOCK_ROWS + 2 * RADIUS
NEAR = WIN_ROWS * (TILE_W + 2 * RADIUS)
FLOOR = -1e30
LOG2E = 1.4426950408889634
BF = jnp.bfloat16
F32 = jnp.float32
SMEM = pl.BlockSpec(memory_space=pltpu.SMEM)
VMEM = pl.BlockSpec(memory_space=pltpu.VMEM)
PARAMS = pltpu.CompilerParams(vmem_limit_bytes=56 << 20)


def nt(a, b):
    return lax.dot_general(a, b, (((1,), (1,)), ((), ())), preferred_element_type=F32)


def tn(a, b):
    return lax.dot_general(a, b, (((0,), (0,)), ((), ())), preferred_element_type=F32)


def nn(a, b):
    return lax.dot_general(a, b, (((1,), (0,)), ((), ())), preferred_element_type=F32)


def sds(*shape):
    return jax.ShapeDtypeStruct(shape, BF)


def exchange(value, rows, which):
    count = lax.axis_size("seq")
    pairs = []
    for source in range(count):
        row, col = divmod(source, TILES_X)
        place, extent = (row, count // TILES_X) if rows else (col, TILES_X)
        target = ((place + which) ^ 1) - which
        if not 0 <= target < extent:
            target = place
        pairs.append((source, target * TILES_X + col if rows else row * TILES_X + target))
    return lax.ppermute(value, "seq", pairs)


def widened(block, stride):
    count = lax.axis_size("seq")

    def swapped(mask):
        pairs = [(source, source ^ (mask * stride)) for source in range(count)]
        return lax.ppermute(block, "seq", pairs)

    return [block] + [swapped(mask) for mask in (1, 2, 3)]


def pairs_to_heads_kernel(k, v, kv):
    for i, x in enumerate((k, v)):
        kv[:, i] = jnp.swapaxes(x[0], 0, 1)


def pairs_to_heads(k, v):
    t, h, d = k.shape[1:]
    n = t // BLOCKS
    tokens = pl.BlockSpec((1, n, h, d), lambda g: (0, g, 0, 0))
    return pl.pallas_call(
        pairs_to_heads_kernel,
        grid=(BLOCKS,),
        in_specs=[tokens, tokens],
        out_specs=pl.BlockSpec((h, 2, n, d), lambda g: (0, 0, g, 0)),
        out_shape=sds(h, 2, t, d),
        compiler_params=PARAMS,
        name="pairs_to_heads",
    )(k, v)


def to_heads_kernel(x, y, a, b):
    a[...] = jnp.swapaxes(x[0], 0, 1)
    b[...] = jnp.swapaxes(y[0], 0, 1)


def to_heads(x, y):
    t, h, d = x.shape[1:]
    n = t // BLOCKS
    tokens = pl.BlockSpec((1, n, h, d), lambda g: (0, g, 0, 0))
    heads = pl.BlockSpec((h, n, d), lambda g: (0, g, 0))
    return pl.pallas_call(
        to_heads_kernel,
        grid=(BLOCKS,),
        in_specs=[tokens, tokens],
        out_specs=[heads, heads],
        out_shape=[sds(h, t, d)] * 2,
        compiler_params=PARAMS,
        name="to_heads",
    )(x, y)


def halo_to_heads_kernel(even, x, y, up, dn):
    a = jnp.swapaxes(x[:, 0], 0, 1)
    b = jnp.swapaxes(y[:, 0], 0, 1)
    up[:, 0] = lax.select(even[0] == 1, b, a)
    dn[:, 0] = lax.select(even[0] == 1, a, b)


def halo_to_heads(even, x, y):
    t, _, h, d = x.shape
    tokens = pl.BlockSpec((t, 1, h, d), lambda g: (0, g, 0, 0))
    heads = pl.BlockSpec((h, 1, t, d), lambda g: (0, g, 0, 0))
    return pl.pallas_call(
        halo_to_heads_kernel,
        grid=(2,),
        in_specs=[SMEM, tokens, tokens],
        out_specs=[heads, heads],
        out_shape=[sds(h, 2, t, d)] * 2,
        compiler_params=PARAMS,
        name="halo_to_heads",
    )(even, x, y)


def far_kernel(*refs):
    out = refs[-1]
    n = refs[0].shape[0]
    for j, piece in enumerate(refs[:-1]):
        out[:, 0, j * n : (j + 1) * n] = jnp.swapaxes(piece[:, 0], 0, 1)


def far_heads(pieces):
    n, _, h, d = pieces[0].shape
    t = n * len(pieces)
    return pl.pallas_call(
        far_kernel,
        grid=(2,),
        in_specs=[pl.BlockSpec((n, 1, h, d), lambda g: (0, g, 0, 0))] * len(pieces),
        out_specs=pl.BlockSpec((h, 1, t, d), lambda g: (0, g, 0, 0)),
        out_shape=sds(h, 2, t, d),
        compiler_params=PARAMS,
        name="far_heads",
    )(*pieces)


def sides_kernel(even, a, b, ka, kb, va, vb, *outs):
    h, d = a.shape[2:]
    n = h // CHUNKS
    for j, (mine, e) in enumerate((((ka, va), even[1]), ((kb, vb), 1 - even[1]))):
        for i in range(2):
            x = mine[i][...].reshape(SIDE, h, d)
            for c in range(CHUNKS):
                outs[j * CHUNKS + c][CORNER : CORNER + SIDE, i] = x[:, c * n : (c + 1) * n]
            for g, rows in enumerate((a, b)):
                end = (STRIP - CORNER) * (g ^ even[0])
                for r in range(RADIUS):
                    x = rows[pl.ds(r * TILE_W + (TILE_W - RADIUS) * e, RADIUS), i]
                    for c in range(CHUNKS):
                        outs[j * CHUNKS + c][pl.ds(end + r * RADIUS, RADIUS), i] = x[:, c * n : (c + 1) * n]


def sides(even, a, b, k, v):
    h, d = a.shape[2:]
    k = k.reshape(TILE_H, TILE_W, h, d)
    v = v.reshape(TILE_H, TILE_W, h, d)
    block = (TILE_H, RADIUS, h, d)
    last = TILE_W // RADIUS - 1
    whole = pl.BlockSpec(a.shape, lambda g, e: (0, 0, 0, 0))
    side_a = pl.BlockSpec(block, lambda g, e: (0, last * e[1], 0, 0))
    side_b = pl.BlockSpec(block, lambda g, e: (0, last * (1 - e[1]), 0, 0))
    shape = (STRIP, 2, h // CHUNKS, d)
    outs = pl.pallas_call(
        sides_kernel,
        grid_spec=pltpu.PrefetchScalarGridSpec(
            num_scalar_prefetch=1,
            grid=(1,),
            in_specs=[whole, whole, side_a, side_b, side_a, side_b],
            out_specs=[pl.BlockSpec(shape, lambda g, e: (0, 0, 0, 0))] * (2 * CHUNKS),
        ),
        out_shape=[sds(*shape)] * (2 * CHUNKS),
        compiler_params=PARAMS,
        name="sides",
    )(even, a, b, k, k, v, v)
    return outs[:CHUNKS], outs[CHUNKS:]


def to_tokens_kernel(*refs):
    n = (len(refs) - 2) // 2
    for j in range(2):
        x = jnp.concatenate([r[...] for r in refs[j * n : (j + 1) * n]], 0)
        refs[2 * n + j][0] = jnp.swapaxes(x, 0, 1)


def to_tokens(xs, ys):
    h, t, d = xs[0].shape
    n = t // BLOCKS
    return pl.pallas_call(
        to_tokens_kernel,
        grid=(BLOCKS,),
        in_specs=[pl.BlockSpec((h, n, d), lambda g: (0, g, 0))] * (2 * len(xs)),
        out_specs=[pl.BlockSpec((1, n, h * len(xs), d), lambda g: (0, g, 0, 0))] * 2,
        out_shape=[sds(1, t, h * len(xs), d)] * 2,
        compiler_params=PARAMS,
        name="to_tokens",
    )(*xs, *ys)


def fold_kernel(even, *refs):
    gup, gdn, from_a, from_b = (refs[c * CHUNKS : (c + 1) * CHUNKS] for c in range(4))
    a, b = refs[4 * CHUNKS :]
    t, _, h, d = a.shape

    def tokens(parts, rows, cols):
        x = jnp.concatenate([r[:, 0, rows] for r in parts], 0)
        return jnp.swapaxes(x, 0, 1).astype(F32).reshape(RADIUS, cols, h, d)

    folded = []
    for g, o in ((gup, 0), (gdn, STRIP - CORNER)):
        x = tokens(g, slice(0, t), TILE_W)
        sa, sb = (tokens(s, slice(o, o + CORNER), RADIUS) for s in (from_a, from_b))
        left = lax.select(even[1] == 1, sb, sa)
        right = lax.select(even[1] == 1, sa, sb)
        x = jnp.concatenate(
            [x[:, :RADIUS] + left, x[:, RADIUS : TILE_W - RADIUS], x[:, TILE_W - RADIUS :] + right], 1
        )
        folded.append(x.reshape(t, h, d).astype(BF))
    a[:, 0] = lax.select(even[0] == 1, folded[1], folded[0])
    b[:, 0] = lax.select(even[0] == 1, folded[0], folded[1])


def fold(even, gup, gdn, from_a, from_b):
    args = (*gup, *gdn, *from_a, *from_b)
    h, _, t, d = gup[0].shape
    h *= CHUNKS
    return pl.pallas_call(
        fold_kernel,
        grid=(2,),
        in_specs=[SMEM]
        + [pl.BlockSpec((x.shape[0], 1) + x.shape[2:], lambda g: (0, g, 0, 0)) for x in args],
        out_specs=[pl.BlockSpec((t, 1, h, d), lambda g: (0, g, 0, 0))] * 2,
        out_shape=[sds(t, 2, h, d)] * 2,
        compiler_params=PARAMS,
        name="fold",
    )(even, *args)


def premerge_kernel(even, *refs):
    own, from_a, from_b = (refs[c * CHUNKS : (c + 1) * CHUNKS] for c in range(3))
    for i, out in enumerate(refs[3 * CHUNKS :]):
        h, d = out.shape[2:]

        def tokens(parts, rows, *lead):
            x = jnp.concatenate([r[:, i, rows] for r in parts], 0)
            return jnp.swapaxes(x, 0, 1).astype(F32).reshape(*lead, h, d)

        t = tokens(own, slice(0, TOKENS), TILE_H, TILE_W)
        sa = tokens(from_a, slice(CORNER, CORNER + SIDE), TILE_H, RADIUS)
        sb = tokens(from_b, slice(CORNER, CORNER + SIDE), TILE_H, RADIUS)
        le = lax.select(even[1] == 1, sb, sa)
        ri = lax.select(even[1] == 1, sa, sb)
        t = jnp.concatenate(
            [t[:, :RADIUS] + le, t[:, RADIUS : TILE_W - RADIUS], t[:, TILE_W - RADIUS :] + ri], 1
        )
        out[0] = t.reshape(TOKENS, h, d).astype(BF)


def premerge(even, own, from_a, from_b):
    h, _, t, d = own[0].shape
    return pl.pallas_call(
        premerge_kernel,
        in_specs=[SMEM] + [VMEM] * (3 * CHUNKS),
        out_shape=[sds(1, t, h * CHUNKS, d)] * 2,
        compiler_params=PARAMS,
        name="premerge",
    )(even, *own, *from_a, *from_b)


def finish_kernel(even, dk, dv, from_a, from_b, dk_out, dv_out):
    for g, part in enumerate((from_a, from_b)):

        @pl.when(pl.program_id(0) == g)
        def _():
            for i, (x, out) in enumerate(((dk, dk_out), (dv, dv_out))):
                out[0] = (x[0].astype(F32) + part[:, i].astype(F32)).astype(BF)


def finish(even, dk, dv, from_a, from_b):
    h, d = dk.shape[2:]
    last = TOKENS // EDGE - 1
    rows = pl.BlockSpec((1, EDGE, h, d), lambda g, e: (0, last * (g ^ e[0]), 0, 0))
    part = pl.BlockSpec(from_a.shape, lambda g, e: (0, 0, 0, 0))
    return pl.pallas_call(
        finish_kernel,
        grid_spec=pltpu.PrefetchScalarGridSpec(
            num_scalar_prefetch=1,
            grid=(2,),
            in_specs=[rows, rows, part, part],
            out_specs=[rows, rows],
        ),
        out_shape=[sds(*dk.shape)] * 2,
        input_output_aliases={1: 0, 2: 1},
        compiler_params=PARAMS,
        name="finish",
    )(even, dk, dv, from_a, from_b)


def attend_kernel(
    heads, q, do, kv, up, dn, far, sa, sb, bias, even, att, dq, own, gup, gdn, ga, gb, strips_lr
):
    @pl.when(pl.program_id(0) == 0)
    def _():
        for src, side in ((sa, even[1]), (sb, 1 - even[1])):
            for i in range(2):
                strips_lr[side, :, i] = jnp.swapaxes(src[:, i], 0, 1)

    first = pl.program_id(0) * heads
    scale = q.shape[-1] ** -0.5
    half = WIN_ROWS * RADIUS
    mid = WIN_ROWS * TILE_W

    def strips(h, i):
        center = jnp.concatenate([up[h, i], kv[h, i], dn[h, i]], 0)
        return center, strips_lr[0, first + h, i], strips_lr[1, first + h, i], far[h, i]

    def window(parts, b):
        c, l, r, f = parts
        o, s = b * BLOCK_ROWS * TILE_W, b * BLOCK_ROWS * RADIUS
        return jnp.concatenate([c[o : o + mid], l[s : s + half], r[s : s + half], f], 0)

    parts = [[strips(h, i) for i in range(2)] for h in range(heads)]
    grads = {}

    def block(h, b):
        rows = slice(b * QUERIES, (b + 1) * QUERIES)
        queries, cots = q[h, rows], do[h, rows]
        keys, values = window(parts[h][0], b), window(parts[h][1], b)
        s = nt(queries, keys)
        dp = nt(cots, values)
        yield
        s = s * (scale * LOG2E)
        s = jnp.concatenate([s[:, :NEAR] + bias[b], s[:, NEAR:]], 1)
        top = jnp.max(s, 1, keepdims=True)
        yield
        e = jnp.exp2(s - top)
        inverse = 1.0 / jnp.sum(e, 1, keepdims=True)
        yield
        p = e * inverse
        rounded = p.astype(BF)
        out = nn(rounded, values).astype(BF)
        dv = tn(rounded[:, :NEAR], cots)
        yield
        att[h, rows] = out
        delta = jnp.sum(out.astype(F32) * cots.astype(F32), 1, keepdims=True)
        ds = (p * (dp - delta) * scale).astype(BF)
        dqs = nn(ds, keys)
        dk = tn(ds[:, :NEAR], queries)
        yield
        dq[h, rows] = dqs.astype(BF)
        grads[h, b] = (dk, dv)

    live = [block(h, b) for h in range(heads) for b in range(BLOCKS)]
    while live:
        for g in list(live):
            try:
                next(g)
            except StopIteration:
                live.remove(g)

    step = BLOCK_ROWS * TILE_W
    for h in range(heads):
        for i in range(2):
            g = [grads[h, b][i] for b in range(BLOCKS)]
            c = [g[0][:step], g[0][step:mid] + g[1][:step], g[1][step:mid] + g[2][:step], g[2][step:mid]]
            c = jnp.concatenate(c, 0)
            gup[h, i] = c[:EDGE].astype(BF)
            own[h, i] = c[EDGE : EDGE + TOKENS].astype(own.dtype)
            gdn[h, i] = c[EDGE + TOKENS :].astype(BF)
            w = BLOCK_ROWS * RADIUS
            sides = []
            for j in range(2):
                s = [x[mid + j * half : mid + (j + 1) * half] for x in g]
                s = jnp.concatenate([s[0][:w], s[0][w:] + s[1][:w], s[1][w:] + s[2][:w], s[2][w:]], 0)
                sides.append(s.astype(BF))
            ga[h, i] = lax.select(even[1] == 1, sides[1], sides[0])
            gb[h, i] = lax.select(even[1] == 1, sides[0], sides[1])


def attend(chunk, even, q, do, kv, up, dn, far, sa, sb, bias, heads=2):
    _, t, d = q.shape
    h = sa.shape[2]
    steps = h // heads

    def spec(x, offset=0):
        return pl.BlockSpec((heads,) + x.shape[1:], lambda g: (g + offset,) + (0,) * (len(x.shape) - 1))

    def whole(x):
        return pl.BlockSpec(x.shape, lambda g: (0,) * len(x.shape))

    outs = [sds(h, t, d)] * 2 + [sds(h, 2, n, d) for n in (t, EDGE, EDGE, STRIP, STRIP)]
    flops = h * BLOCKS * QUERIES * (4 * (NEAR + far.shape[2]) + 2 * NEAR) * d * 2
    args = (q, do, kv, up, dn, far)
    return pl.pallas_call(
        functools.partial(attend_kernel, heads),
        grid=(steps,),
        in_specs=[spec(x, chunk * steps) for x in args] + [whole(x) for x in (sa, sb, bias)] + [SMEM],
        out_specs=[spec(x) for x in outs],
        out_shape=outs,
        scratch_shapes=[pltpu.VMEM((2, h, 2, STRIP, d), BF)],
        compiler_params=PARAMS,
        cost_estimate=pl.CostEstimate(flops=flops, bytes_accessed=12 << 20, transcendentals=0),
        name="attend",
    )(*args, sa, sb, bias, even)


def near_bias():
    position = lax.axis_index("seq")
    tiles_y = lax.axis_size("seq") // TILES_X
    shape = (BLOCKS, QUERIES, NEAR)
    b = lax.broadcasted_iota(jnp.int32, shape, 0)
    i = lax.broadcasted_iota(jnp.int32, shape, 1)
    k = lax.broadcasted_iota(jnp.int32, shape, 2)
    mid = WIN_ROWS * TILE_W
    half = WIN_ROWS * RADIUS
    k_row = jnp.where(k < mid, k // TILE_W, (k - mid) % half // RADIUS) - RADIUS
    side = jnp.where(k < mid + half, k % RADIUS - RADIUS, k % RADIUS + TILE_W)
    k_col = jnp.where(k < mid, k % TILE_W, side)
    seen = (jnp.abs(k_row - i // TILE_W) <= RADIUS) & (jnp.abs(k_col - i % TILE_W) <= RADIUS)
    row = position // TILES_X * TILE_H + b * BLOCK_ROWS + k_row
    col = position % TILES_X * TILE_W + k_col
    inside = (row >= 0) & (row < tiles_y * TILE_H) & (col >= 0) & (col < TILES_X * TILE_W)
    return jnp.where(seen & inside, 0.0, FLOOR).astype(F32)


def shards(fine_queries, fine_keys, fine_values, coarse_keys, coarse_values, out_grad):
    position = lax.axis_index("seq")
    even = jnp.stack([1 - position // TILES_X % 2, 1 - position % TILES_X % 2]).astype(jnp.int32)
    coarse = jnp.concatenate(widened(jnp.stack([coarse_keys[0], coarse_values[0]], 1), 4), 0)
    start = even[0] * (TOKENS - EDGE)
    rows = [
        jnp.stack([lax.dynamic_slice_in_dim(x[0], o, EDGE, 0) for x in (fine_keys, fine_values)], 1)
        for o in (start, TOKENS - EDGE - start)
    ]
    coarse, *rows = lax.optimization_barrier((coarse, *rows))
    row_a, row_b = (exchange(x, True, which) for which, x in enumerate(rows))
    coarse = jnp.concatenate(widened(coarse, 16), 0)
    coarse, fine_queries, out_grad, fine_keys, fine_values = lax.optimization_barrier(
        (coarse, fine_queries, out_grad, fine_keys, fine_values)
    )
    pieces = widened(coarse, 1)
    queries, cots = to_heads(fine_queries, out_grad)
    kv = pairs_to_heads(fine_keys, fine_values)
    bias = near_bias()
    row_a, row_b, kv, queries, cots, bias = lax.optimization_barrier((row_a, row_b, kv, queries, cots, bias))
    strips = sides(even, row_a, row_b, fine_keys[0], fine_values[0])
    side_a, side_b = ([exchange(x, False, which) for x in xs] for which, xs in enumerate(strips))
    up, dn = halo_to_heads(even, row_a, row_b)
    far = far_heads(pieces)
    att, dq, own, gup, gdn, from_a, from_b = ([] for _ in range(7))
    for c in range(CHUNKS):
        a, b, mine, u, n, ga, gb = attend(
            c, even, queries, cots, kv, up, dn, far, side_a[c], side_b[c], bias
        )
        from_a.append(exchange(ga, False, 0))
        from_b.append(exchange(gb, False, 1))
        for xs, x in ((att, a), (dq, b), (own, mine), (gup, u), (gdn, n)):
            xs.append(x)
    to_a, to_b = fold(even, gup, gdn, from_a, from_b)
    to_a, to_b = exchange(to_a, True, 0), exchange(to_b, True, 1)
    attended, query_grad = to_tokens(att, dq)
    dk, dv = premerge(even, own, from_a, from_b)
    key_grad, value_grad = finish(even, dk, dv, to_a, to_b)
    return (attended, query_grad, key_grad, value_grad)


def solution(mesh):
    spec = P("dp", "seq", "head", None)
    return jax.shard_map(
        shards, mesh=mesh, in_specs=(spec,) * 6, out_specs=(spec,) * 4, check_vma=False
    )
```
